32 devices in a mesh: mol: 2 (over y), pair: 4 (over z), tile: 2 (over x), sub: 2 (over core).
Axes of the slice: x: 2, y: 2, z: 4, core: 2. Of those that a mesh axis runs over, the one named last changes fastest.
Arguments:
- lambda_amps: bfloat16 [8, 2, 32, 128, 512], P(('mol', 'pair'), 'sub', None, None, 'tile'), parts along dimension 0, may hold values from -6 to 6
- integral_tiles: bfloat16 [8, 128, 128], P(('mol', 'pair')), parts along dimension 0, may hold values from -0.5 to 0.5
- tile_of: int32 [8, 2, 32], P(('mol', 'pair'), 'sub'), parts along dimension 0, may hold values from 0 to 3
- tile_mask: int32 [8, 2, 32, 4], P(('mol', 'pair'), 'sub', None, 'tile'), parts along dimension 0, may hold values 0 or 1
- pair_list: int32 [512, 2], P('mol'), parts along dimension 0, may hold values from 0 to 399
- coupling: float32 [800, 400], P('mol'), parts along dimension 0, may hold values from -1 to 1
- pair_gap: float32 [8, 2, 32], P('mol', 'sub'), parts along dimension 0, may hold values from 0.5 to 4
- row_energy: float32 [256], P(('mol', 'pair')), parts along dimension 0, may hold values from 0.5 to 4
- col_energy: float32 [1024], P(('mol', 'tile')), parts along dimension 0, may hold values from 0.5 to 4
Outputs:
- new_lambda: bfloat16 [8, 2, 32, 128, 512], P('mol', 'sub', None, 'pair', 'tile'), parts along dimension 0
The draws below stay inside these ranges and needn't reach their ends.
There are 2 independent parts, one for each index of `mol`. The reference program is written for one: setup_inputs(seed, part) draws one part's arguments, and reference() takes and returns one part's arrays. A program takes and returns all parts, laid end to end along the dimension named above; each array names one. Nothing has to cross between parts.
Inputs may be any that keep to these rules, and one draw needn't show every extreme that they name: `tile_of`: an index into the 4 integral tiles.
All inputs are finite; a program needn't handle non-finite values. No bound on the sum of `tile_mask` on one device may be relied on, other than what follows from the above.
Results may differ from the reference program's by a relative error of at most 0.0055.
Values may be sent and summed in bfloat16 or wider, within the bound.
No kernel may reach another device: no remote copies, remote signals or barrier semaphores. Data moves between devices by JAX's collectives and lax.ppermute only.
A program may use at most 64 MiB of HBM per device.

```python
import math
import jax
import jax.numpy as jnp
import numpy as np
from jax import lax

VT = 128
VB = 4
NOCC = 400
PAIR_DEV = 32
VW = 512
OWNERS = 4
SUBS = 2
PAIRS = 256
NT = 4


def set_ends(drawn, stream_key, smallest, largest):
    spot = [jax.random.randint(jax.random.fold_in(stream_key, axis), (), 0, length) for axis, length in enumerate(drawn.shape)]
    widest = drawn.shape.index(max(drawn.shape))
    next_to = spot[:widest] + [(spot[widest] + 1) % drawn.shape[widest]] + spot[widest + 1:]
    return drawn.at[tuple(spot)].set(smallest).at[tuple(next_to)].set(largest)


def block_scale(own_key, dims, pieces, least, largest):
    factor_of, own = 1.0, jax.random.fold_in(own_key, 6)
    for axis_at, blocks in pieces:
        heights = jnp.exp(jax.random.uniform(jax.random.fold_in(own, axis_at), (blocks,), jnp.float32, least / len(pieces), largest / len(pieces)))
        factor_of = factor_of * jnp.repeat(heights, dims[axis_at] // blocks).reshape([-1 if axis == axis_at else 1 for axis in range(len(dims))])
    return factor_of


def rank_table(count, slope):
    portions = [(1 << 20) // math.isqrt(grade ** slope) + 1 for grade in range(1, count + 1)]
    scale = 1 + sum(portions) // (1 << 30)
    return np.cumsum(np.array([max(1, weight // scale) for weight in portions]))


def skewed_ids(stream_key, extent, amount, slope):
    table = rank_table(amount, slope)
    ticket = jax.random.randint(jax.random.fold_in(stream_key, 1), extent, 0, int(table[amount - 1]))
    rank = jnp.searchsorted(jnp.asarray(table, jnp.int32), ticket, side="right")
    return jax.random.permutation(jax.random.fold_in(stream_key, 2), amount)[rank].astype(jnp.int32)


def centred(own_key, extent, spread, reach, cuts=(), held_as=jnp.bfloat16):
    result = spread * jax.random.normal(own_key, extent, jnp.float32)
    if cuts:
        result = result * block_scale(own_key, extent, cuts, -0.22, 0.18)
    return jnp.clip(result, -reach, reach).astype(held_as)


def setup_inputs(seed: int = 0, part: int = 0) -> dict:
    splits = jax.random.split(jax.random.key(seed), 10)
    part_keys = jax.random.split(jax.random.fold_in(splits[9], part), 10)
    lambda_amps = centred(part_keys[0], (OWNERS, SUBS, PAIR_DEV, VT, VW), 1.0, 6.0, ((0, 4), (1, 2), (4, 2)))
    integral_tiles = centred(part_keys[1], (NT, VT, VT), VT ** -0.5, 0.5, ((0, 4),))
    tile_of = set_ends(skewed_ids(part_keys[2], (OWNERS, SUBS, PAIR_DEV), NT, 2), jax.random.fold_in(part_keys[2], 3), 0, NT - 1).astype(jnp.int32)
    tile_mask = set_ends((jax.random.randint(part_keys[3], (OWNERS, SUBS, PAIR_DEV, VB), 0, 4) < 3).astype(jnp.int32), jax.random.fold_in(part_keys[3], 1), 0, 1)
    pair_list = set_ends(jax.random.randint(part_keys[4], (PAIRS, 2), 0, NOCC), jax.random.fold_in(part_keys[4], 1), 0, NOCC - 1).astype(jnp.int32)
    coupling = centred(part_keys[5], (NOCC, NOCC), 0.15, 1.0, (), jnp.float32)
    pair_gap = jnp.clip(jnp.exp(math.log(4.0) - 2.0794415 * jax.random.uniform(part_keys[6], (OWNERS, SUBS, PAIR_DEV), jnp.float32) ** block_scale(part_keys[6], (OWNERS, SUBS, PAIR_DEV), ((1, 2),), -0.2, 0.2)), 0.5, 4.0)
    row_energy = jnp.clip(jnp.exp(math.log(4.0) - 2.0794415 * jax.random.uniform(part_keys[7], (VT,), jnp.float32) ** block_scale(part_keys[7], (VT,), ((0, 4),), -0.2, 0.2)), 0.5, 4.0)
    col_energy = jnp.clip(jnp.exp(math.log(4.0) - 2.0794415 * jax.random.uniform(part_keys[8], (VW,), jnp.float32) ** block_scale(part_keys[8], (VW,), ((0, 2),), -0.2, 0.2)), 0.5, 4.0)
    return {"lambda_amps": lambda_amps, "integral_tiles": integral_tiles, "tile_of": tile_of, "tile_mask": tile_mask, "pair_list": pair_list, "coupling": coupling, "pair_gap": pair_gap, "row_energy": row_energy, "col_energy": col_energy}


def column_tables(coupling, col_pairs):
    left_table = jnp.take(coupling.T, col_pairs[:, 0], axis=0).T
    right_table = jnp.take(coupling.T, col_pairs[:, 1], axis=0).T
    return left_table, right_table


def cycle_rows(left_table, right_table, row_pairs, flat_rhs):
    left_part = jnp.take(left_table, row_pairs[:, 0], axis=0)
    right_part = jnp.take(right_table, row_pairs[:, 1], axis=0)
    weights = (left_part * right_part).astype(jnp.bfloat16)
    return jnp.dot(weights, flat_rhs, preferred_element_type=jnp.float32)


def reference(lambda_amps, integral_tiles, tile_of, tile_mask, pair_list, coupling, pair_gap, row_energy, col_energy):
    amplitudes = lambda_amps.reshape(PAIRS, VT, VW)
    chosen = integral_tiles[tile_of.reshape(PAIRS).astype(jnp.int32)].astype(jnp.float32)
    ladder = jnp.einsum('pac,pcb->pab', chosen, amplitudes.astype(jnp.float32))
    keep_mask = tile_mask.reshape(PAIRS, 1, VB, 1).astype(jnp.float32)
    ladder = (ladder.reshape(PAIRS, VT, VB, VT) * keep_mask).reshape(PAIRS, VT, VW)
    dressed = (amplitudes.astype(jnp.float32) + ladder).astype(jnp.bfloat16)
    flat_rhs = dressed.reshape(PAIRS, VT * VW)
    left_table, right_table = column_tables(coupling, pair_list)
    step_rows = math.gcd(PAIRS, 512)
    row_blocks = pair_list.reshape(PAIRS // step_rows, step_rows, 2)

    def one_block(row_pairs):
        return cycle_rows(left_table, right_table, row_pairs, flat_rhs)

    cycle_term = lax.map(one_block, row_blocks).reshape(PAIRS, VT, VW)
    energy_gap = pair_gap.reshape(PAIRS)[:, None, None] + row_energy[None, :, None] + col_energy[None, None, :]
    new_lambda = (-(dressed.astype(jnp.float32) + cycle_term) / energy_gap).astype(jnp.bfloat16)
    return new_lambda.reshape(OWNERS, SUBS, PAIR_DEV, VT, VW)
```

```python
import functools
import math

import jax
import jax.numpy as jnp
from jax import lax
from jax.experimental import pallas as pl
from jax.experimental.pallas import tpu as pltpu
from jax.sharding import PartitionSpec as P

ROWS = 16
LANES = 128


def column_tables(coupling, col_pairs):
    left_table = jnp.take(coupling.T, col_pairs[:, 0], axis=0).T
    right_table = jnp.take(coupling.T, col_pairs[:, 1], axis=0).T
    return (left_table, right_table)


def cycle_rows(left_table, right_table, row_pairs):
    left_part = jnp.take(left_table, row_pairs[:, 0], axis=0)
    right_part = jnp.take(right_table, row_pairs[:, 1], axis=0)
    return (left_part * right_part).astype(jnp.bfloat16)


def cycle_all(coupling, pair_list, col_pairs, flat_rhs):
    total_pairs = pair_list.shape[0]
    step_rows = math.gcd(total_pairs, 512)
    row_blocks = pair_list.reshape(total_pairs // step_rows, step_rows, 2)
    left_table, right_table = column_tables(coupling, col_pairs)

    def one_block(row_pairs):
        weights = cycle_rows(left_table, right_table, row_pairs)
        return jnp.dot(weights, flat_rhs, preferred_element_type=jnp.float32)

    return lax.map(one_block, row_blocks).reshape(total_pairs, -1)


def local_general(
    lambda_amps,
    integral_tiles,
    tile_of,
    tile_mask,
    pair_list,
    coupling,
    pair_gap,
    row_energy,
    col_energy,
):
    pair_count = lambda_amps.shape[2]
    tile_rows = lambda_amps.shape[3]
    col_count = lambda_amps.shape[4]
    owners = lax.axis_size("pair")
    sub_count = lax.axis_size("sub")
    wanted = tile_of.reshape(pair_count)
    empty_tiles = jnp.zeros((pair_count, tile_rows, tile_rows), integral_tiles.dtype)
    shard_piece = lax.all_gather(integral_tiles, "pair", axis=0, tiled=True)
    inside = (wanted >= 0) & (wanted < shard_piece.shape[0])
    taken_rows = shard_piece[jnp.clip(wanted, 0, shard_piece.shape[0] - 1)]
    chosen = jnp.where(inside[:, None, None], taken_rows, empty_tiles)
    amplitudes = lambda_amps.reshape(pair_count, tile_rows, col_count)
    ladder = jnp.einsum("pac,pcb->pab", chosen, amplitudes, preferred_element_type=jnp.float32)
    blocks = tile_mask.shape[3]
    keep_mask = tile_mask.reshape(pair_count, 1, blocks, 1).astype(jnp.float32)
    ladder = (
        ladder.reshape(pair_count, tile_rows, blocks, col_count // blocks) * keep_mask
    ).reshape(pair_count, tile_rows, col_count)
    dressed = (amplitudes.astype(jnp.float32) + ladder).astype(jnp.bfloat16)
    dressed = dressed.reshape(1, 1, pair_count, tile_rows, col_count)
    relayed = lax.all_to_all(dressed, "pair", split_axis=3, concat_axis=0, tiled=True)
    sub_index = lax.axis_index("sub")
    block_ids = jnp.arange(owners, dtype=jnp.int32) * sub_count + sub_index
    mine_ids = (
        block_ids[:, None] * pair_count + jnp.arange(pair_count, dtype=jnp.int32)[None, :]
    ).reshape(-1)
    col_pairs = pair_list[mine_ids]
    flat_rhs = relayed.reshape(owners * pair_count, -1)
    partial_value = cycle_all(coupling, pair_list, col_pairs, flat_rhs)
    partial_value = partial_value.reshape(
        owners, sub_count, pair_count, relayed.shape[3], col_count
    )
    cycle_term = lax.psum_scatter(
        partial_value.astype(jnp.bfloat16), "sub", scatter_dimension=1, tiled=True
    ).astype(jnp.float32)
    total_sum = relayed.astype(jnp.float32) + cycle_term
    energy_gap = (
        pair_gap[:, :, :, None, None]
        + row_energy[None, None, None, :, None]
        + col_energy[None, None, None, None, :]
    )
    return (-total_sum / energy_gap).astype(jnp.bfloat16)


def dress_kernel(owners, rows, me_ref, tile_of_ref, mask_ref, *refs):
    tile_refs, lam_ref = refs[:owners], refs[owners]
    chunks = rows // ROWS
    out_refs = refs[owners + 1 : owners + 1 + owners * chunks]
    tiles, dressed = refs[owners + 1 + owners * chunks :]
    me = me_ref[0]
    step = pl.program_id(0)

    @pl.when(step == 0)
    def _():
        for k in range(owners):
            tiles[k] = tile_refs[k][0]

    block = lam_ref.shape[2]
    for i in range(block):
        pair = step * block + i
        amps = lam_ref[0, 0, i]
        ladder = jnp.dot(
            tiles[tile_of_ref[0, 0, pair] ^ me], amps, preferred_element_type=jnp.float32
        )
        for part in range(mask_ref.shape[3]):
            width = amps.shape[1] // mask_ref.shape[3]
            cols = slice(part * width, (part + 1) * width)
            keep = mask_ref[0, 0, pair, part].astype(jnp.float32)
            dressed[i, :, cols] = (
                amps[:, cols].astype(jnp.float32) + keep * ladder[:, cols]
            ).astype(jnp.bfloat16)
        for k in range(owners):
            for c in range(chunks):
                start = pl.multiple_of((me ^ k) * rows + c * ROWS, ROWS)
                out_refs[k * chunks + c][i] = dressed[i, pl.ds(start, ROWS), :]


def dress(me, tile_of, tile_mask, tiles, lambda_amps):
    owners = len(tiles)
    pairs, tile_rows, cols = lambda_amps.shape[2:]
    rows = tile_rows // owners
    block = 8
    pieces = owners * (rows // ROWS)
    smem = pl.BlockSpec(memory_space=pltpu.SMEM)
    whole_tile = pl.BlockSpec((1, tile_rows, tile_rows), lambda i: (0, 0, 0))
    return pl.pallas_call(
        functools.partial(dress_kernel, owners, rows),
        grid=(pairs // block,),
        in_specs=[smem] * 3
        + [whole_tile] * owners
        + [pl.BlockSpec((1, 1, block, tile_rows, cols), lambda i: (0, 0, i, 0, 0))],
        out_specs=[pl.BlockSpec((block, ROWS, cols), lambda i: (i, 0, 0))] * pieces,
        out_shape=[jax.ShapeDtypeStruct((pairs, ROWS, cols), jnp.bfloat16)] * pieces,
        scratch_shapes=[
            pltpu.VMEM((owners, tile_rows, tile_rows), jnp.bfloat16),
            pltpu.VMEM((block, tile_rows, cols), jnp.bfloat16),
        ],
        compiler_params=pltpu.CompilerParams(vmem_limit_bytes=24 * 2**20),
        cost_estimate=pl.CostEstimate(
            flops=2 * pairs * tile_rows * tile_rows * cols,
            bytes_accessed=4 * pairs * tile_rows * cols,
            transcendentals=0,
        ),
    )(me, tile_of, tile_mask, *tiles, lambda_amps)


def finish_kernel(pieces, chunk, me_ref, row_ref, w_ref, gap_ref, col_ref, *refs):
    piece_refs = refs[:pieces]
    out_ref, xs, ys = refs[-3:]
    owners = pieces // 2
    me = me_ref[0]
    pairs, rows, cols = piece_refs[0].shape
    for j in range(pieces):
        values = piece_refs[j][...].reshape(pairs * rows, cols).astype(jnp.float32)
        xs[pl.ds(j * pairs * rows, pairs * rows), :] = values
    weights = w_ref[...]
    base = gap_ref[...]
    col = col_ref[...]
    mine = owners * pairs
    for a in range(rows):
        part = xs[pl.ds(a, pieces * pairs, stride=rows), :]
        cycle = jnp.dot(weights, part.astype(jnp.bfloat16), preferred_element_type=jnp.float32)
        energy = base + row_ref[chunk * rows + a] + col
        ys[pl.ds(a, mine, stride=rows), :] = -(part[:mine] + cycle) / energy
    for k in range(owners):
        values = ys[pl.ds(k * pairs * rows, pairs * rows), :].astype(jnp.bfloat16)
        out_ref[me ^ k, 0] = values.reshape(pairs, rows, cols)


def finish(chunk, me, row_energy, weights, gaps, col_energy, pieces, before, shape):
    pairs, rows, cols = pieces[0].shape
    owners = len(pieces) // 2
    parts = cols // LANES
    smem = pl.BlockSpec(memory_space=pltpu.SMEM)
    args = [me, row_energy, weights, gaps, col_energy, *pieces]
    in_specs = [
        smem,
        smem,
        pl.BlockSpec(weights.shape, lambda i: (0, 0)),
        pl.BlockSpec(gaps.shape, lambda i: (0, 0)),
        pl.BlockSpec((1, LANES), lambda i: (0, i)),
    ] + [pl.BlockSpec((pairs, rows, LANES), lambda i: (0, 0, i))] * len(pieces)
    aliases = {}
    if before is not None:
        aliases = {len(args): 0}
        args.append(before)
        in_specs.append(pl.BlockSpec(memory_space=pl.ANY))
    return pl.pallas_call(
        functools.partial(finish_kernel, len(pieces), chunk),
        grid=(parts,),
        in_specs=in_specs,
        out_specs=pl.BlockSpec(
            (owners, 1, pairs, rows, LANES), lambda i: (0, 0, 0, chunk, i)
        ),
        out_shape=jax.ShapeDtypeStruct(shape, jnp.bfloat16),
        scratch_shapes=[
            pltpu.VMEM((len(pieces) * pairs * rows, LANES), jnp.float32),
            pltpu.VMEM((owners * pairs * rows, LANES), jnp.float32),
        ],
        input_output_aliases=aliases,
        compiler_params=pltpu.CompilerParams(vmem_limit_bytes=24 * 2**20),
        cost_estimate=pl.CostEstimate(
            flops=2 * weights.size * rows * cols,
            bytes_accessed=3 * len(pieces) * pairs * rows * cols,
            transcendentals=0,
        ),
    )(*args)


def local_chunked(
    lambda_amps,
    integral_tiles,
    tile_of,
    tile_mask,
    pair_list,
    coupling,
    pair_gap,
    row_energy,
    col_energy,
):
    pairs, tile_rows, cols = lambda_amps.shape[2:]
    owners = lax.axis_size("pair")
    subs = lax.axis_size("sub")
    rows = tile_rows // owners
    chunks = rows // ROWS
    me = lax.axis_index("pair")
    sub = lax.axis_index("sub")
    me_ref = me.reshape(1).astype(jnp.int32)

    def to_owner(value, k):
        return lax.ppermute(value, "pair", [(o, o ^ k) for o in range(owners)])

    def to_sibling(value):
        return lax.ppermute(value, "sub", [(0, 1), (1, 0)])

    tiles = [integral_tiles] + [to_owner(integral_tiles, k) for k in range(1, owners)]
    sent = dress(me_ref, tile_of, tile_mask, tiles, lambda_amps)
    order = list(range(owners - 1, 0, -1))

    direct = [[None] * owners for _ in range(chunks)]
    other = [[None] * owners for _ in range(chunks)]
    for c in range(chunks):
        direct[c][0] = sent[c]
        other[c][0] = to_sibling(sent[c])
        for k in order:
            piece = sent[k * chunks + c]
            direct[c][k] = to_owner(piece, k)
            other[c][k] = to_sibling(direct[c][k])

    slot_owner = me ^ jnp.arange(owners, dtype=jnp.int32)
    sub_of = jnp.stack([sub, 1 - sub]).astype(jnp.int32)
    block_ids = slot_owner[None, :] * subs + sub_of[:, None]
    ids = (
        block_ids[:, :, None] * pairs + jnp.arange(pairs, dtype=jnp.int32)
    ).reshape(-1)
    slot_pairs = pair_list[ids]
    left_table, right_table = column_tables(coupling, slot_pairs)
    weights = cycle_rows(left_table, right_table, slot_pairs[: owners * pairs])
    gaps = jnp.broadcast_to(
        pair_gap[slot_owner].reshape(owners * pairs, 1), (owners * pairs, LANES)
    )
    col = col_energy.reshape(1, cols)

    shape = (owners, 1, pairs, rows, cols)
    result = None
    for c in range(chunks):
        result = finish(
            c, me_ref, row_energy, weights, gaps, col, direct[c] + other[c], result, shape
        )
    return result


def solution(mesh):
    placed = (
        P(("mol", "pair"), "sub", None, None, "tile"),
        P(("mol", "pair"), None, None),
        P(("mol", "pair"), "sub", None),
        P(("mol", "pair"), "sub", None, "tile"),
        P("mol", None),
        P("mol", None),
        P("mol", "sub", None),
        P(("mol", "pair")),
        P(("mol", "tile")),
    )
    owners, subs = mesh.shape["pair"], mesh.shape["sub"]

    def local(*args):
        tile_rows, cols = args[0].shape[3:]
        rows = tile_rows // owners
        power = owners & (owners - 1) == 0
        fits = rows % ROWS == 0 and cols % LANES == 0 and args[1].shape[0] == 1
        if power and fits and subs == 2 and args[0].shape[2] % 8 == 0:
            return local_chunked(*args)
        return local_general(*args)

    return jax.shard_map(
        local,
        mesh=mesh,
        in_specs=placed,
        out_specs=P("mol", "sub", None, "pair", "tile"),
        check_vma=False,
    )
```

```python
import functools
import math

import jax
import jax.numpy as jnp
from jax import lax
from jax.experimental import pallas as pl
from jax.experimental.pallas import tpu as pltpu
from jax.sharding import PartitionSpec as P

ROWS = 16
LANES = 128
VMEM_BYTES = 24 * 2**20


def column_tables(coupling, col_pairs):
    left_table = jnp.take(coupling.T, col_pairs[:, 0], axis=0).T
    right_table = jnp.take(coupling.T, col_pairs[:, 1], axis=0).T
    return (left_table, right_table)


def cycle_rows(left_table, right_table, row_pairs):
    left_part = jnp.take(left_table, row_pairs[:, 0], axis=0)
    right_part = jnp.take(right_table, row_pairs[:, 1], axis=0)
    return (left_part * right_part).astype(jnp.bfloat16)


def cycle_all(coupling, pair_list, col_pairs, flat_rhs):
    total_pairs = pair_list.shape[0]
    step_rows = math.gcd(total_pairs, 512)
    row_blocks = pair_list.reshape(total_pairs // step_rows, step_rows, 2)
    left_table, right_table = column_tables(coupling, col_pairs)

    def one_block(row_pairs):
        weights = cycle_rows(left_table, right_table, row_pairs)
        return jnp.dot(weights, flat_rhs, preferred_element_type=jnp.float32)

    return lax.map(one_block, row_blocks).reshape(total_pairs, -1)


def local_general(
    lambda_amps,
    integral_tiles,
    tile_of,
    tile_mask,
    pair_list,
    coupling,
    pair_gap,
    row_energy,
    col_energy,
):
    pair_count = lambda_amps.shape[2]
    tile_rows = lambda_amps.shape[3]
    col_count = lambda_amps.shape[4]
    owners = lax.axis_size("pair")
    sub_count = lax.axis_size("sub")
    wanted = tile_of.reshape(pair_count)
    empty_tiles = jnp.zeros((pair_count, tile_rows, tile_rows), integral_tiles.dtype)
    shard_piece = lax.all_gather(integral_tiles, "pair", axis=0, tiled=True)
    inside = (wanted >= 0) & (wanted < shard_piece.shape[0])
    taken_rows = shard_piece[jnp.clip(wanted, 0, shard_piece.shape[0] - 1)]
    chosen = jnp.where(inside[:, None, None], taken_rows, empty_tiles)
    amplitudes = lambda_amps.reshape(pair_count, tile_rows, col_count)
    ladder = jnp.einsum("pac,pcb->pab", chosen, amplitudes, preferred_element_type=jnp.float32)
    blocks = tile_mask.shape[3]
    keep_mask = tile_mask.reshape(pair_count, 1, blocks, 1).astype(jnp.float32)
    ladder = (
        ladder.reshape(pair_count, tile_rows, blocks, col_count // blocks) * keep_mask
    ).reshape(pair_count, tile_rows, col_count)
    dressed = (amplitudes.astype(jnp.float32) + ladder).astype(jnp.bfloat16)
    dressed = dressed.reshape(1, 1, pair_count, tile_rows, col_count)
    relayed = lax.all_to_all(dressed, "pair", split_axis=3, concat_axis=0, tiled=True)
    sub_index = lax.axis_index("sub")
    block_ids = jnp.arange(owners, dtype=jnp.int32) * sub_count + sub_index
    mine_ids = (
        block_ids[:, None] * pair_count + jnp.arange(pair_count, dtype=jnp.int32)[None, :]
    ).reshape(-1)
    col_pairs = pair_list[mine_ids]
    flat_rhs = relayed.reshape(owners * pair_count, -1)
    partial_value = cycle_all(coupling, pair_list, col_pairs, flat_rhs)
    partial_value = partial_value.reshape(
        owners, sub_count, pair_count, relayed.shape[3], col_count
    )
    cycle_term = lax.psum_scatter(
        partial_value.astype(jnp.bfloat16), "sub", scatter_dimension=1, tiled=True
    ).astype(jnp.float32)
    total_sum = relayed.astype(jnp.float32) + cycle_term
    energy_gap = (
        pair_gap[:, :, :, None, None]
        + row_energy[None, None, None, :, None]
        + col_energy[None, None, None, None, :]
    )
    return (-total_sum / energy_gap).astype(jnp.bfloat16)


def one_hot(shape, hits):
    return jnp.where(hits, 1.0, 0.0).astype(jnp.bfloat16).reshape(shape)


def swap_matrix():
    size = ROWS * ROWS
    to = lax.broadcasted_iota(jnp.int32, (size, size), 0)
    frm = lax.broadcasted_iota(jnp.int32, (size, size), 1)
    hits = to == (frm % ROWS) * ROWS + frm // ROWS
    return one_hot((size, size), hits)


def split3(value):
    high = value.astype(jnp.bfloat16)
    rest = value - high.astype(jnp.float32)
    mid = rest.astype(jnp.bfloat16)
    low = (rest - mid.astype(jnp.float32)).astype(jnp.bfloat16)
    return high, mid, low


def pick_columns(value, columns):
    high, mid, low = (
        jnp.dot(part, columns, preferred_element_type=jnp.float32) for part in split3(value)
    )
    return high + (mid + low)


def pick_rows(columns, value):
    dims = (((0,), (0,)), ((), ()))
    high, mid, low = (
        lax.dot_general(columns, part, dims, preferred_element_type=jnp.float32)
        for part in split3(value)
    )
    return high + (mid + low)


def weights_kernel(pair_ref, coupling_ref, gap_ref, sub_ref, w_ref, gaps_ref, full):
    total = pair_ref.shape[1]
    depth = coupling_ref.shape[0]
    orbital = lax.broadcasted_iota(jnp.int32, (depth, total), 0)
    coupling = coupling_ref[...]
    product = None
    for side in range(2):
        columns = one_hot((depth, total), orbital == pair_ref[side : side + 1, :])
        picked = pick_rows(columns, pick_columns(coupling, columns))
        product = picked if product is None else product * picked
    full[...] = product
    owners, _, pairs = gap_ref.shape
    subs = total // (owners * pairs)
    diagonal = lax.broadcasted_iota(jnp.int32, (pairs, pairs), 0) == lax.broadcasted_iota(
        jnp.int32, (pairs, pairs), 1
    )
    for o in range(owners):
        start = pl.multiple_of((o * subs + sub_ref[0]) * pairs, pairs)
        rows = pl.ds(o * pairs, pairs)
        w_ref[rows, :] = full[pl.ds(start, pairs), :].astype(jnp.bfloat16)
        column = jnp.sum(jnp.where(diagonal, gap_ref[o], 0.0), axis=1, keepdims=True)
        gaps_ref[rows, :] = jnp.broadcast_to(column, (pairs, LANES))


def make_weights(pair_list, coupling, pair_gap, sub_ref):
    owners, _, pairs = pair_gap.shape
    total = pair_list.shape[0]
    mine = owners * pairs
    vmem = pl.BlockSpec(memory_space=pltpu.VMEM)
    return pl.pallas_call(
        weights_kernel,
        in_specs=[vmem, vmem, vmem, pl.BlockSpec(memory_space=pltpu.SMEM)],
        out_specs=[vmem, vmem],
        out_shape=[
            jax.ShapeDtypeStruct((mine, total), jnp.bfloat16),
            jax.ShapeDtypeStruct((mine, LANES), jnp.float32),
        ],
        scratch_shapes=[pltpu.VMEM((total, total), jnp.float32)],
        compiler_params=pltpu.CompilerParams(vmem_limit_bytes=VMEM_BYTES),
        cost_estimate=pl.CostEstimate(
            flops=12 * total * coupling.size, bytes_accessed=4 * coupling.size, transcendentals=0
        ),
    )(pair_list.T, coupling, pair_gap, sub_ref)


def dress_kernel(owners, rows, chunk, me_ref, tile_of_ref, mask_ref, *refs):
    tile_refs, lam_ref = refs[:owners], refs[owners]
    out_refs = refs[owners + 1 : 2 * owners + 1]
    tiles = refs[-1]
    me = me_ref[0]
    step = pl.program_id(0)
    starts = [pl.multiple_of((me ^ k) * rows + chunk * ROWS, ROWS) for k in range(owners)]

    @pl.when(step == 0)
    def _():
        for k in range(owners):
            for j in range(owners):
                tiles[k, pl.ds(j * ROWS, ROWS), :] = tile_refs[k][0, pl.ds(starts[j], ROWS), :]

    block = lam_ref.shape[2]
    parts = mask_ref.shape[2]
    for i in range(block):
        pair = step * block + i
        ladder = jnp.dot(
            tiles[tile_of_ref[0, 0, pair] ^ me],
            lam_ref[0, 0, i],
            preferred_element_type=jnp.float32,
        )
        width = ladder.shape[1] // parts
        for part in range(parts):
            keep = mask_ref[0, 0, part, pair].astype(jnp.float32)
            cols = slice(part * width, (part + 1) * width)
            for k in range(owners):
                amps = lam_ref[0, 0, i, pl.ds(starts[k], ROWS), cols].astype(jnp.float32)
                kept = keep * ladder[k * ROWS : (k + 1) * ROWS, cols]
                out_refs[k][i, :, cols] = (amps + kept).astype(jnp.bfloat16)


def dress(chunk, me, tile_of, tile_mask, tiles, lambda_amps):
    owners = len(tiles)
    pairs, tile_rows, cols = lambda_amps.shape[2:]
    rows = tile_rows // owners
    block = 8
    smem = pl.BlockSpec(memory_space=pltpu.SMEM)
    whole_tile = pl.BlockSpec((1, tile_rows, tile_rows), lambda i: (0, 0, 0))
    return pl.pallas_call(
        functools.partial(dress_kernel, owners, rows, chunk),
        grid=(pairs // block,),
        in_specs=[smem] * 3
        + [whole_tile] * owners
        + [pl.BlockSpec((1, 1, block, tile_rows, cols), lambda i: (0, 0, i, 0, 0))],
        out_specs=[pl.BlockSpec((block, ROWS, cols), lambda i: (i, 0, 0))] * owners,
        out_shape=[jax.ShapeDtypeStruct((pairs, ROWS, cols), jnp.bfloat16)] * owners,
        scratch_shapes=[pltpu.VMEM((owners, owners * ROWS, tile_rows), jnp.bfloat16)],
        compiler_params=pltpu.CompilerParams(vmem_limit_bytes=VMEM_BYTES),
        cost_estimate=pl.CostEstimate(
            flops=2 * pairs * owners * ROWS * tile_rows * cols,
            bytes_accessed=3 * pairs * tile_rows * cols,
            transcendentals=0,
        ),
    )(me, tile_of, jnp.swapaxes(tile_mask, 2, 3), *tiles, lambda_amps)


def finish_kernel(pieces, chunk, place_ref, row_ref, w_ref, gap_ref, col_ref, *refs):
    piece_refs = refs[:pieces]
    out_ref, landed, xs, ys, done, in_sems, out_sems = refs[-7:]
    pairs, rows, cols = piece_refs[0].shape
    owners = pieces // 2
    halves = pairs // ROWS
    me, sub = place_ref[0], place_ref[1]
    arrivals = [
        pltpu.make_async_copy(piece_refs[j], landed.at[j], in_sems.at[j]) for j in range(pieces)
    ]
    for copy in arrivals:
        copy.start()
    swap = swap_matrix()
    for j in range(pieces):
        arrivals[j].wait()
        block = ((me ^ (j % owners)) * 2 + (sub ^ (j // owners))) * pairs
        for h in range(halves):
            rows_in = landed[j, pl.ds(h * ROWS, ROWS)].reshape(ROWS * rows, cols)
            turned = jnp.dot(swap, rows_in, preferred_element_type=jnp.float32)
            place = pl.multiple_of(block + h * ROWS, ROWS)
            xs[:, pl.ds(place, ROWS), :] = turned.astype(jnp.bfloat16).reshape(rows, ROWS, cols)
    weights = w_ref[...]
    col = col_ref[...]
    for a in range(rows):
        cycle = jnp.dot(weights, xs[a], preferred_element_type=jnp.float32)
        row = row_ref[chunk * rows + a]
        for o in range(owners):
            mine = slice(o * pairs, (o + 1) * pairs)
            start = pl.multiple_of((o * 2 + sub) * pairs, pairs)
            own = xs[a, pl.ds(start, pairs), :].astype(jnp.float32)
            level = gap_ref[mine, :] + row
            energy = jnp.concatenate([level] * (cols // LANES), axis=1) + col
            value = (-(own + cycle[mine]) / energy).astype(jnp.bfloat16)
            for h in range(halves):
                ys[o * halves + h, pl.ds(a * ROWS, ROWS), :] = value[h * ROWS : (h + 1) * ROWS]
    leaving = []
    for g in range(owners * halves):
        turned = jnp.dot(swap, ys[g], preferred_element_type=jnp.float32)
        done[g] = turned.astype(jnp.bfloat16).reshape(ROWS, rows, cols)
        o, h = g // halves, g % halves
        copy = pltpu.make_async_copy(
            done.at[g],
            out_ref.at[o, 0, pl.ds(h * ROWS, ROWS), pl.ds(chunk * rows, rows), :],
            out_sems.at[g],
        )
        copy.start()
        leaving.append(copy)
    for copy in leaving:
        copy.wait()


def finish(chunk, place, row_energy, weights, gaps, col_energy, pieces, before, shape):
    pairs, rows, cols = pieces[0].shape
    owners = len(pieces) // 2
    groups = owners * (pairs // ROWS)
    smem = pl.BlockSpec(memory_space=pltpu.SMEM)
    vmem = pl.BlockSpec(memory_space=pltpu.VMEM)
    anywhere = pl.BlockSpec(memory_space=pl.ANY)
    args = [place, row_energy, weights, gaps, col_energy, *pieces]
    in_specs = [smem, smem, vmem, vmem, vmem] + [anywhere] * len(pieces)
    aliases = {}
    if before is not None:
        aliases = {len(args): 0}
        args.append(before)
        in_specs.append(anywhere)
    return pl.pallas_call(
        functools.partial(finish_kernel, len(pieces), chunk),
        in_specs=in_specs,
        out_specs=anywhere,
        out_shape=jax.ShapeDtypeStruct(shape, jnp.bfloat16),
        scratch_shapes=[
            pltpu.VMEM((len(pieces), pairs, rows, cols), jnp.bfloat16),
            pltpu.VMEM((rows, len(pieces) * pairs, cols), jnp.bfloat16),
            pltpu.VMEM((groups, ROWS * rows, cols), jnp.bfloat16),
            pltpu.VMEM((groups, ROWS, rows, cols), jnp.bfloat16),
            pltpu.SemaphoreType.DMA((len(pieces),)),
            pltpu.SemaphoreType.DMA((groups,)),
        ],
        input_output_aliases=aliases,
        compiler_params=pltpu.CompilerParams(vmem_limit_bytes=VMEM_BYTES),
        cost_estimate=pl.CostEstimate(
            flops=8 * weights.size * rows * cols,
            bytes_accessed=3 * len(pieces) * pairs * rows * cols,
            transcendentals=0,
        ),
    )(*args)


def local_chunked(
    lambda_amps,
    integral_tiles,
    tile_of,
    tile_mask,
    pair_list,
    coupling,
    pair_gap,
    row_energy,
    col_energy,
):
    pairs, tile_rows, cols = lambda_amps.shape[2:]
    owners = lax.axis_size("pair")
    rows = tile_rows // owners
    chunks = rows // ROWS
    me = lax.axis_index("pair").astype(jnp.int32)
    sub = lax.axis_index("sub").astype(jnp.int32)
    place = jnp.stack([me, sub])

    def to_owner(value, k):
        return lax.ppermute(value, "pair", [(o, o ^ k) for o in range(owners)])

    def to_sibling(value):
        return lax.ppermute(value, "sub", [(0, 1), (1, 0)])

    def after(value, earlier):
        return value if earlier is None else lax.optimization_barrier((value, earlier))[0]

    tiles = [integral_tiles] + [to_owner(integral_tiles, k) for k in range(1, owners)]
    weights, gaps = make_weights(pair_list, coupling, pair_gap, sub.reshape(1))
    sent = [
        dress(c, me.reshape(1), tile_of, tile_mask, tiles, lambda_amps) for c in range(chunks)
    ]
    direct = [[sent[c][0]] + [None] * (owners - 1) for c in range(chunks)]
    other = [[None] * owners for _ in range(chunks)]
    queue = [(c, k) for c in range(chunks) for k in range(owners - 1, 0, -1)]
    ahead = 4
    for n, (c, k) in enumerate(queue):
        earlier = None
        if n >= ahead:
            was, slot = queue[n - ahead]
            earlier = direct[was][slot]
            earlier = (earlier, weights)
        direct[c][k] = to_owner(after(sent[c][k], earlier), k)

    shape = (owners, 1, pairs, rows, cols)
    col = col_energy.reshape(1, cols)
    result = None
    for c in range(chunks):
        other[c][0] = to_sibling(after(sent[c][0], direct[c][owners - 1]))
        for k in range(owners - 1, 0, -1):
            other[c][k] = to_sibling(after(direct[c][k], result if k == 1 else None))
        result = finish(
            c, place, row_energy, weights, gaps, col, direct[c] + other[c], result, shape
        )
    return result


def solution(mesh):
    placed = (
        P(("mol", "pair"), "sub", None, None, "tile"),
        P(("mol", "pair"), None, None),
        P(("mol", "pair"), "sub", None),
        P(("mol", "pair"), "sub", None, "tile"),
        P("mol", None),
        P("mol", None),
        P("mol", "sub", None),
        P(("mol", "pair")),
        P(("mol", "tile")),
    )
    owners, subs = mesh.shape["pair"], mesh.shape["sub"]

    def local(*args):
        tile_rows, cols = args[0].shape[3:]
        rows = tile_rows // owners
        power = owners & (owners - 1) == 0
        fits = rows % ROWS == 0 and cols % LANES == 0 and args[1].shape[0] == 1
        if power and fits and subs == 2 and args[0].shape[2] % ROWS == 0:
            return local_chunked(*args)
        return local_general(*args)

    return jax.shard_map(
        local,
        mesh=mesh,
        in_specs=placed,
        out_specs=P("mol", "sub", None, "pair", "tile"),
        check_vma=False,
    )
```

```python
import functools
import math

import jax
import jax.numpy as jnp
from jax import lax
from jax.experimental import pallas as pl
from jax.experimental.pallas import tpu as pltpu
from jax.sharding import PartitionSpec as P

ROWS = 16
LANES = 128
VMEM_BYTES = 24 * 2**20


def column_tables(coupling, col_pairs):
    left_table = jnp.take(coupling.T, col_pairs[:, 0], axis=0).T
    right_table = jnp.take(coupling.T, col_pairs[:, 1], axis=0).T
    return (left_table, right_table)


def cycle_rows(left_table, right_table, row_pairs):
    left_part = jnp.take(left_table, row_pairs[:, 0], axis=0)
    right_part = jnp.take(right_table, row_pairs[:, 1], axis=0)
    return (left_part * right_part).astype(jnp.bfloat16)


def cycle_all(coupling, pair_list, col_pairs, flat_rhs):
    total_pairs = pair_list.shape[0]
    step_rows = math.gcd(total_pairs, 512)
    row_blocks = pair_list.reshape(total_pairs // step_rows, step_rows, 2)
    left_table, right_table = column_tables(coupling, col_pairs)

    def one_block(row_pairs):
        weights = cycle_rows(left_table, right_table, row_pairs)
        return jnp.dot(weights, flat_rhs, preferred_element_type=jnp.float32)

    return lax.map(one_block, row_blocks).reshape(total_pairs, -1)


def local_general(
    lambda_amps,
    integral_tiles,
    tile_of,
    tile_mask,
    pair_list,
    coupling,
    pair_gap,
    row_energy,
    col_energy,
):
    pair_count = lambda_amps.shape[2]
    tile_rows = lambda_amps.shape[3]
    col_count = lambda_amps.shape[4]
    owners = lax.axis_size("pair")
    sub_count = lax.axis_size("sub")
    wanted = tile_of.reshape(pair_count)
    empty_tiles = jnp.zeros((pair_count, tile_rows, tile_rows), integral_tiles.dtype)
    shard_piece = lax.all_gather(integral_tiles, "pair", axis=0, tiled=True)
    inside = (wanted >= 0) & (wanted < shard_piece.shape[0])
    taken_rows = shard_piece[jnp.clip(wanted, 0, shard_piece.shape[0] - 1)]
    chosen = jnp.where(inside[:, None, None], taken_rows, empty_tiles)
    amplitudes = lambda_amps.reshape(pair_count, tile_rows, col_count)
    ladder = jnp.einsum("pac,pcb->pab", chosen, amplitudes, preferred_element_type=jnp.float32)
    blocks = tile_mask.shape[3]
    keep_mask = tile_mask.reshape(pair_count, 1, blocks, 1).astype(jnp.float32)
    ladder = (
        ladder.reshape(pair_count, tile_rows, blocks, col_count // blocks) * keep_mask
    ).reshape(pair_count, tile_rows, col_count)
    dressed = (amplitudes.astype(jnp.float32) + ladder).astype(jnp.bfloat16)
    dressed = dressed.reshape(1, 1, pair_count, tile_rows, col_count)
    relayed = lax.all_to_all(dressed, "pair", split_axis=3, concat_axis=0, tiled=True)
    sub_index = lax.axis_index("sub")
    block_ids = jnp.arange(owners, dtype=jnp.int32) * sub_count + sub_index
    mine_ids = (
        block_ids[:, None] * pair_count + jnp.arange(pair_count, dtype=jnp.int32)[None, :]
    ).reshape(-1)
    col_pairs = pair_list[mine_ids]
    flat_rhs = relayed.reshape(owners * pair_count, -1)
    partial_value = cycle_all(coupling, pair_list, col_pairs, flat_rhs)
    partial_value = partial_value.reshape(
        owners, sub_count, pair_count, relayed.shape[3], col_count
    )
    cycle_term = lax.psum_scatter(
        partial_value.astype(jnp.bfloat16), "sub", scatter_dimension=1, tiled=True
    ).astype(jnp.float32)
    total_sum = relayed.astype(jnp.float32) + cycle_term
    energy_gap = (
        pair_gap[:, :, :, None, None]
        + row_energy[None, None, None, :, None]
        + col_energy[None, None, None, None, :]
    )
    return (-total_sum / energy_gap).astype(jnp.bfloat16)


def one_hot(hits):
    return jnp.where(hits, 1.0, 0.0).astype(jnp.bfloat16)


def square_iotas(size):
    return (lax.broadcasted_iota(jnp.int32, (size, size), axis) for axis in range(2))


def swap_matrix():
    to, frm = square_iotas(ROWS * ROWS)
    return one_hot(to == (frm % ROWS) * ROWS + frm // ROWS)


def split3(value):
    high = value.astype(jnp.bfloat16)
    rest = value - high.astype(jnp.float32)
    mid = rest.astype(jnp.bfloat16)
    low = (rest - mid.astype(jnp.float32)).astype(jnp.bfloat16)
    return high, mid, low


def pick_columns(value, columns):
    high, mid, low = (
        jnp.dot(part, columns, preferred_element_type=jnp.float32) for part in split3(value)
    )
    return high + (mid + low)


def pick_rows(columns, value):
    dims = (((0,), (0,)), ((), ()))
    high, mid, low = (
        lax.dot_general(columns, part, dims, preferred_element_type=jnp.float32)
        for part in split3(value)
    )
    return high + (mid + low)


def prepare_kernel(pair_ref, coupling_ref, gap_ref, place_ref, lam_ref, w_ref, gaps_ref, held_ref, full, sems):
    halves = sems.shape[0]
    step = lam_ref.shape[2] // halves
    copies = [
        pltpu.make_async_copy(
            lam_ref.at[:, :, pl.ds(i * step, step)], held_ref.at[:, :, pl.ds(i * step, step)], sems.at[i]
        )
        for i in range(halves)
    ]
    for copy in copies:
        copy.start()
    total = pair_ref.shape[1]
    depth = coupling_ref.shape[0]
    owners, _, pairs = gap_ref.shape
    me, sub = place_ref[0], place_ref[1]
    orbital = lax.broadcasted_iota(jnp.int32, (depth, total), 0)
    coupling = coupling_ref[...]
    product = None
    for side in range(2):
        columns = one_hot(orbital == pair_ref[side : side + 1, :])
        picked = pick_rows(columns, pick_columns(coupling, columns))
        product = picked if product is None else product * picked
    frm, to = square_iotas(total)
    block, within = to // pairs, to % pairs
    source = ((me ^ (block % owners)) * 2 + (sub ^ (block // owners))) * pairs + within
    turned = jnp.dot(
        product.astype(jnp.bfloat16), one_hot(frm == source), preferred_element_type=jnp.float32
    )
    full[...] = turned
    row, column = square_iotas(pairs)
    for k in range(owners):
        start = pl.multiple_of(((me ^ k) * 2 + sub) * pairs, pairs)
        rows = pl.ds(k * pairs, pairs)
        w_ref[rows, :] = full[pl.ds(start, pairs), :].astype(jnp.bfloat16)
        gap = jnp.sum(jnp.where(row == column, gap_ref[me ^ k], 0.0), axis=1, keepdims=True)
        gaps_ref[rows, :] = jnp.broadcast_to(gap, (pairs, LANES))
    for copy in copies:
        copy.wait()


def prepare(pair_list, coupling, pair_gap, place, lambda_amps):
    owners, _, pairs = pair_gap.shape
    total = pair_list.shape[0]
    mine = owners * pairs
    vmem = pl.BlockSpec(memory_space=pltpu.VMEM)
    anywhere = pl.BlockSpec(memory_space=pl.ANY)
    fixed = [
        pltpu.with_memory_space_constraint(value, pltpu.HBM)
        for value in (pair_list.T, coupling, pair_gap)
    ]
    return pl.pallas_call(
        prepare_kernel,
        in_specs=[vmem, vmem, vmem, pl.BlockSpec(memory_space=pltpu.SMEM), anywhere],
        out_specs=[vmem, vmem, anywhere],
        out_shape=[
            jax.ShapeDtypeStruct((mine, total), jnp.bfloat16),
            jax.ShapeDtypeStruct((mine, LANES), jnp.float32),
            jax.ShapeDtypeStruct(lambda_amps.shape, lambda_amps.dtype),
        ],
        scratch_shapes=[
            pltpu.VMEM((total, total), jnp.float32),
            pltpu.SemaphoreType.DMA((4,)),
        ],
        compiler_params=pltpu.CompilerParams(vmem_limit_bytes=VMEM_BYTES),
        cost_estimate=pl.CostEstimate(
            flops=12 * total * coupling.size,
            bytes_accessed=4 * coupling.size + 4 * lambda_amps.size,
            transcendentals=0,
        ),
    )(*fixed, place, pltpu.with_memory_space_constraint(lambda_amps, pltpu.HBM))


def dress_kernel(owners, rows, groups, place_ref, tile_of_ref, mask_ref, *refs):
    tile_refs, lam_ref = refs[:owners], refs[owners]
    out_refs = refs[owners + 1 : -2]
    tiles, stage = refs[-2:]
    me = place_ref[0]
    flat = [(k, c, out, j) for out, group in zip(out_refs, groups) for j, (k, c) in enumerate(group)]
    starts = [pl.multiple_of((me ^ k) * rows + c * ROWS, ROWS) for k, c, _, _ in flat]
    for k in range(owners):
        for n, start in enumerate(starts):
            tiles[k, pl.ds(n * ROWS, ROWS), :] = tile_refs[k][0, pl.ds(start, ROWS), :]
    swap = swap_matrix()
    parts = mask_ref.shape[2]
    for g in range(lam_ref.shape[2] // ROWS):
        for i in range(ROWS):
            pair = g * ROWS + i
            ladder = jnp.dot(
                tiles[tile_of_ref[0, 0, pair] ^ me],
                lam_ref[0, 0, pair],
                preferred_element_type=jnp.float32,
            )
            width = ladder.shape[1] // parts
            for part in range(parts):
                keep = mask_ref[0, 0, part, pair].astype(jnp.float32)
                cols = slice(part * width, (part + 1) * width)
                for n, start in enumerate(starts):
                    amps = lam_ref[0, 0, pair, pl.ds(start, ROWS), cols].astype(jnp.float32)
                    kept = keep * ladder[n * ROWS : (n + 1) * ROWS, cols]
                    stage[g, n, pl.ds(i * ROWS, ROWS), cols] = (amps + kept).astype(jnp.bfloat16)
        for n, (_, _, out, j) in enumerate(flat):
            turned = jnp.dot(swap, stage[g, n], preferred_element_type=jnp.float32)
            out[j, :, pl.ds(g * ROWS, ROWS), :] = turned.astype(jnp.bfloat16).reshape(
                ROWS, ROWS, turned.shape[1]
            )


def dress(groups, place, tile_of, tile_mask, tiles, lambda_amps):
    owners = len(tiles)
    pairs, tile_rows, cols = lambda_amps.shape[2:]
    rows = tile_rows // owners
    smem = pl.BlockSpec(memory_space=pltpu.SMEM)
    vmem = pl.BlockSpec(memory_space=pltpu.VMEM)
    count = sum(len(group) for group in groups)
    return pl.pallas_call(
        functools.partial(dress_kernel, owners, rows, groups),
        in_specs=[smem] * 3 + [vmem] * (owners + 1),
        out_specs=[vmem] * len(groups),
        out_shape=[
            jax.ShapeDtypeStruct((len(group), ROWS, pairs, cols), jnp.bfloat16)
            for group in groups
        ],
        scratch_shapes=[
            pltpu.VMEM((owners, count * ROWS, tile_rows), jnp.bfloat16),
            pltpu.VMEM((pairs // ROWS, count, ROWS * ROWS, cols), jnp.bfloat16),
        ],
        compiler_params=pltpu.CompilerParams(vmem_limit_bytes=VMEM_BYTES),
        cost_estimate=pl.CostEstimate(
            flops=2 * pairs * count * ROWS * tile_rows * cols,
            bytes_accessed=3 * pairs * tile_rows * cols,
            transcendentals=0,
        ),
    )(place, tile_of, jnp.swapaxes(tile_mask, 2, 3), *tiles, lambda_amps)


def finish_kernel(pieces, chunk, place_ref, row_ref, w_ref, gap_ref, col_ref, *refs):
    piece_refs = refs[:pieces]
    out_ref, ys, done, sems = refs[-4:]
    _, rows, pairs, cols = piece_refs[0].shape
    owners = pieces // 2
    halves = pairs // ROWS
    mine = owners * pairs
    me = place_ref[0]
    weights = w_ref[...]
    col = col_ref[...]
    for a in range(rows):
        amps = jnp.concatenate([piece_refs[j][0, a] for j in range(pieces)], axis=0)
        cycle = jnp.dot(weights, amps, preferred_element_type=jnp.float32)
        level = gap_ref[...] + row_ref[chunk * rows + a]
        energy = jnp.concatenate([level] * (cols // LANES), axis=1) + col
        value = (-(amps[:mine].astype(jnp.float32) + cycle) / energy).astype(jnp.bfloat16)
        for g in range(owners * halves):
            ys[g, pl.ds(a * ROWS, ROWS), :] = value[g * ROWS : (g + 1) * ROWS]
    swap = swap_matrix()
    leaving = []
    for g in range(owners * halves):
        turned = jnp.dot(swap, ys[g], preferred_element_type=jnp.float32)
        done[g] = turned.astype(jnp.bfloat16).reshape(ROWS, rows, cols)
        k, h = g // halves, g % halves
        copy = pltpu.make_async_copy(
            done.at[g],
            out_ref.at[me ^ k, 0, pl.ds(h * ROWS, ROWS), pl.ds(chunk * rows, rows), :],
            sems.at[g],
        )
        copy.start()
        leaving.append(copy)
    for copy in leaving:
        copy.wait()


def finish(chunk, place, row_energy, weights, gaps, col_energy, pieces, before, shape):
    _, rows, pairs, cols = pieces[0][0].shape
    owners = len(pieces) // 2
    groups = owners * (pairs // ROWS)
    smem = pl.BlockSpec(memory_space=pltpu.SMEM)
    anywhere = pl.BlockSpec(memory_space=pl.ANY)
    args = [place, row_energy, weights, gaps, col_energy] + [piece for piece, _ in pieces]
    in_specs = [smem, smem]
    in_specs += [pl.BlockSpec(value.shape, lambda i: (0, 0)) for value in args[2:5]]
    for _, index in pieces:
        in_specs.append(
            pl.BlockSpec((1, rows, pairs, cols), lambda i, index=index: (index, 0, 0, 0))
        )
    aliases = {}
    if before is not None:
        aliases = {len(args): 0}
        args.append(before)
        in_specs.append(anywhere)
    return pl.pallas_call(
        functools.partial(finish_kernel, len(pieces), chunk),
        grid=(1,),
        in_specs=in_specs,
        out_specs=anywhere,
        out_shape=jax.ShapeDtypeStruct(shape, jnp.bfloat16),
        scratch_shapes=[
            pltpu.VMEM((groups, ROWS * rows, cols), jnp.bfloat16),
            pltpu.VMEM((groups, ROWS, rows, cols), jnp.bfloat16),
            pltpu.SemaphoreType.DMA((groups,)),
        ],
        input_output_aliases=aliases,
        compiler_params=pltpu.CompilerParams(vmem_limit_bytes=VMEM_BYTES),
        cost_estimate=pl.CostEstimate(flops=0, bytes_accessed=0, transcendentals=0),
    )(*args)


def local_chunked(
    lambda_amps,
    integral_tiles,
    tile_of,
    tile_mask,
    pair_list,
    coupling,
    pair_gap,
    row_energy,
    col_energy,
):
    pairs, tile_rows, cols = lambda_amps.shape[2:]
    owners = lax.axis_size("pair")
    rows = tile_rows // owners
    chunks = rows // ROWS
    me = lax.axis_index("pair").astype(jnp.int32)
    sub = lax.axis_index("sub").astype(jnp.int32)
    place = jnp.stack([me, sub])

    def to_owner(value, k):
        return lax.ppermute(value, "pair", [(o, o ^ k) for o in range(owners)])

    def to_sibling(value):
        return lax.ppermute(value, "sub", [(0, 1), (1, 0)])

    def after(value, earlier):
        return value if earlier is None else lax.optimization_barrier((value, earlier))[0]

    tiles = [integral_tiles] + [to_owner(integral_tiles, k) for k in range(1, owners)]
    weights, gaps, held = prepare(pair_list, coupling, pair_gap, place, lambda_amps)

    far = list(range(owners - 1, 1, -1))
    first = [((k, 0),) for k in far]
    near = [tuple((k, c) for c in range(chunks)) for k in (1, 0)]
    rest = near + [((k, c),) for c in range(1, chunks) for k in far]
    direct = {}
    for groups in (first, rest):
        sent = dress(groups, place, tile_of, tile_mask, tiles, held)
        held = after(held, sent[0])
        for group, value in zip(groups, sent):
            k = group[0][0]
            landed = to_owner(value, k) if k else value
            for index, key in enumerate(group):
                direct[key] = (landed, index)

    shape = (owners, 1, pairs, rows, cols)
    col = col_energy.reshape(1, cols)
    result, other = None, {}
    for c in range(chunks):
        for k in far:
            value, index = direct[k, c]
            other[k, c] = (to_sibling(value), index)
        if c == 0:
            for k in (0, 1):
                value, _ = direct[k, 0]
                if k == 0:
                    value = after(value, direct[far[0], 0][0])
                passed = to_sibling(value)
                for index in range(chunks):
                    other[k, index] = (passed, index)
        pieces = [held_by[k, c] for held_by in (direct, other) for k in range(owners)]
        result = finish(c, place, row_energy, weights, gaps, col, pieces, result, shape)
    return result


def solution(mesh):
    placed = (
        P(("mol", "pair"), "sub", None, None, "tile"),
        P(("mol", "pair"), None, None),
        P(("mol", "pair"), "sub", None),
        P(("mol", "pair"), "sub", None, "tile"),
        P("mol", None),
        P("mol", None),
        P("mol", "sub", None),
        P(("mol", "pair")),
        P(("mol", "tile")),
    )
    owners, subs = mesh.shape["pair"], mesh.shape["sub"]

    def local(*args):
        tile_rows, cols = args[0].shape[3:]
        rows = tile_rows // owners
        power = owners & (owners - 1) == 0
        fits = rows % ROWS == 0 and cols % LANES == 0 and args[1].shape[0] == 1
        if power and fits and subs == 2 and args[0].shape[2] % ROWS == 0:
            return local_chunked(*args)
        return local_general(*args)

    return jax.shard_map(
        local,
        mesh=mesh,
        in_specs=placed,
        out_specs=P("mol", "sub", None, "pair", "tile"),
        check_vma=False,
    )
```

```python
import functools
import math

import jax
import jax.numpy as jnp
from jax import lax
from jax.experimental import pallas as pl
from jax.experimental.pallas import tpu as pltpu
from jax.sharding import PartitionSpec as P

ROWS = 16
LANES = 128
VMEM_BYTES = 24 * 2**20


def column_tables(coupling, col_pairs):
    left_table = jnp.take(coupling.T, col_pairs[:, 0], axis=0).T
    right_table = jnp.take(coupling.T, col_pairs[:, 1], axis=0).T
    return (left_table, right_table)


def cycle_rows(left_table, right_table, row_pairs):
    left_part = jnp.take(left_table, row_pairs[:, 0], axis=0)
    right_part = jnp.take(right_table, row_pairs[:, 1], axis=0)
    return (left_part * right_part).astype(jnp.bfloat16)


def cycle_all(coupling, pair_list, col_pairs, flat_rhs):
    total_pairs = pair_list.shape[0]
    step_rows = math.gcd(total_pairs, 512)
    row_blocks = pair_list.reshape(total_pairs // step_rows, step_rows, 2)
    left_table, right_table = column_tables(coupling, col_pairs)

    def one_block(row_pairs):
        weights = cycle_rows(left_table, right_table, row_pairs)
        return jnp.dot(weights, flat_rhs, preferred_element_type=jnp.float32)

    return lax.map(one_block, row_blocks).reshape(total_pairs, -1)


def local_general(
    lambda_amps,
    integral_tiles,
    tile_of,
    tile_mask,
    pair_list,
    coupling,
    pair_gap,
    row_energy,
    col_energy,
):
    pair_count = lambda_amps.shape[2]
    tile_rows = lambda_amps.shape[3]
    col_count = lambda_amps.shape[4]
    owners = lax.axis_size("pair")
    sub_count = lax.axis_size("sub")
    wanted = tile_of.reshape(pair_count)
    empty_tiles = jnp.zeros((pair_count, tile_rows, tile_rows), integral_tiles.dtype)
    shard_piece = lax.all_gather(integral_tiles, "pair", axis=0, tiled=True)
    inside = (wanted >= 0) & (wanted < shard_piece.shape[0])
    taken_rows = shard_piece[jnp.clip(wanted, 0, shard_piece.shape[0] - 1)]
    chosen = jnp.where(inside[:, None, None], taken_rows, empty_tiles)
    amplitudes = lambda_amps.reshape(pair_count, tile_rows, col_count)
    ladder = jnp.einsum("pac,pcb->pab", chosen, amplitudes, preferred_element_type=jnp.float32)
    blocks = tile_mask.shape[3]
    keep_mask = tile_mask.reshape(pair_count, 1, blocks, 1).astype(jnp.float32)
    ladder = (
        ladder.reshape(pair_count, tile_rows, blocks, col_count // blocks) * keep_mask
    ).reshape(pair_count, tile_rows, col_count)
    dressed = (amplitudes.astype(jnp.float32) + ladder).astype(jnp.bfloat16)
    dressed = dressed.reshape(1, 1, pair_count, tile_rows, col_count)
    relayed = lax.all_to_all(dressed, "pair", split_axis=3, concat_axis=0, tiled=True)
    sub_index = lax.axis_index("sub")
    block_ids = jnp.arange(owners, dtype=jnp.int32) * sub_count + sub_index
    mine_ids = (
        block_ids[:, None] * pair_count + jnp.arange(pair_count, dtype=jnp.int32)[None, :]
    ).reshape(-1)
    col_pairs = pair_list[mine_ids]
    flat_rhs = relayed.reshape(owners * pair_count, -1)
    partial_value = cycle_all(coupling, pair_list, col_pairs, flat_rhs)
    partial_value = partial_value.reshape(
        owners, sub_count, pair_count, relayed.shape[3], col_count
    )
    cycle_term = lax.psum_scatter(
        partial_value.astype(jnp.bfloat16), "sub", scatter_dimension=1, tiled=True
    ).astype(jnp.float32)
    total_sum = relayed.astype(jnp.float32) + cycle_term
    energy_gap = (
        pair_gap[:, :, :, None, None]
        + row_energy[None, None, None, :, None]
        + col_energy[None, None, None, None, :]
    )
    return (-total_sum / energy_gap).astype(jnp.bfloat16)


def in_hbm(value):
    return pltpu.with_memory_space_constraint(value, pltpu.HBM)


def one_hot(hits):
    return jnp.where(hits, 1.0, 0.0).astype(jnp.bfloat16)


def square_iotas(size):
    return (lax.broadcasted_iota(jnp.int32, (size, size), axis) for axis in range(2))


def swap_matrix():
    to, frm = square_iotas(ROWS * ROWS)
    return one_hot(to == (frm % ROWS) * ROWS + frm // ROWS)


def split3(value):
    high = value.astype(jnp.bfloat16)
    rest = value - high.astype(jnp.float32)
    mid = rest.astype(jnp.bfloat16)
    low = (rest - mid.astype(jnp.float32)).astype(jnp.bfloat16)
    return high, mid, low


def pick_columns(value, columns):
    high, mid, low = (
        jnp.dot(part, columns, preferred_element_type=jnp.float32) for part in split3(value)
    )
    return high + (mid + low)


def pick_rows(columns, value):
    dims = (((0,), (0,)), ((), ()))
    high, mid, low = (
        lax.dot_general(columns, part, dims, preferred_element_type=jnp.float32)
        for part in split3(value)
    )
    return high + (mid + low)


def weights_kernel(pair_ref, coupling_ref, gap_ref, place_ref, w_ref, gaps_ref, full):
    total = pair_ref.shape[1]
    depth = coupling_ref.shape[0]
    owners, _, pairs = gap_ref.shape
    me, sub = place_ref[0], place_ref[1]
    orbital = lax.broadcasted_iota(jnp.int32, (depth, total), 0)
    coupling = coupling_ref[...]
    product = None
    for side in range(2):
        columns = one_hot(orbital == pair_ref[side : side + 1, :])
        picked = pick_rows(columns, pick_columns(coupling, columns))
        product = picked if product is None else product * picked
    frm, to = square_iotas(total)
    block, within = to // pairs, to % pairs
    source = ((me ^ (block % owners)) * 2 + (sub ^ (block // owners))) * pairs + within
    full[...] = jnp.dot(
        product.astype(jnp.bfloat16), one_hot(frm == source), preferred_element_type=jnp.float32
    )
    row, column = square_iotas(pairs)
    for k in range(owners):
        start = pl.multiple_of(((me ^ k) * 2 + sub) * pairs, pairs)
        rows = pl.ds(k * pairs, pairs)
        w_ref[rows, :] = full[pl.ds(start, pairs), :].astype(jnp.bfloat16)
        gap = jnp.sum(jnp.where(row == column, gap_ref[me ^ k], 0.0), axis=1, keepdims=True)
        gaps_ref[rows, :] = jnp.broadcast_to(gap, (pairs, LANES))


def make_weights(pair_list, coupling, pair_gap, place):
    owners, _, pairs = pair_gap.shape
    total = pair_list.shape[0]
    mine = owners * pairs
    vmem = pl.BlockSpec(memory_space=pltpu.VMEM)
    return pl.pallas_call(
        weights_kernel,
        in_specs=[vmem, vmem, vmem, pl.BlockSpec(memory_space=pltpu.SMEM)],
        out_specs=[vmem, vmem],
        out_shape=[
            jax.ShapeDtypeStruct((mine, total), jnp.bfloat16),
            jax.ShapeDtypeStruct((mine, LANES), jnp.float32),
        ],
        scratch_shapes=[pltpu.VMEM((total, total), jnp.float32)],
        compiler_params=pltpu.CompilerParams(vmem_limit_bytes=VMEM_BYTES),
        cost_estimate=pl.CostEstimate(
            flops=12 * total * coupling.size, bytes_accessed=4 * coupling.size, transcendentals=0
        ),
    )(pair_list.T, coupling, pair_gap, place)


def dress_kernel(owners, rows, groups, place_ref, tile_of_ref, mask_ref, *refs):
    tile_refs, lam_ref = refs[:owners], refs[owners]
    out_refs = refs[owners + 1 : -4]
    tiles, stage, amps_ref, sems = refs[-4:]
    brought = lam_ref.shape[2] // sems.shape[0]
    copies = []
    for n in range(sems.shape[0]):
        block = pl.ds(n * brought, brought)
        copy = pltpu.make_async_copy(lam_ref.at[0, 0, block], amps_ref.at[block], sems.at[n])
        copy.start()
        copies.append(copy)
    me = place_ref[0]
    flat = [(k, c, out, j) for out, group in zip(out_refs, groups) for j, (k, c) in enumerate(group)]
    starts = [pl.multiple_of((me ^ k) * rows + c * ROWS, ROWS) for k, c, _, _ in flat]
    for k in range(owners):
        for n, start in enumerate(starts):
            tiles[k, pl.ds(n * ROWS, ROWS), :] = tile_refs[k][0, pl.ds(start, ROWS), :]
    swap = swap_matrix()
    parts = mask_ref.shape[2]
    for g in range(lam_ref.shape[2] // ROWS):
        for i in range(ROWS):
            pair = g * ROWS + i
            if pair % brought == 0:
                copies[pair // brought].wait()
            ladder = jnp.dot(
                tiles[tile_of_ref[0, 0, pair] ^ me],
                amps_ref[pair],
                preferred_element_type=jnp.float32,
            )
            width = ladder.shape[1] // parts
            for part in range(parts):
                keep = mask_ref[0, 0, part, pair].astype(jnp.float32)
                cols = slice(part * width, (part + 1) * width)
                for n, start in enumerate(starts):
                    amps = amps_ref[pair, pl.ds(start, ROWS), cols].astype(jnp.float32)
                    kept = keep * ladder[n * ROWS : (n + 1) * ROWS, cols]
                    stage[g, n, pl.ds(i * ROWS, ROWS), cols] = (amps + kept).astype(jnp.bfloat16)
        for n, (_, _, out, j) in enumerate(flat):
            turned = jnp.dot(swap, stage[g, n], preferred_element_type=jnp.float32)
            out[j, :, pl.ds(g * ROWS, ROWS), :] = turned.astype(jnp.bfloat16).reshape(
                ROWS, ROWS, turned.shape[1]
            )


def dress(groups, place, tile_of, tile_mask, tiles, lambda_amps):
    owners = len(tiles)
    pairs, tile_rows, cols = lambda_amps.shape[2:]
    rows = tile_rows // owners
    smem = pl.BlockSpec(memory_space=pltpu.SMEM)
    vmem = pl.BlockSpec(memory_space=pltpu.VMEM)
    count = sum(len(group) for group in groups)
    return pl.pallas_call(
        functools.partial(dress_kernel, owners, rows, groups),
        in_specs=[smem] * 3 + [vmem] * owners + [pl.BlockSpec(memory_space=pl.ANY)],
        out_specs=[vmem] * len(groups),
        out_shape=[
            jax.ShapeDtypeStruct((len(group), ROWS, pairs, cols), jnp.bfloat16)
            for group in groups
        ],
        scratch_shapes=[
            pltpu.VMEM((owners, count * ROWS, tile_rows), jnp.bfloat16),
            pltpu.VMEM((pairs // ROWS, count, ROWS * ROWS, cols), jnp.bfloat16),
            pltpu.VMEM((pairs, tile_rows, cols), jnp.bfloat16),
            pltpu.SemaphoreType.DMA((pairs // 4,)),
        ],
        compiler_params=pltpu.CompilerParams(vmem_limit_bytes=VMEM_BYTES),
        cost_estimate=pl.CostEstimate(
            flops=2 * pairs * count * ROWS * tile_rows * cols,
            bytes_accessed=3 * pairs * tile_rows * cols,
            transcendentals=0,
        ),
    )(
        place,
        in_hbm(tile_of),
        in_hbm(jnp.swapaxes(tile_mask, 2, 3)),
        in_hbm(tiles[0]),
        *tiles[1:],
        in_hbm(lambda_amps),
    )


def finish_kernel(indices, chunk, place_ref, row_ref, w_ref, gap_ref, col_ref, *refs):
    pieces = len(indices)
    piece_refs = refs[:pieces]
    out_ref, xs, ys, done, in_sems, out_sems = refs[-6:]
    _, rows, pairs, cols = piece_refs[0].shape
    owners = pieces // 2
    halves = pairs // ROWS
    mine = owners * pairs
    me = place_ref[0]
    steps = in_sems.shape[0]
    some = rows // steps
    arriving = []
    for n in range(steps):
        block = pl.ds(n * some, some)
        for j, index in enumerate(indices):
            copy = pltpu.make_async_copy(
                piece_refs[j].at[index, block],
                xs.at[block, pl.ds(j * pairs, pairs), :],
                in_sems.at[n, j],
            )
            copy.start()
            arriving.append(copy)
    weights = w_ref[...]
    col = col_ref[...]
    for a in range(rows):
        if a % some == 0:
            for copy in arriving[a // some * pieces : (a // some + 1) * pieces]:
                copy.wait()
        amps = xs[a]
        cycle = jnp.dot(weights, amps, preferred_element_type=jnp.float32)
        level = gap_ref[...] + row_ref[chunk * rows + a]
        energy = jnp.concatenate([level] * (cols // LANES), axis=1) + col
        rough = pl.reciprocal(energy, approx=True)
        inverse = rough * (energy * rough - 2.0)
        value = ((amps[:mine].astype(jnp.float32) + cycle) * inverse).astype(jnp.bfloat16)
        for g in range(owners * halves):
            ys[g, pl.ds(a * ROWS, ROWS), :] = value[g * ROWS : (g + 1) * ROWS]
    swap = swap_matrix()
    leaving = []
    for g in range(owners * halves):
        turned = jnp.dot(swap, ys[g], preferred_element_type=jnp.float32)
        done[g] = turned.astype(jnp.bfloat16).reshape(ROWS, rows, cols)
        k, h = g // halves, g % halves
        copy = pltpu.make_async_copy(
            done.at[g],
            out_ref.at[me ^ k, 0, pl.ds(h * ROWS, ROWS), pl.ds(chunk * rows, rows), :],
            out_sems.at[g],
        )
        copy.start()
        leaving.append(copy)
    for copy in leaving:
        copy.wait()


def finish(chunk, place, row_energy, weights, gaps, col_energy, pieces, before, shape):
    _, rows, pairs, cols = pieces[0][0].shape
    owners = len(pieces) // 2
    groups = owners * (pairs // ROWS)
    smem = pl.BlockSpec(memory_space=pltpu.SMEM)
    vmem = pl.BlockSpec(memory_space=pltpu.VMEM)
    anywhere = pl.BlockSpec(memory_space=pl.ANY)
    args = [place, row_energy, weights, gaps, col_energy] + [piece for piece, _ in pieces]
    in_specs = [smem, smem, vmem, vmem, vmem] + [anywhere] * len(pieces)
    aliases = {}
    if before is not None:
        aliases = {len(args): 0}
        args.append(before)
        in_specs.append(anywhere)
    return pl.pallas_call(
        functools.partial(finish_kernel, [index for _, index in pieces], chunk),
        in_specs=in_specs,
        out_specs=anywhere,
        out_shape=jax.ShapeDtypeStruct(shape, jnp.bfloat16),
        scratch_shapes=[
            pltpu.VMEM((rows, len(pieces) * pairs, cols), jnp.bfloat16),
            pltpu.VMEM((groups, ROWS * rows, cols), jnp.bfloat16),
            pltpu.VMEM((groups, ROWS, rows, cols), jnp.bfloat16),
            pltpu.SemaphoreType.DMA((4, len(pieces))),
            pltpu.SemaphoreType.DMA((groups,)),
        ],
        input_output_aliases=aliases,
        compiler_params=pltpu.CompilerParams(vmem_limit_bytes=VMEM_BYTES),
        cost_estimate=pl.CostEstimate(flops=0, bytes_accessed=0, transcendentals=0),
    )(*args)


def local_chunked(
    lambda_amps,
    integral_tiles,
    tile_of,
    tile_mask,
    pair_list,
    coupling,
    pair_gap,
    row_energy,
    col_energy,
):
    pairs, tile_rows, cols = lambda_amps.shape[2:]
    owners = lax.axis_size("pair")
    rows = tile_rows // owners
    chunks = rows // ROWS
    me = lax.axis_index("pair").astype(jnp.int32)
    sub = lax.axis_index("sub").astype(jnp.int32)
    place = jnp.stack([me, sub])

    def to_owner(value, k):
        return lax.ppermute(value, "pair", [(o, o ^ k) for o in range(owners)])

    def to_sibling(value):
        return lax.ppermute(value, "sub", [(0, 1), (1, 0)])

    def after(value, earlier):
        return value if earlier is None else lax.optimization_barrier((value, earlier))[0]

    tiles = [integral_tiles] + [to_owner(integral_tiles, k) for k in range(1, owners)]

    far = list(range(owners - 1, 1, -1))
    groups = [((k, c),) for c in range(chunks) for k in far]
    groups += [tuple((k, c) for c in range(chunks)) for k in (1, 0)]
    sent = dress(groups, place, tile_of, tile_mask, tiles, lambda_amps)
    direct = {}
    for group, value in zip(groups, sent):
        k = group[0][0]
        landed = to_owner(value, k) if k else value
        for index, key in enumerate(group):
            direct[key] = (landed, index)
    weights, gaps = make_weights(after(pair_list, sent[0]), coupling, pair_gap, place)

    shape = (owners, 1, pairs, rows, cols)
    col = col_energy.reshape(1, cols)
    result, other = None, {}
    for c in range(chunks):
        for k in far:
            value, index = direct[k, c]
            other[k, c] = (to_sibling(value), index)
        if c == 0:
            for k in (0, 1):
                value, _ = direct[k, 0]
                value = after(value, weights if k else direct[far[0], 0][0])
                passed = to_sibling(value)
                for index in range(chunks):
                    other[k, index] = (passed, index)
        pieces = [held_by[k, c] for held_by in (direct, other) for k in range(owners)]
        result = finish(c, place, row_energy, weights, gaps, col, pieces, result, shape)
    return result


def solution(mesh):
    placed = (
        P(("mol", "pair"), "sub", None, None, "tile"),
        P(("mol", "pair"), None, None),
        P(("mol", "pair"), "sub", None),
        P(("mol", "pair"), "sub", None, "tile"),
        P("mol", None),
        P("mol", None),
        P("mol", "sub", None),
        P(("mol", "pair")),
        P(("mol", "tile")),
    )
    owners, subs = mesh.shape["pair"], mesh.shape["sub"]

    def local(*args):
        tile_rows, cols = args[0].shape[3:]
        rows = tile_rows // owners
        power = owners & (owners - 1) == 0
        fits = rows % ROWS == 0 and cols % LANES == 0 and args[1].shape[0] == 1
        if power and fits and subs == 2 and args[0].shape[2] % ROWS == 0:
            return local_chunked(*args)
        return local_general(*args)

    return jax.shard_map(
        local,
        mesh=mesh,
        in_specs=placed,
        out_specs=P("mol", "sub", None, "pair", "tile"),
        check_vma=False,
    )
```

```python
import functools
import math

import jax
import jax.numpy as jnp
from jax import lax
from jax.experimental import pallas as pl
from jax.experimental.pallas import tpu as pltpu
from jax.sharding import PartitionSpec as P

ROWS = 16
LANES = 128
VMEM_BYTES = 24 * 2**20


def column_tables(coupling, col_pairs):
    left_table = jnp.take(coupling.T, col_pairs[:, 0], axis=0).T
    right_table = jnp.take(coupling.T, col_pairs[:, 1], axis=0).T
    return (left_table, right_table)


def cycle_rows(left_table, right_table, row_pairs):
    left_part = jnp.take(left_table, row_pairs[:, 0], axis=0)
    right_part = jnp.take(right_table, row_pairs[:, 1], axis=0)
    return (left_part * right_part).astype(jnp.bfloat16)


def cycle_all(coupling, pair_list, col_pairs, flat_rhs):
    total_pairs = pair_list.shape[0]
    step_rows = math.gcd(total_pairs, 512)
    row_blocks = pair_list.reshape(total_pairs // step_rows, step_rows, 2)
    left_table, right_table = column_tables(coupling, col_pairs)

    def one_block(row_pairs):
        weights = cycle_rows(left_table, right_table, row_pairs)
        return jnp.dot(weights, flat_rhs, preferred_element_type=jnp.float32)

    return lax.map(one_block, row_blocks).reshape(total_pairs, -1)


def local_general(
    lambda_amps,
    integral_tiles,
    tile_of,
    tile_mask,
    pair_list,
    coupling,
    pair_gap,
    row_energy,
    col_energy,
):
    pair_count = lambda_amps.shape[2]
    tile_rows = lambda_amps.shape[3]
    col_count = lambda_amps.shape[4]
    owners = lax.axis_size("pair")
    sub_count = lax.axis_size("sub")
    wanted = tile_of.reshape(pair_count)
    empty_tiles = jnp.zeros((pair_count, tile_rows, tile_rows), integral_tiles.dtype)
    shard_piece = lax.all_gather(integral_tiles, "pair", axis=0, tiled=True)
    inside = (wanted >= 0) & (wanted < shard_piece.shape[0])
    taken_rows = shard_piece[jnp.clip(wanted, 0, shard_piece.shape[0] - 1)]
    chosen = jnp.where(inside[:, None, None], taken_rows, empty_tiles)
    amplitudes = lambda_amps.reshape(pair_count, tile_rows, col_count)
    ladder = jnp.einsum("pac,pcb->pab", chosen, amplitudes, preferred_element_type=jnp.float32)
    blocks = tile_mask.shape[3]
    keep_mask = tile_mask.reshape(pair_count, 1, blocks, 1).astype(jnp.float32)
    ladder = (
        ladder.reshape(pair_count, tile_rows, blocks, col_count // blocks) * keep_mask
    ).reshape(pair_count, tile_rows, col_count)
    dressed = (amplitudes.astype(jnp.float32) + ladder).astype(jnp.bfloat16)
    dressed = dressed.reshape(1, 1, pair_count, tile_rows, col_count)
    relayed = lax.all_to_all(dressed, "pair", split_axis=3, concat_axis=0, tiled=True)
    sub_index = lax.axis_index("sub")
    block_ids = jnp.arange(owners, dtype=jnp.int32) * sub_count + sub_index
    mine_ids = (
        block_ids[:, None] * pair_count + jnp.arange(pair_count, dtype=jnp.int32)[None, :]
    ).reshape(-1)
    col_pairs = pair_list[mine_ids]
    flat_rhs = relayed.reshape(owners * pair_count, -1)
    partial_value = cycle_all(coupling, pair_list, col_pairs, flat_rhs)
    partial_value = partial_value.reshape(
        owners, sub_count, pair_count, relayed.shape[3], col_count
    )
    cycle_term = lax.psum_scatter(
        partial_value.astype(jnp.bfloat16), "sub", scatter_dimension=1, tiled=True
    ).astype(jnp.float32)
    total_sum = relayed.astype(jnp.float32) + cycle_term
    energy_gap = (
        pair_gap[:, :, :, None, None]
        + row_energy[None, None, None, :, None]
        + col_energy[None, None, None, None, :]
    )
    return (-total_sum / energy_gap).astype(jnp.bfloat16)


def in_hbm(value):
    return pltpu.with_memory_space_constraint(value, pltpu.HBM)


def one_hot(hits):
    return jnp.where(hits, 1.0, 0.0).astype(jnp.bfloat16)


def square_iotas(size):
    return (lax.broadcasted_iota(jnp.int32, (size, size), axis) for axis in range(2))


def split3(value):
    high = value.astype(jnp.bfloat16)
    rest = value - high.astype(jnp.float32)
    mid = rest.astype(jnp.bfloat16)
    low = (rest - mid.astype(jnp.float32)).astype(jnp.bfloat16)
    return high, mid, low


def pick_columns(value, columns):
    high, mid, low = (
        jnp.dot(part, columns, preferred_element_type=jnp.float32) for part in split3(value)
    )
    return high + (mid + low)


def pick_rows(columns, value):
    dims = (((0,), (0,)), ((), ()))
    high, mid, low = (
        lax.dot_general(columns, part, dims, preferred_element_type=jnp.float32)
        for part in split3(value)
    )
    return high + (mid + low)


def hold_kernel(lam_ref, held_ref, swap_ref, sems):
    step = lam_ref.shape[2] // sems.shape[0]
    copies = []
    for i in range(sems.shape[0]):
        block = pl.ds(i * step, step)
        copy = pltpu.make_async_copy(
            lam_ref.at[:, :, block], held_ref.at[:, :, block], sems.at[i]
        )
        copy.start()
        copies.append(copy)
    to, frm = square_iotas(ROWS * ROWS)
    swap_ref[...] = one_hot(to == (frm % ROWS) * ROWS + frm // ROWS)
    for copy in copies:
        copy.wait()


def hold(lambda_amps):
    anywhere = pl.BlockSpec(memory_space=pl.ANY)
    return pl.pallas_call(
        hold_kernel,
        in_specs=[anywhere],
        out_specs=[anywhere, pl.BlockSpec(memory_space=pltpu.VMEM)],
        out_shape=[
            jax.ShapeDtypeStruct(lambda_amps.shape, lambda_amps.dtype),
            jax.ShapeDtypeStruct((ROWS * ROWS, ROWS * ROWS), jnp.bfloat16),
        ],
        scratch_shapes=[pltpu.SemaphoreType.DMA((8,))],
        compiler_params=pltpu.CompilerParams(vmem_limit_bytes=VMEM_BYTES),
        cost_estimate=pl.CostEstimate(
            flops=0, bytes_accessed=4 * lambda_amps.size, transcendentals=0
        ),
    )(in_hbm(lambda_amps))


def weights_kernel(
    pair_ref, coupling_ref, gap_ref, place_ref, row_ref, col_ref, w_ref, inverse_ref, full
):
    total = pair_ref.shape[1]
    depth = coupling_ref.shape[0]
    owners, _, pairs = gap_ref.shape
    me, sub = place_ref[0], place_ref[1]
    orbital = lax.broadcasted_iota(jnp.int32, (depth, total), 0)
    coupling = coupling_ref[...]
    product = None
    for side in range(2):
        columns = one_hot(orbital == pair_ref[side : side + 1, :])
        picked = pick_rows(columns, pick_columns(coupling, columns))
        product = picked if product is None else product * picked
    frm, to = square_iotas(total)
    block, within = to // pairs, to % pairs
    source = ((me ^ (block % owners)) * 2 + (sub ^ (block // owners))) * pairs + within
    full[...] = jnp.dot(
        product.astype(jnp.bfloat16), one_hot(frm == source), preferred_element_type=jnp.float32
    )
    row, column = square_iotas(pairs)
    for k in range(owners):
        start = pl.multiple_of(((me ^ k) * 2 + sub) * pairs, pairs)
        rows = pl.ds(k * pairs, pairs)
        w_ref[rows, :] = full[pl.ds(start, pairs), :].astype(jnp.bfloat16)
        gap = jnp.sum(jnp.where(row == column, gap_ref[me ^ k], 0.0), axis=1, keepdims=True)
        for a in range(inverse_ref.shape[0]):
            inverse_ref[a, rows, :] = -1.0 / ((gap + row_ref[a]) + col_ref[...])


def make_weights(pair_list, coupling, pair_gap, place, row_energy, col_energy):
    owners, _, pairs = pair_gap.shape
    total = pair_list.shape[0]
    mine = owners * pairs
    rows, cols = row_energy.shape[0], col_energy.shape[0]
    smem = pl.BlockSpec(memory_space=pltpu.SMEM)
    vmem = pl.BlockSpec(memory_space=pltpu.VMEM)
    return pl.pallas_call(
        weights_kernel,
        in_specs=[vmem, vmem, vmem, smem, smem, vmem],
        out_specs=[vmem, vmem],
        out_shape=[
            jax.ShapeDtypeStruct((mine, total), jnp.bfloat16),
            jax.ShapeDtypeStruct((rows, mine, cols), jnp.float32),
        ],
        scratch_shapes=[pltpu.VMEM((total, total), jnp.float32)],
        compiler_params=pltpu.CompilerParams(vmem_limit_bytes=VMEM_BYTES),
        cost_estimate=pl.CostEstimate(
            flops=12 * total * coupling.size, bytes_accessed=4 * coupling.size, transcendentals=0
        ),
    )(pair_list.T, coupling, pair_gap, place, row_energy, col_energy.reshape(1, cols))


def dress_kernel(owners, rows, groups, place_ref, tile_of_ref, mask_ref, *refs):
    tile_refs, lam_ref = (refs[0], refs[owners - 1], *refs[1 : owners - 1]), refs[owners]
    swap_ref = refs[owners + 1]
    out_refs = refs[owners + 2 : -2]
    tiles, stage = refs[-2:]
    me = place_ref[0]
    flat = [(k, c, out, j) for out, group in zip(out_refs, groups) for j, (k, c) in enumerate(group)]
    starts = [pl.multiple_of((me ^ k) * rows + c * ROWS, ROWS) for k, c, _, _ in flat]
    for k in range(owners):
        for n, start in enumerate(starts):
            tiles[k, pl.ds(n * ROWS, ROWS), :] = tile_refs[k][0, pl.ds(start, ROWS), :]
    swap = swap_ref[...]
    parts = mask_ref.shape[2]
    for g in range(lam_ref.shape[2] // ROWS):
        for i in range(ROWS):
            pair = g * ROWS + i
            ladder = jnp.dot(
                tiles[tile_of_ref[0, 0, pair] ^ me],
                lam_ref[0, 0, pair],
                preferred_element_type=jnp.float32,
            )
            width = ladder.shape[1] // parts
            for part in range(parts):
                keep = mask_ref[0, 0, part, pair].astype(jnp.float32)
                cols = slice(part * width, (part + 1) * width)
                for n, start in enumerate(starts):
                    amps = lam_ref[0, 0, pair, pl.ds(start, ROWS), cols].astype(jnp.float32)
                    kept = keep * ladder[n * ROWS : (n + 1) * ROWS, cols]
                    stage[g, n, pl.ds(i * ROWS, ROWS), cols] = (amps + kept).astype(jnp.bfloat16)
        for n, (_, _, out, j) in enumerate(flat):
            turned = jnp.dot(swap, stage[g, n], preferred_element_type=jnp.float32)
            out[j, :, pl.ds(g * ROWS, ROWS), :] = turned.astype(jnp.bfloat16).reshape(
                ROWS, ROWS, turned.shape[1]
            )


def dress(groups, place, tile_of, tile_mask, tiles, lambda_amps, swap):
    owners = len(tiles)
    pairs, tile_rows, cols = lambda_amps.shape[2:]
    rows = tile_rows // owners
    smem = pl.BlockSpec(memory_space=pltpu.SMEM)
    vmem = pl.BlockSpec(memory_space=pltpu.VMEM)
    count = sum(len(group) for group in groups)
    return pl.pallas_call(
        functools.partial(dress_kernel, owners, rows, groups),
        in_specs=[smem] * 3 + [vmem] * (owners + 2),
        out_specs=[vmem] * len(groups),
        out_shape=[
            jax.ShapeDtypeStruct((len(group), ROWS, pairs, cols), jnp.bfloat16)
            for group in groups
        ],
        scratch_shapes=[
            pltpu.VMEM((owners, count * ROWS, tile_rows), jnp.bfloat16),
            pltpu.VMEM((pairs // ROWS, count, ROWS * ROWS, cols), jnp.bfloat16),
        ],
        compiler_params=pltpu.CompilerParams(vmem_limit_bytes=VMEM_BYTES),
        cost_estimate=pl.CostEstimate(
            flops=2 * pairs * count * ROWS * tile_rows * cols,
            bytes_accessed=3 * pairs * tile_rows * cols,
            transcendentals=0,
        ),
    )(
        place,
        in_hbm(tile_of),
        in_hbm(jnp.swapaxes(tile_mask, 2, 3)),
        in_hbm(tiles[0]),
        *tiles[2:],
        tiles[1],
        lambda_amps,
        swap,
    )


def finish_kernel(pieces, chunk, place_ref, swap_ref, w_ref, inverse_ref, *refs):
    piece_refs = refs[:pieces]
    out_ref, ys, done, sems = refs[-4:]
    _, rows, pairs, cols = piece_refs[0].shape
    owners = pieces // 2
    halves = pairs // ROWS
    mine = owners * pairs
    me = place_ref[0]
    weights = w_ref[...]
    for a in range(rows):
        amps = jnp.concatenate([piece_refs[j][0, a] for j in range(pieces)], axis=0)
        cycle = jnp.dot(weights, amps, preferred_element_type=jnp.float32)
        total = amps[:mine].astype(jnp.float32) + cycle
        value = (total * inverse_ref[chunk * rows + a]).astype(jnp.bfloat16)
        for g in range(owners * halves):
            ys[g, pl.ds(a * ROWS, ROWS), :] = value[g * ROWS : (g + 1) * ROWS]
    swap = swap_ref[...]
    leaving = []
    for g in range(owners * halves):
        turned = jnp.dot(swap, ys[g], preferred_element_type=jnp.float32)
        done[g] = turned.astype(jnp.bfloat16).reshape(ROWS, rows, cols)
        k, h = g // halves, g % halves
        copy = pltpu.make_async_copy(
            done.at[g],
            out_ref.at[me ^ k, 0, pl.ds(h * ROWS, ROWS), pl.ds(chunk * rows, rows), :],
            sems.at[g],
        )
        copy.start()
        leaving.append(copy)
    for copy in leaving:
        copy.wait()


def finish(chunk, place, swap, weights, inverse, pieces, before, shape):
    _, rows, pairs, cols = pieces[0][0].shape
    owners = len(pieces) // 2
    groups = owners * (pairs // ROWS)
    anywhere = pl.BlockSpec(memory_space=pl.ANY)
    args = [place, swap, weights, inverse] + [piece for piece, _ in pieces]
    in_specs = [pl.BlockSpec(memory_space=pltpu.SMEM)]
    in_specs += [pl.BlockSpec(memory_space=pltpu.VMEM)] * 3
    for _, index in pieces:
        in_specs.append(
            pl.BlockSpec((1, rows, pairs, cols), lambda i, index=index: (index, 0, 0, 0))
        )
    aliases = {}
    if before is not None:
        aliases = {len(args): 0}
        args.append(before)
        in_specs.append(anywhere)
    return pl.pallas_call(
        functools.partial(finish_kernel, len(pieces), chunk),
        grid=(1,),
        in_specs=in_specs,
        out_specs=anywhere,
        out_shape=jax.ShapeDtypeStruct(shape, jnp.bfloat16),
        scratch_shapes=[
            pltpu.VMEM((groups, ROWS * rows, cols), jnp.bfloat16),
            pltpu.VMEM((groups, ROWS, rows, cols), jnp.bfloat16),
            pltpu.SemaphoreType.DMA((groups,)),
        ],
        input_output_aliases=aliases,
        compiler_params=pltpu.CompilerParams(vmem_limit_bytes=VMEM_BYTES),
        cost_estimate=pl.CostEstimate(flops=0, bytes_accessed=0, transcendentals=0),
    )(*args)


def local_chunked(
    lambda_amps,
    integral_tiles,
    tile_of,
    tile_mask,
    pair_list,
    coupling,
    pair_gap,
    row_energy,
    col_energy,
):
    pairs, tile_rows, cols = lambda_amps.shape[2:]
    owners = lax.axis_size("pair")
    rows = tile_rows // owners
    chunks = rows // ROWS
    me = lax.axis_index("pair").astype(jnp.int32)
    sub = lax.axis_index("sub").astype(jnp.int32)
    place = jnp.stack([me, sub])

    def to_owner(value, k):
        return lax.ppermute(value, "pair", [(o, o ^ k) for o in range(owners)])

    def to_sibling(value):
        return lax.ppermute(value, "sub", [(0, 1), (1, 0)])

    def after(value, earlier):
        return value if earlier is None else lax.optimization_barrier((value, earlier))[0]

    tiles = [integral_tiles] + [to_owner(integral_tiles, k) for k in range(1, owners)]

    far = list(range(owners - 1, 1, -1))
    groups = [((k, c),) for c in range(chunks) for k in far]
    groups += [tuple((k, c) for c in range(chunks)) for k in (1, 0)]
    held, swap = hold(lambda_amps)
    sent = dress(groups, place, tile_of, tile_mask, tiles, held, swap)
    weights, inverse = make_weights(
        after(pair_list, sent[0]), coupling, pair_gap, place, row_energy, col_energy
    )
    direct = {}
    for group, value in zip(groups, sent):
        k = group[0][0]
        landed = to_owner(value, k) if k else value
        for index, key in enumerate(group):
            direct[key] = (landed, index)

    shape = (owners, 1, pairs, rows, cols)
    result, other = None, {}
    for c in range(chunks):
        for k in far:
            value, index = direct[k, c]
            other[k, c] = (to_sibling(value), index)
        if c == 0:
            for k in (0, 1):
                value, _ = direct[k, 0]
                value = after(value, weights if k else direct[far[0], 0][0])
                passed = to_sibling(value)
                for index in range(chunks):
                    other[k, index] = (passed, index)
        pieces = [held_by[k, c] for held_by in (direct, other) for k in range(owners)]
        result = finish(c, place, swap, weights, inverse, pieces, result, shape)
    return result


def solution(mesh):
    placed = (
        P(("mol", "pair"), "sub", None, None, "tile"),
        P(("mol", "pair"), None, None),
        P(("mol", "pair"), "sub", None),
        P(("mol", "pair"), "sub", None, "tile"),
        P("mol", None),
        P("mol", None),
        P("mol", "sub", None),
        P(("mol", "pair")),
        P(("mol", "tile")),
    )
    owners, subs = mesh.shape["pair"], mesh.shape["sub"]

    def local(*args):
        tile_rows, cols = args[0].shape[3:]
        rows = tile_rows // owners
        power = owners & (owners - 1) == 0
        fits = rows % ROWS == 0 and cols % LANES == 0 and args[1].shape[0] == 1
        if power and fits and subs == 2 and args[0].shape[2] % ROWS == 0:
            return local_chunked(*args)
        return local_general(*args)

    return jax.shard_map(
        local,
        mesh=mesh,
        in_specs=placed,
        out_specs=P("mol", "sub", None, "pair", "tile"),
        check_vma=False,
    )
```

```python
import functools
import math

import jax
import jax.numpy as jnp
from jax import lax
from jax.experimental import pallas as pl
from jax.experimental.pallas import tpu as pltpu
from jax.sharding import PartitionSpec as P

ROWS = 16
LANES = 128
VMEM_BYTES = 24 * 2**20


def column_tables(coupling, col_pairs):
    left_table = jnp.take(coupling.T, col_pairs[:, 0], axis=0).T
    right_table = jnp.take(coupling.T, col_pairs[:, 1], axis=0).T
    return (left_table, right_table)


def cycle_rows(left_table, right_table, row_pairs):
    left_part = jnp.take(left_table, row_pairs[:, 0], axis=0)
    right_part = jnp.take(right_table, row_pairs[:, 1], axis=0)
    return (left_part * right_part).astype(jnp.bfloat16)


def cycle_all(coupling, pair_list, col_pairs, flat_rhs):
    total_pairs = pair_list.shape[0]
    step_rows = math.gcd(total_pairs, 512)
    row_blocks = pair_list.reshape(total_pairs // step_rows, step_rows, 2)
    left_table, right_table = column_tables(coupling, col_pairs)

    def one_block(row_pairs):
        weights = cycle_rows(left_table, right_table, row_pairs)
        return jnp.dot(weights, flat_rhs, preferred_element_type=jnp.float32)

    return lax.map(one_block, row_blocks).reshape(total_pairs, -1)


def local_general(
    lambda_amps,
    integral_tiles,
    tile_of,
    tile_mask,
    pair_list,
    coupling,
    pair_gap,
    row_energy,
    col_energy,
):
    pair_count = lambda_amps.shape[2]
    tile_rows = lambda_amps.shape[3]
    col_count = lambda_amps.shape[4]
    owners = lax.axis_size("pair")
    sub_count = lax.axis_size("sub")
    wanted = tile_of.reshape(pair_count)
    empty_tiles = jnp.zeros((pair_count, tile_rows, tile_rows), integral_tiles.dtype)
    shard_piece = lax.all_gather(integral_tiles, "pair", axis=0, tiled=True)
    inside = (wanted >= 0) & (wanted < shard_piece.shape[0])
    taken_rows = shard_piece[jnp.clip(wanted, 0, shard_piece.shape[0] - 1)]
    chosen = jnp.where(inside[:, None, None], taken_rows, empty_tiles)
    amplitudes = lambda_amps.reshape(pair_count, tile_rows, col_count)
    ladder = jnp.einsum("pac,pcb->pab", chosen, amplitudes, preferred_element_type=jnp.float32)
    blocks = tile_mask.shape[3]
    keep_mask = tile_mask.reshape(pair_count, 1, blocks, 1).astype(jnp.float32)
    ladder = (
        ladder.reshape(pair_count, tile_rows, blocks, col_count // blocks) * keep_mask
    ).reshape(pair_count, tile_rows, col_count)
    dressed = (amplitudes.astype(jnp.float32) + ladder).astype(jnp.bfloat16)
    dressed = dressed.reshape(1, 1, pair_count, tile_rows, col_count)
    relayed = lax.all_to_all(dressed, "pair", split_axis=3, concat_axis=0, tiled=True)
    sub_index = lax.axis_index("sub")
    block_ids = jnp.arange(owners, dtype=jnp.int32) * sub_count + sub_index
    mine_ids = (
        block_ids[:, None] * pair_count + jnp.arange(pair_count, dtype=jnp.int32)[None, :]
    ).reshape(-1)
    col_pairs = pair_list[mine_ids]
    flat_rhs = relayed.reshape(owners * pair_count, -1)
    partial_value = cycle_all(coupling, pair_list, col_pairs, flat_rhs)
    partial_value = partial_value.reshape(
        owners, sub_count, pair_count, relayed.shape[3], col_count
    )
    cycle_term = lax.psum_scatter(
        partial_value.astype(jnp.bfloat16), "sub", scatter_dimension=1, tiled=True
    ).astype(jnp.float32)
    total_sum = relayed.astype(jnp.float32) + cycle_term
    energy_gap = (
        pair_gap[:, :, :, None, None]
        + row_energy[None, None, None, :, None]
        + col_energy[None, None, None, None, :]
    )
    return (-total_sum / energy_gap).astype(jnp.bfloat16)


def in_hbm(value):
    return pltpu.with_memory_space_constraint(value, pltpu.HBM)


def one_hot(hits):
    return jnp.where(hits, 1.0, 0.0).astype(jnp.bfloat16)


def square_iotas(size):
    return (lax.broadcasted_iota(jnp.int32, (size, size), axis) for axis in range(2))


def split3(value):
    high = value.astype(jnp.bfloat16)
    rest = value - high.astype(jnp.float32)
    mid = rest.astype(jnp.bfloat16)
    low = (rest - mid.astype(jnp.float32)).astype(jnp.bfloat16)
    return high, mid, low


def pick_columns(value, columns):
    high, mid, low = (
        jnp.dot(part, columns, preferred_element_type=jnp.float32) for part in split3(value)
    )
    return high + (mid + low)


def pick_rows(columns, value):
    dims = (((0,), (0,)), ((), ()))
    high, mid, low = (
        lax.dot_general(columns, part, dims, preferred_element_type=jnp.float32)
        for part in split3(value)
    )
    return high + (mid + low)


def hold_kernel(lam_ref, held_ref, swap_ref, sems):
    step = lam_ref.shape[2] // sems.shape[0]
    copies = []
    for i in range(sems.shape[0]):
        block = pl.ds(i * step, step)
        copy = pltpu.make_async_copy(
            lam_ref.at[:, :, block], held_ref.at[:, :, block], sems.at[i]
        )
        copy.start()
        copies.append(copy)
    to, frm = square_iotas(ROWS * ROWS)
    swap_ref[...] = one_hot(to == (frm % ROWS) * ROWS + frm // ROWS)
    for copy in copies:
        copy.wait()


def hold(lambda_amps):
    anywhere = pl.BlockSpec(memory_space=pl.ANY)
    return pl.pallas_call(
        hold_kernel,
        in_specs=[anywhere],
        out_specs=[anywhere, pl.BlockSpec(memory_space=pltpu.VMEM)],
        out_shape=[
            jax.ShapeDtypeStruct(lambda_amps.shape, lambda_amps.dtype),
            jax.ShapeDtypeStruct((ROWS * ROWS, ROWS * ROWS), jnp.bfloat16),
        ],
        scratch_shapes=[pltpu.SemaphoreType.DMA((8,))],
        compiler_params=pltpu.CompilerParams(vmem_limit_bytes=VMEM_BYTES),
        cost_estimate=pl.CostEstimate(
            flops=0, bytes_accessed=4 * lambda_amps.size, transcendentals=0
        ),
    )(in_hbm(lambda_amps))


def weights_kernel(
    pair_ref, coupling_ref, gap_ref, place_ref, row_ref, col_ref, w_ref, inverse_ref, full
):
    total = pair_ref.shape[1]
    depth = coupling_ref.shape[0]
    owners, _, pairs = gap_ref.shape
    me, sub = place_ref[0], place_ref[1]
    orbital = lax.broadcasted_iota(jnp.int32, (depth, total), 0)
    coupling = coupling_ref[...]
    product = None
    for side in range(2):
        columns = one_hot(orbital == pair_ref[side : side + 1, :])
        picked = pick_rows(columns, pick_columns(coupling, columns))
        product = picked if product is None else product * picked
    frm, to = square_iotas(total)
    block, within = to // pairs, to % pairs
    source = ((me ^ (block % owners)) * 2 + (sub ^ (block // owners))) * pairs + within
    full[...] = jnp.dot(
        product.astype(jnp.bfloat16), one_hot(frm == source), preferred_element_type=jnp.float32
    )
    row, column = square_iotas(pairs)
    for k in range(owners):
        start = pl.multiple_of(((me ^ k) * 2 + sub) * pairs, pairs)
        rows = pl.ds(k * pairs, pairs)
        w_ref[rows, :] = full[pl.ds(start, pairs), :].astype(jnp.bfloat16)
        gap = jnp.sum(jnp.where(row == column, gap_ref[me ^ k], 0.0), axis=1, keepdims=True)
        for a in range(inverse_ref.shape[0]):
            inverse_ref[a, rows, :] = -1.0 / ((gap + row_ref[a]) + col_ref[...])


def make_weights(pair_list, coupling, pair_gap, place, row_energy, col_energy):
    owners, _, pairs = pair_gap.shape
    total = pair_list.shape[0]
    mine = owners * pairs
    rows, cols = row_energy.shape[0], col_energy.shape[0]
    smem = pl.BlockSpec(memory_space=pltpu.SMEM)
    vmem = pl.BlockSpec(memory_space=pltpu.VMEM)
    return pl.pallas_call(
        weights_kernel,
        in_specs=[vmem, vmem, vmem, smem, smem, vmem],
        out_specs=[vmem, vmem],
        out_shape=[
            jax.ShapeDtypeStruct((mine, total), jnp.bfloat16),
            jax.ShapeDtypeStruct((rows, mine, cols), jnp.float32),
        ],
        scratch_shapes=[pltpu.VMEM((total, total), jnp.float32)],
        compiler_params=pltpu.CompilerParams(vmem_limit_bytes=VMEM_BYTES),
        cost_estimate=pl.CostEstimate(
            flops=12 * total * coupling.size, bytes_accessed=4 * coupling.size, transcendentals=0
        ),
    )(pair_list.T, coupling, pair_gap, place, row_energy, col_energy.reshape(1, cols))


def dress_kernel(owners, rows, groups, place_ref, tile_of_ref, mask_ref, *refs):
    tile_refs, lam_ref = (refs[0], refs[owners - 1], *refs[1 : owners - 1]), refs[owners]
    swap_ref = refs[owners + 1]
    out_refs = refs[owners + 2 : -2]
    tiles, stage = refs[-2:]
    me = place_ref[0]
    flat = [(k, c, out, j) for out, group in zip(out_refs, groups) for j, (k, c) in enumerate(group)]
    starts = [pl.multiple_of((me ^ k) * rows + c * ROWS, ROWS) for k, c, _, _ in flat]
    for k in range(owners):
        for n, start in enumerate(starts):
            tiles[k, pl.ds(n * ROWS, ROWS), :] = tile_refs[k][0, pl.ds(start, ROWS), :]
    swap = swap_ref[...]
    parts = mask_ref.shape[2]
    for g in range(lam_ref.shape[2] // ROWS):
        for i in range(ROWS):
            pair = g * ROWS + i
            ladder = jnp.dot(
                tiles[tile_of_ref[0, 0, pair] ^ me],
                lam_ref[0, 0, pair],
                preferred_element_type=jnp.float32,
            )
            width = ladder.shape[1] // parts
            for part in range(parts):
                keep = mask_ref[0, 0, part, pair].astype(jnp.float32)
                cols = slice(part * width, (part + 1) * width)
                for n, start in enumerate(starts):
                    amps = lam_ref[0, 0, pair, pl.ds(start, ROWS), cols].astype(jnp.float32)
                    kept = keep * ladder[n * ROWS : (n + 1) * ROWS, cols]
                    stage[g, n, pl.ds(i * ROWS, ROWS), cols] = (amps + kept).astype(jnp.bfloat16)
        for n, (_, _, out, j) in enumerate(flat):
            turned = jnp.dot(swap, stage[g, n], preferred_element_type=jnp.float32)
            out[j, :, pl.ds(g * ROWS, ROWS), :] = turned.astype(jnp.bfloat16).reshape(
                ROWS, ROWS, turned.shape[1]
            )


def dress(groups, place, tile_of, tile_mask, tiles, lambda_amps, swap):
    owners = len(tiles)
    pairs, tile_rows, cols = lambda_amps.shape[2:]
    rows = tile_rows // owners
    smem = pl.BlockSpec(memory_space=pltpu.SMEM)
    vmem = pl.BlockSpec(memory_space=pltpu.VMEM)
    count = sum(len(group) for group in groups)
    return pl.pallas_call(
        functools.partial(dress_kernel, owners, rows, groups),
        in_specs=[smem] * 3 + [vmem] * (owners + 2),
        out_specs=[vmem] * len(groups),
        out_shape=[
            jax.ShapeDtypeStruct((len(group), ROWS, pairs, cols), jnp.bfloat16)
            for group in groups
        ],
        scratch_shapes=[
            pltpu.VMEM((owners, count * ROWS, tile_rows), jnp.bfloat16),
            pltpu.VMEM((pairs // ROWS, count, ROWS * ROWS, cols), jnp.bfloat16),
        ],
        compiler_params=pltpu.CompilerParams(vmem_limit_bytes=VMEM_BYTES),
        cost_estimate=pl.CostEstimate(
            flops=2 * pairs * count * ROWS * tile_rows * cols,
            bytes_accessed=3 * pairs * tile_rows * cols,
            transcendentals=0,
        ),
    )(
        place,
        in_hbm(tile_of),
        in_hbm(jnp.swapaxes(tile_mask, 2, 3)),
        in_hbm(tiles[0]),
        *tiles[2:],
        tiles[1],
        lambda_amps,
        swap,
    )


def finish_kernel(indices, chunk, place_ref, swap_ref, w_ref, inverse_ref, *refs):
    pieces = len(indices)
    piece_refs = refs[:pieces]
    out_ref, ys, done, sems = refs[-4:]
    _, rows, pairs, cols = piece_refs[0].shape
    owners = pieces // 2
    halves = pairs // ROWS
    mine = owners * pairs
    me = place_ref[0]
    weights = w_ref[...]
    for a in range(rows):
        amps = jnp.concatenate([ref[index, a] for ref, index in zip(piece_refs, indices)], axis=0)
        cycle = jnp.dot(weights, amps, preferred_element_type=jnp.float32)
        total = amps[:mine].astype(jnp.float32) + cycle
        value = (total * inverse_ref[chunk * rows + a]).astype(jnp.bfloat16)
        for g in range(owners * halves):
            ys[g, pl.ds(a * ROWS, ROWS), :] = value[g * ROWS : (g + 1) * ROWS]
    swap = swap_ref[...]
    leaving = []
    for g in range(owners * halves):
        turned = jnp.dot(swap, ys[g], preferred_element_type=jnp.float32)
        done[g] = turned.astype(jnp.bfloat16).reshape(ROWS, rows, cols)
        k, h = g // halves, g % halves
        copy = pltpu.make_async_copy(
            done.at[g],
            out_ref.at[me ^ k, 0, pl.ds(h * ROWS, ROWS), pl.ds(chunk * rows, rows), :],
            sems.at[g],
        )
        copy.start()
        leaving.append(copy)
    for copy in leaving:
        copy.wait()


def finish(chunk, place, swap, weights, inverse, pieces, before, shape):
    _, rows, pairs, cols = pieces[0][0].shape
    owners = len(pieces) // 2
    groups = owners * (pairs // ROWS)
    anywhere = pl.BlockSpec(memory_space=pl.ANY)
    args = [place, swap, weights, inverse] + [piece for piece, _ in pieces]
    in_specs = [pl.BlockSpec(memory_space=pltpu.SMEM)]
    in_specs += [pl.BlockSpec(memory_space=pltpu.VMEM)] * (3 + len(pieces))
    aliases = {}
    if before is not None:
        aliases = {len(args): 0}
        args.append(before)
        in_specs.append(anywhere)
    return pl.pallas_call(
        functools.partial(finish_kernel, [index for _, index in pieces], chunk),
        in_specs=in_specs,
        out_specs=anywhere,
        out_shape=jax.ShapeDtypeStruct(shape, jnp.bfloat16),
        scratch_shapes=[
            pltpu.VMEM((groups, ROWS * rows, cols), jnp.bfloat16),
            pltpu.VMEM((groups, ROWS, rows, cols), jnp.bfloat16),
            pltpu.SemaphoreType.DMA((groups,)),
        ],
        input_output_aliases=aliases,
        compiler_params=pltpu.CompilerParams(vmem_limit_bytes=VMEM_BYTES),
        cost_estimate=pl.CostEstimate(flops=0, bytes_accessed=0, transcendentals=0),
    )(*args)


def local_chunked(
    lambda_amps,
    integral_tiles,
    tile_of,
    tile_mask,
    pair_list,
    coupling,
    pair_gap,
    row_energy,
    col_energy,
):
    pairs, tile_rows, cols = lambda_amps.shape[2:]
    owners = lax.axis_size("pair")
    rows = tile_rows // owners
    chunks = rows // ROWS
    me = lax.axis_index("pair").astype(jnp.int32)
    sub = lax.axis_index("sub").astype(jnp.int32)
    place = jnp.stack([me, sub])

    def to_owner(value, k):
        return lax.ppermute(value, "pair", [(o, o ^ k) for o in range(owners)])

    def to_sibling(value):
        return lax.ppermute(value, "sub", [(0, 1), (1, 0)])

    def after(value, earlier):
        return value if earlier is None else lax.optimization_barrier((value, earlier))[0]

    tiles = [integral_tiles] + [to_owner(integral_tiles, k) for k in range(1, owners)]

    far = list(range(owners - 1, 1, -1))
    groups = [((k, c),) for c in range(chunks) for k in far]
    groups += [tuple((k, c) for c in range(chunks)) for k in (1, 0)]
    held, swap = hold(lambda_amps)
    sent = dress(groups, place, tile_of, tile_mask, tiles, held, swap)
    own = to_sibling(sent[-1])
    weights, inverse = make_weights(
        after(pair_list, sent[0]), coupling, pair_gap, place, row_energy, col_energy
    )
    direct = {}
    for group, value in zip(groups, sent):
        k = group[0][0]
        landed = to_owner(value, k) if k else value
        for index, key in enumerate(group):
            direct[key] = (landed, index)

    shape = (owners, 1, pairs, rows, cols)
    result, other = None, {}
    for c in range(chunks):
        for k in far:
            value, index = direct[k, c]
            other[k, c] = (to_sibling(after(value, result if k == far[-1] else None)), index)
        if c == 0:
            near = to_sibling(after(direct[1, 0][0], (weights, own)))
            for index in range(chunks):
                other[0, index], other[1, index] = (own, index), (near, index)
        pieces = [held_by[k, c] for held_by in (direct, other) for k in range(owners)]
        result = finish(c, place, swap, weights, inverse, pieces, result, shape)
    return result


def solution(mesh):
    placed = (
        P(("mol", "pair"), "sub", None, None, "tile"),
        P(("mol", "pair"), None, None),
        P(("mol", "pair"), "sub", None),
        P(("mol", "pair"), "sub", None, "tile"),
        P("mol", None),
        P("mol", None),
        P("mol", "sub", None),
        P(("mol", "pair")),
        P(("mol", "tile")),
    )
    owners, subs = mesh.shape["pair"], mesh.shape["sub"]

    def local(*args):
        tile_rows, cols = args[0].shape[3:]
        rows = tile_rows // owners
        power = owners >= 4 and owners & (owners - 1) == 0
        fits = rows % ROWS == 0 and cols % LANES == 0 and args[1].shape[0] == 1
        if power and fits and subs == 2 and args[0].shape[2] % ROWS == 0:
            return local_chunked(*args)
        return local_general(*args)

    return jax.shard_map(
        local,
        mesh=mesh,
        in_specs=placed,
        out_specs=P("mol", "sub", None, "pair", "tile"),
        check_vma=False,
    )
```

```python
import functools
import math

import jax
import jax.numpy as jnp
from jax import lax
from jax.experimental import pallas as pl
from jax.experimental.pallas import tpu as pltpu
from jax.sharding import PartitionSpec as P

ROWS = 16
LANES = 128
VMEM_BYTES = 24 * 2**20


def column_tables(coupling, col_pairs):
    left_table = jnp.take(coupling.T, col_pairs[:, 0], axis=0).T
    right_table = jnp.take(coupling.T, col_pairs[:, 1], axis=0).T
    return (left_table, right_table)


def cycle_rows(left_table, right_table, row_pairs):
    left_part = jnp.take(left_table, row_pairs[:, 0], axis=0)
    right_part = jnp.take(right_table, row_pairs[:, 1], axis=0)
    return (left_part * right_part).astype(jnp.bfloat16)


def cycle_all(coupling, pair_list, col_pairs, flat_rhs):
    total_pairs = pair_list.shape[0]
    step_rows = math.gcd(total_pairs, 512)
    row_blocks = pair_list.reshape(total_pairs // step_rows, step_rows, 2)
    left_table, right_table = column_tables(coupling, col_pairs)

    def one_block(row_pairs):
        weights = cycle_rows(left_table, right_table, row_pairs)
        return jnp.dot(weights, flat_rhs, preferred_element_type=jnp.float32)

    return lax.map(one_block, row_blocks).reshape(total_pairs, -1)


def local_general(
    lambda_amps,
    integral_tiles,
    tile_of,
    tile_mask,
    pair_list,
    coupling,
    pair_gap,
    row_energy,
    col_energy,
):
    pair_count = lambda_amps.shape[2]
    tile_rows = lambda_amps.shape[3]
    col_count = lambda_amps.shape[4]
    owners = lax.axis_size("pair")
    sub_count = lax.axis_size("sub")
    wanted = tile_of.reshape(pair_count)
    empty_tiles = jnp.zeros((pair_count, tile_rows, tile_rows), integral_tiles.dtype)
    shard_piece = lax.all_gather(integral_tiles, "pair", axis=0, tiled=True)
    inside = (wanted >= 0) & (wanted < shard_piece.shape[0])
    taken_rows = shard_piece[jnp.clip(wanted, 0, shard_piece.shape[0] - 1)]
    chosen = jnp.where(inside[:, None, None], taken_rows, empty_tiles)
    amplitudes = lambda_amps.reshape(pair_count, tile_rows, col_count)
    ladder = jnp.einsum("pac,pcb->pab", chosen, amplitudes, preferred_element_type=jnp.float32)
    blocks = tile_mask.shape[3]
    keep_mask = tile_mask.reshape(pair_count, 1, blocks, 1).astype(jnp.float32)
    ladder = (
        ladder.reshape(pair_count, tile_rows, blocks, col_count // blocks) * keep_mask
    ).reshape(pair_count, tile_rows, col_count)
    dressed = (amplitudes.astype(jnp.float32) + ladder).astype(jnp.bfloat16)
    dressed = dressed.reshape(1, 1, pair_count, tile_rows, col_count)
    relayed = lax.all_to_all(dressed, "pair", split_axis=3, concat_axis=0, tiled=True)
    sub_index = lax.axis_index("sub")
    block_ids = jnp.arange(owners, dtype=jnp.int32) * sub_count + sub_index
    mine_ids = (
        block_ids[:, None] * pair_count + jnp.arange(pair_count, dtype=jnp.int32)[None, :]
    ).reshape(-1)
    col_pairs = pair_list[mine_ids]
    flat_rhs = relayed.reshape(owners * pair_count, -1)
    partial_value = cycle_all(coupling, pair_list, col_pairs, flat_rhs)
    partial_value = partial_value.reshape(
        owners, sub_count, pair_count, relayed.shape[3], col_count
    )
    cycle_term = lax.psum_scatter(
        partial_value.astype(jnp.bfloat16), "sub", scatter_dimension=1, tiled=True
    ).astype(jnp.float32)
    total_sum = relayed.astype(jnp.float32) + cycle_term
    energy_gap = (
        pair_gap[:, :, :, None, None]
        + row_energy[None, None, None, :, None]
        + col_energy[None, None, None, None, :]
    )
    return (-total_sum / energy_gap).astype(jnp.bfloat16)


def in_hbm(value):
    return pltpu.with_memory_space_constraint(value, pltpu.HBM)


def one_hot(hits):
    return jnp.where(hits, 1.0, 0.0).astype(jnp.bfloat16)


def square_iotas(size):
    return (lax.broadcasted_iota(jnp.int32, (size, size), axis) for axis in range(2))


def split3(value):
    high = value.astype(jnp.bfloat16)
    rest = value - high.astype(jnp.float32)
    mid = rest.astype(jnp.bfloat16)
    low = (rest - mid.astype(jnp.float32)).astype(jnp.bfloat16)
    return high, mid, low


def pick_columns(value, columns):
    high, mid, low = (
        jnp.dot(part, columns, preferred_element_type=jnp.float32) for part in split3(value)
    )
    return high + (mid + low)


def pick_rows(columns, value):
    dims = (((0,), (0,)), ((), ()))
    high, mid, low = (
        lax.dot_general(columns, part, dims, preferred_element_type=jnp.float32)
        for part in split3(value)
    )
    return high + (mid + low)


def hold_kernel(lam_ref, held_ref, swap_ref, sems):
    step = lam_ref.shape[2] // sems.shape[0]
    copies = []
    for i in range(sems.shape[0]):
        block = pl.ds(i * step, step)
        copy = pltpu.make_async_copy(
            lam_ref.at[:, :, block], held_ref.at[:, :, block], sems.at[i]
        )
        copy.start()
        copies.append(copy)
    to, frm = square_iotas(ROWS * ROWS)
    swap_ref[...] = one_hot(to == (frm % ROWS) * ROWS + frm // ROWS)
    for copy in copies:
        copy.wait()


def hold(lambda_amps):
    anywhere = pl.BlockSpec(memory_space=pl.ANY)
    return pl.pallas_call(
        hold_kernel,
        in_specs=[anywhere],
        out_specs=[anywhere, pl.BlockSpec(memory_space=pltpu.VMEM)],
        out_shape=[
            jax.ShapeDtypeStruct(lambda_amps.shape, lambda_amps.dtype),
            jax.ShapeDtypeStruct((ROWS * ROWS, ROWS * ROWS), jnp.bfloat16),
        ],
        scratch_shapes=[pltpu.SemaphoreType.DMA((8,))],
        compiler_params=pltpu.CompilerParams(vmem_limit_bytes=VMEM_BYTES),
        cost_estimate=pl.CostEstimate(
            flops=0, bytes_accessed=4 * lambda_amps.size, transcendentals=0
        ),
    )(in_hbm(lambda_amps))


def weights_kernel(
    pair_ref, coupling_ref, gap_ref, place_ref, row_ref, col_ref, w_ref, inverse_ref, full
):
    total = pair_ref.shape[1]
    depth = coupling_ref.shape[0]
    owners, _, pairs = gap_ref.shape
    me, sub = place_ref[0], place_ref[1]
    orbital = lax.broadcasted_iota(jnp.int32, (depth, total), 0)
    coupling = coupling_ref[...]
    product = None
    for side in range(2):
        columns = one_hot(orbital == pair_ref[side : side + 1, :])
        picked = pick_rows(columns, pick_columns(coupling, columns))
        product = picked if product is None else product * picked
    frm, to = square_iotas(total)
    block, within = to // pairs, to % pairs
    source = ((me ^ (block % owners)) * 2 + (sub ^ (block // owners))) * pairs + within
    full[...] = jnp.dot(
        product.astype(jnp.bfloat16), one_hot(frm == source), preferred_element_type=jnp.float32
    )
    row, column = square_iotas(pairs)
    for k in range(owners):
        start = pl.multiple_of(((me ^ k) * 2 + sub) * pairs, pairs)
        rows = pl.ds(k * pairs, pairs)
        w_ref[rows, :] = full[pl.ds(start, pairs), :].astype(jnp.bfloat16)
        gap = jnp.sum(jnp.where(row == column, gap_ref[me ^ k], 0.0), axis=1, keepdims=True)
        for a in range(inverse_ref.shape[0]):
            inverse_ref[a, rows, :] = -1.0 / ((gap + row_ref[a]) + col_ref[...])


def make_weights(pair_list, coupling, pair_gap, place, row_energy, col_energy):
    owners, _, pairs = pair_gap.shape
    total = pair_list.shape[0]
    mine = owners * pairs
    rows, cols = row_energy.shape[0], col_energy.shape[0]
    smem = pl.BlockSpec(memory_space=pltpu.SMEM)
    vmem = pl.BlockSpec(memory_space=pltpu.VMEM)
    return pl.pallas_call(
        weights_kernel,
        in_specs=[vmem, vmem, vmem, smem, smem, vmem],
        out_specs=[vmem, vmem],
        out_shape=[
            jax.ShapeDtypeStruct((mine, total), jnp.bfloat16),
            jax.ShapeDtypeStruct((rows, mine, cols), jnp.float32),
        ],
        scratch_shapes=[pltpu.VMEM((total, total), jnp.float32)],
        compiler_params=pltpu.CompilerParams(vmem_limit_bytes=VMEM_BYTES),
        cost_estimate=pl.CostEstimate(
            flops=12 * total * coupling.size, bytes_accessed=4 * coupling.size, transcendentals=0
        ),
    )(pair_list.T, coupling, pair_gap, place, row_energy, col_energy.reshape(1, cols))


def dress_kernel(owners, rows, groups, place_ref, tile_of_ref, mask_ref, *refs):
    tile_refs, lam_ref = (refs[0], refs[owners - 1], *refs[1 : owners - 1]), refs[owners]
    swap_ref = refs[owners + 1]
    out_refs = refs[owners + 2 : -2]
    tiles, stage = refs[-2:]
    me = place_ref[0]
    flat = [(k, c, out, j) for out, group in zip(out_refs, groups) for j, (k, c) in enumerate(group)]
    starts = [pl.multiple_of((me ^ k) * rows + c * ROWS, ROWS) for k, c, _, _ in flat]
    tile_rows, cols = lam_ref.shape[3:]
    row = lax.broadcasted_iota(jnp.int32, (ROWS, tile_rows), 0)
    column = lax.broadcasted_iota(jnp.int32, (ROWS, tile_rows), 1)
    for n, start in enumerate(starts):
        block = pl.ds(n * ROWS, ROWS)
        own_row = one_hot(column == row + start)
        for k in range(owners):
            tiles[k, block, :tile_rows] = tile_refs[k][0, pl.ds(start, ROWS), :]
            tiles[k, block, tile_rows:] = own_row
    swap = swap_ref[...]
    parts = mask_ref.shape[2]
    width = cols // parts
    for g in range(lam_ref.shape[2] // ROWS):
        for i in range(ROWS):
            pair = g * ROWS + i
            amps = lam_ref[0, 0, pair]
            kept = [
                amps[:, part * width : (part + 1) * width]
                * mask_ref[0, 0, part, pair].astype(jnp.float32).astype(jnp.bfloat16)
                for part in range(parts)
            ]
            both = jnp.concatenate([jnp.concatenate(kept, axis=1), amps], axis=0)
            full = jnp.dot(
                tiles[tile_of_ref[0, 0, pair] ^ me], both, preferred_element_type=jnp.float32
            ).astype(jnp.bfloat16)
            for n in range(len(flat)):
                stage[g, n, pl.ds(i * ROWS, ROWS), :] = full[n * ROWS : (n + 1) * ROWS]
        for n, (_, _, out, j) in enumerate(flat):
            turned = jnp.dot(swap, stage[g, n], preferred_element_type=jnp.float32)
            out[j, :, pl.ds(g * ROWS, ROWS), :] = turned.astype(jnp.bfloat16).reshape(
                ROWS, ROWS, turned.shape[1]
            )


def dress(groups, place, tile_of, tile_mask, tiles, lambda_amps, swap):
    owners = len(tiles)
    pairs, tile_rows, cols = lambda_amps.shape[2:]
    rows = tile_rows // owners
    smem = pl.BlockSpec(memory_space=pltpu.SMEM)
    vmem = pl.BlockSpec(memory_space=pltpu.VMEM)
    count = sum(len(group) for group in groups)
    return pl.pallas_call(
        functools.partial(dress_kernel, owners, rows, groups),
        in_specs=[smem] * 3 + [vmem] * (owners + 2),
        out_specs=[vmem] * len(groups),
        out_shape=[
            jax.ShapeDtypeStruct((len(group), ROWS, pairs, cols), jnp.bfloat16)
            for group in groups
        ],
        scratch_shapes=[
            pltpu.VMEM((owners, count * ROWS, 2 * tile_rows), jnp.bfloat16),
            pltpu.VMEM((pairs // ROWS, count, ROWS * ROWS, cols), jnp.bfloat16),
        ],
        compiler_params=pltpu.CompilerParams(vmem_limit_bytes=VMEM_BYTES),
        cost_estimate=pl.CostEstimate(
            flops=2 * pairs * count * ROWS * tile_rows * cols,
            bytes_accessed=3 * pairs * tile_rows * cols,
            transcendentals=0,
        ),
    )(
        place,
        in_hbm(tile_of),
        in_hbm(jnp.swapaxes(tile_mask, 2, 3)),
        in_hbm(tiles[0]),
        *tiles[2:],
        tiles[1],
        lambda_amps,
        swap,
    )


def finish_kernel(indices, chunk, place_ref, swap_ref, w_ref, inverse_ref, *refs):
    pieces = len(indices)
    piece_refs = refs[:pieces]
    out_ref, ys, done, sems = refs[-4:]
    _, rows, pairs, cols = piece_refs[0].shape
    owners = pieces // 2
    halves = pairs // ROWS
    mine = owners * pairs
    me = place_ref[0]
    weights = w_ref[...]
    for a in range(rows):
        amps = jnp.concatenate([ref[index, a] for ref, index in zip(piece_refs, indices)], axis=0)
        cycle = jnp.dot(weights, amps, preferred_element_type=jnp.float32)
        total = amps[:mine].astype(jnp.float32) + cycle
        value = (total * inverse_ref[chunk * rows + a]).astype(jnp.bfloat16)
        for g in range(owners * halves):
            ys[g, pl.ds(a * ROWS, ROWS), :] = value[g * ROWS : (g + 1) * ROWS]
    swap = swap_ref[...]
    leaving = []
    for g in range(owners * halves):
        turned = jnp.dot(swap, ys[g], preferred_element_type=jnp.float32)
        done[g] = turned.astype(jnp.bfloat16).reshape(ROWS, rows, cols)
        k, h = g // halves, g % halves
        copy = pltpu.make_async_copy(
            done.at[g],
            out_ref.at[me ^ k, 0, pl.ds(h * ROWS, ROWS), pl.ds(chunk * rows, rows), :],
            sems.at[g],
        )
        copy.start()
        leaving.append(copy)
    for copy in leaving:
        copy.wait()


def finish(chunk, place, swap, weights, inverse, pieces, before, shape):
    _, rows, pairs, cols = pieces[0][0].shape
    owners = len(pieces) // 2
    groups = owners * (pairs // ROWS)
    anywhere = pl.BlockSpec(memory_space=pl.ANY)
    args = [place, swap, weights, inverse] + [piece for piece, _ in pieces]
    in_specs = [pl.BlockSpec(memory_space=pltpu.SMEM)]
    in_specs += [pl.BlockSpec(memory_space=pltpu.VMEM)] * (3 + len(pieces))
    aliases = {}
    if before is not None:
        aliases = {len(args): 0}
        args.append(before)
        in_specs.append(anywhere)
    return pl.pallas_call(
        functools.partial(finish_kernel, [index for _, index in pieces], chunk),
        in_specs=in_specs,
        out_specs=anywhere,
        out_shape=jax.ShapeDtypeStruct(shape, jnp.bfloat16),
        scratch_shapes=[
            pltpu.VMEM((groups, ROWS * rows, cols), jnp.bfloat16),
            pltpu.VMEM((groups, ROWS, rows, cols), jnp.bfloat16),
            pltpu.SemaphoreType.DMA((groups,)),
        ],
        input_output_aliases=aliases,
        compiler_params=pltpu.CompilerParams(vmem_limit_bytes=VMEM_BYTES),
        cost_estimate=pl.CostEstimate(flops=0, bytes_accessed=0, transcendentals=0),
    )(*args)


def local_chunked(
    lambda_amps,
    integral_tiles,
    tile_of,
    tile_mask,
    pair_list,
    coupling,
    pair_gap,
    row_energy,
    col_energy,
):
    pairs, tile_rows, cols = lambda_amps.shape[2:]
    owners = lax.axis_size("pair")
    rows = tile_rows // owners
    chunks = rows // ROWS
    me = lax.axis_index("pair").astype(jnp.int32)
    sub = lax.axis_index("sub").astype(jnp.int32)
    place = jnp.stack([me, sub])

    def to_owner(value, k):
        return lax.ppermute(value, "pair", [(o, o ^ k) for o in range(owners)])

    def to_sibling(value):
        return lax.ppermute(value, "sub", [(0, 1), (1, 0)])

    def after(value, earlier):
        return value if earlier is None else lax.optimization_barrier((value, earlier))[0]

    tiles = [integral_tiles] + [to_owner(integral_tiles, k) for k in range(1, owners)]

    far = list(range(2, owners))
    last = far[-1]
    groups = [((k, c),) for c in range(chunks) for k in far[::-1]]
    groups += [tuple((k, c) for c in range(chunks)) for k in (1, 0)]
    held, swap = hold(lambda_amps)
    sent = dict(zip(groups, dress(groups, place, tile_of, tile_mask, tiles, held, swap)))
    weights, inverse = make_weights(
        after(pair_list, sent[groups[0]]), coupling, pair_gap, place, row_energy, col_energy
    )
    own, near = sent[groups[-1]], to_owner(sent[groups[-2]], 1)
    direct, other = {}, {}
    for k in far:
        for c in range(chunks):
            earlier = direct[k, c - 1] if c and k == last else None
            direct[k, c] = to_owner(after(sent[((k, c),)], earlier), k)
    own_passed = to_sibling(after(own, direct[last, 0]))
    near_passed = to_sibling(after(near, (weights, direct[far[0], 0])))
    for k in far:
        for c in range(chunks):
            earlier = other[k, c - 1] if c else None
            other[k, c] = to_sibling(after(direct[k, c], earlier))

    result = None
    for c in range(chunks):
        pieces = [(own, c), (near, c)] + [(direct[k, c], 0) for k in far]
        pieces += [(own_passed, c), (near_passed, c)] + [(other[k, c], 0) for k in far]
        shape = (owners, 1, pairs, rows, cols)
        result = finish(c, place, swap, weights, inverse, pieces, result, shape)
    return result


def solution(mesh):
    placed = (
        P(("mol", "pair"), "sub", None, None, "tile"),
        P(("mol", "pair"), None, None),
        P(("mol", "pair"), "sub", None),
        P(("mol", "pair"), "sub", None, "tile"),
        P("mol", None),
        P("mol", None),
        P("mol", "sub", None),
        P(("mol", "pair")),
        P(("mol", "tile")),
    )
    owners, subs = mesh.shape["pair"], mesh.shape["sub"]

    def local(*args):
        tile_rows, cols = args[0].shape[3:]
        rows = tile_rows // owners
        power = owners >= 4 and owners & (owners - 1) == 0
        fits = rows % ROWS == 0 and cols % LANES == 0 and args[1].shape[0] == 1
        if power and fits and subs == 2 and args[0].shape[2] % ROWS == 0:
            return local_chunked(*args)
        return local_general(*args)

    return jax.shard_map(
        local,
        mesh=mesh,
        in_specs=placed,
        out_specs=P("mol", "sub", None, "pair", "tile"),
        check_vma=False,
    )
```

```python
import functools
import math

import jax
import jax.numpy as jnp
from jax import lax
from jax.experimental import pallas as pl
from jax.experimental.pallas import tpu as pltpu
from jax.sharding import PartitionSpec as P

ROWS = 16
LANES = 128
VMEM_BYTES = 24 * 2**20


def column_tables(coupling, col_pairs):
    left_table = jnp.take(coupling.T, col_pairs[:, 0], axis=0).T
    right_table = jnp.take(coupling.T, col_pairs[:, 1], axis=0).T
    return (left_table, right_table)


def cycle_rows(left_table, right_table, row_pairs):
    left_part = jnp.take(left_table, row_pairs[:, 0], axis=0)
    right_part = jnp.take(right_table, row_pairs[:, 1], axis=0)
    return (left_part * right_part).astype(jnp.bfloat16)


def cycle_all(coupling, pair_list, col_pairs, flat_rhs):
    total_pairs = pair_list.shape[0]
    step_rows = math.gcd(total_pairs, 512)
    row_blocks = pair_list.reshape(total_pairs // step_rows, step_rows, 2)
    left_table, right_table = column_tables(coupling, col_pairs)

    def one_block(row_pairs):
        weights = cycle_rows(left_table, right_table, row_pairs)
        return jnp.dot(weights, flat_rhs, preferred_element_type=jnp.float32)

    return lax.map(one_block, row_blocks).reshape(total_pairs, -1)


def local_general(
    lambda_amps,
    integral_tiles,
    tile_of,
    tile_mask,
    pair_list,
    coupling,
    pair_gap,
    row_energy,
    col_energy,
):
    pair_count = lambda_amps.shape[2]
    tile_rows = lambda_amps.shape[3]
    col_count = lambda_amps.shape[4]
    owners = lax.axis_size("pair")
    sub_count = lax.axis_size("sub")
    wanted = tile_of.reshape(pair_count)
    empty_tiles = jnp.zeros((pair_count, tile_rows, tile_rows), integral_tiles.dtype)
    shard_piece = lax.all_gather(integral_tiles, "pair", axis=0, tiled=True)
    inside = (wanted >= 0) & (wanted < shard_piece.shape[0])
    taken_rows = shard_piece[jnp.clip(wanted, 0, shard_piece.shape[0] - 1)]
    chosen = jnp.where(inside[:, None, None], taken_rows, empty_tiles)
    amplitudes = lambda_amps.reshape(pair_count, tile_rows, col_count)
    ladder = jnp.einsum("pac,pcb->pab", chosen, amplitudes, preferred_element_type=jnp.float32)
    blocks = tile_mask.shape[3]
    keep_mask = tile_mask.reshape(pair_count, 1, blocks, 1).astype(jnp.float32)
    ladder = (
        ladder.reshape(pair_count, tile_rows, blocks, col_count // blocks) * keep_mask
    ).reshape(pair_count, tile_rows, col_count)
    dressed = (amplitudes.astype(jnp.float32) + ladder).astype(jnp.bfloat16)
    dressed = dressed.reshape(1, 1, pair_count, tile_rows, col_count)
    relayed = lax.all_to_all(dressed, "pair", split_axis=3, concat_axis=0, tiled=True)
    sub_index = lax.axis_index("sub")
    block_ids = jnp.arange(owners, dtype=jnp.int32) * sub_count + sub_index
    mine_ids = (
        block_ids[:, None] * pair_count + jnp.arange(pair_count, dtype=jnp.int32)[None, :]
    ).reshape(-1)
    col_pairs = pair_list[mine_ids]
    flat_rhs = relayed.reshape(owners * pair_count, -1)
    partial_value = cycle_all(coupling, pair_list, col_pairs, flat_rhs)
    partial_value = partial_value.reshape(
        owners, sub_count, pair_count, relayed.shape[3], col_count
    )
    cycle_term = lax.psum_scatter(
        partial_value.astype(jnp.bfloat16), "sub", scatter_dimension=1, tiled=True
    ).astype(jnp.float32)
    total_sum = relayed.astype(jnp.float32) + cycle_term
    energy_gap = (
        pair_gap[:, :, :, None, None]
        + row_energy[None, None, None, :, None]
        + col_energy[None, None, None, None, :]
    )
    return (-total_sum / energy_gap).astype(jnp.bfloat16)


def in_hbm(value):
    return pltpu.with_memory_space_constraint(value, pltpu.HBM)


def one_hot(hits):
    return jnp.where(hits, 1.0, 0.0).astype(jnp.bfloat16)


def square_iotas(size):
    return (lax.broadcasted_iota(jnp.int32, (size, size), axis) for axis in range(2))


def split3(value):
    high = value.astype(jnp.bfloat16)
    rest = value - high.astype(jnp.float32)
    mid = rest.astype(jnp.bfloat16)
    low = (rest - mid.astype(jnp.float32)).astype(jnp.bfloat16)
    return high, mid, low


def pick_columns(value, columns):
    high, mid, low = (
        jnp.dot(part, columns, preferred_element_type=jnp.float32) for part in split3(value)
    )
    return high + (mid + low)


def pick_rows(columns, value):
    dims = (((0,), (0,)), ((), ()))
    high, mid, low = (
        lax.dot_general(columns, part, dims, preferred_element_type=jnp.float32)
        for part in split3(value)
    )
    return high + (mid + low)


def hold_kernel(lam_ref, held_ref, swap_ref, sems):
    step = lam_ref.shape[2] // sems.shape[0]
    copies = []
    for i in range(sems.shape[0]):
        block = pl.ds(i * step, step)
        copy = pltpu.make_async_copy(
            lam_ref.at[:, :, block], held_ref.at[:, :, block], sems.at[i]
        )
        copy.start()
        copies.append(copy)
    to, frm = square_iotas(ROWS * ROWS)
    swap_ref[...] = one_hot(to == (frm % ROWS) * ROWS + frm // ROWS)
    for copy in copies:
        copy.wait()


def hold(lambda_amps):
    anywhere = pl.BlockSpec(memory_space=pl.ANY)
    return pl.pallas_call(
        hold_kernel,
        in_specs=[anywhere],
        out_specs=[anywhere, pl.BlockSpec(memory_space=pltpu.VMEM)],
        out_shape=[
            jax.ShapeDtypeStruct(lambda_amps.shape, lambda_amps.dtype),
            jax.ShapeDtypeStruct((ROWS * ROWS, ROWS * ROWS), jnp.bfloat16),
        ],
        scratch_shapes=[pltpu.SemaphoreType.DMA((8,))],
        compiler_params=pltpu.CompilerParams(vmem_limit_bytes=VMEM_BYTES),
        cost_estimate=pl.CostEstimate(
            flops=0, bytes_accessed=4 * lambda_amps.size, transcendentals=0
        ),
    )(in_hbm(lambda_amps))


def weights_kernel(
    pair_ref, coupling_ref, gap_ref, place_ref, row_ref, col_ref, w_ref, inverse_ref, full
):
    total = pair_ref.shape[1]
    depth = coupling_ref.shape[0]
    owners, _, pairs = gap_ref.shape
    me, sub = place_ref[0], place_ref[1]
    orbital = lax.broadcasted_iota(jnp.int32, (depth, total), 0)
    coupling = coupling_ref[...]
    product = None
    for side in range(2):
        columns = one_hot(orbital == pair_ref[side : side + 1, :])
        picked = pick_rows(columns, pick_columns(coupling, columns))
        product = picked if product is None else product * picked
    frm, to = square_iotas(total)
    block, within = to // pairs, to % pairs
    source = ((me ^ (block % owners)) * 2 + (sub ^ (block // owners))) * pairs + within
    full[...] = jnp.dot(
        product.astype(jnp.bfloat16), one_hot(frm == source), preferred_element_type=jnp.float32
    )
    row, column = square_iotas(pairs)
    for k in range(owners):
        start = pl.multiple_of(((me ^ k) * 2 + sub) * pairs, pairs)
        rows = pl.ds(k * pairs, pairs)
        w_ref[rows, :] = full[pl.ds(start, pairs), :].astype(jnp.bfloat16)
        gap = jnp.sum(jnp.where(row == column, gap_ref[me ^ k], 0.0), axis=1, keepdims=True)
        for a in range(inverse_ref.shape[0]):
            inverse_ref[a, rows, :] = -1.0 / ((gap + row_ref[a]) + col_ref[...])


def make_weights(pair_list, coupling, pair_gap, place, row_energy, col_energy):
    owners, _, pairs = pair_gap.shape
    total = pair_list.shape[0]
    mine = owners * pairs
    rows, cols = row_energy.shape[0], col_energy.shape[0]
    smem = pl.BlockSpec(memory_space=pltpu.SMEM)
    vmem = pl.BlockSpec(memory_space=pltpu.VMEM)
    return pl.pallas_call(
        weights_kernel,
        in_specs=[vmem, vmem, vmem, smem, smem, vmem],
        out_specs=[vmem, vmem],
        out_shape=[
            jax.ShapeDtypeStruct((mine, total), jnp.bfloat16),
            jax.ShapeDtypeStruct((rows, mine, cols), jnp.float32),
        ],
        scratch_shapes=[pltpu.VMEM((total, total), jnp.float32)],
        compiler_params=pltpu.CompilerParams(vmem_limit_bytes=VMEM_BYTES),
        cost_estimate=pl.CostEstimate(
            flops=12 * total * coupling.size, bytes_accessed=4 * coupling.size, transcendentals=0
        ),
    )(pair_list.T, coupling, pair_gap, place, row_energy, col_energy.reshape(1, cols))


def dress_kernel(owners, rows, groups, place_ref, tile_of_ref, mask_ref, *refs):
    tile_refs, lam_ref = (refs[0], refs[owners - 1], *refs[1 : owners - 1]), refs[owners]
    swap_ref = refs[owners + 1]
    out_refs = refs[owners + 2 : -2]
    tiles, stage = refs[-2:]
    me = place_ref[0]
    flat = [(k, c, out, j) for out, group in zip(out_refs, groups) for j, (k, c) in enumerate(group)]
    starts = [pl.multiple_of((me ^ k) * rows + c * ROWS, ROWS) for k, c, _, _ in flat]
    tile_rows, cols = lam_ref.shape[3:]
    row = lax.broadcasted_iota(jnp.int32, (ROWS, tile_rows), 0)
    column = lax.broadcasted_iota(jnp.int32, (ROWS, tile_rows), 1)
    for n, start in enumerate(starts):
        block = pl.ds(n * ROWS, ROWS)
        own_row = one_hot(column == row + start)
        for k in range(owners):
            tiles[k, block, :tile_rows] = tile_refs[k][0, pl.ds(start, ROWS), :]
            tiles[k, block, tile_rows:] = own_row
    swap = swap_ref[...]
    parts = mask_ref.shape[2]
    width = cols // parts
    for g in range(lam_ref.shape[2] // ROWS):
        for i in range(ROWS):
            pair = g * ROWS + i
            amps = lam_ref[0, 0, pair]
            kept = [
                amps[:, part * width : (part + 1) * width]
                * mask_ref[0, 0, part, pair].astype(jnp.float32).astype(jnp.bfloat16)
                for part in range(parts)
            ]
            both = jnp.concatenate([jnp.concatenate(kept, axis=1), amps], axis=0)
            full = jnp.dot(
                tiles[tile_of_ref[0, 0, pair] ^ me], both, preferred_element_type=jnp.float32
            ).astype(jnp.bfloat16)
            for n in range(len(flat)):
                stage[g, n, pl.ds(i * ROWS, ROWS), :] = full[n * ROWS : (n + 1) * ROWS]
        for n, (_, _, out, j) in enumerate(flat):
            turned = jnp.dot(swap, stage[g, n], preferred_element_type=jnp.float32)
            out[j, :, pl.ds(g * ROWS, ROWS), :] = turned.astype(jnp.bfloat16).reshape(
                ROWS, ROWS, turned.shape[1]
            )


def dress(groups, place, tile_of, tile_mask, tiles, lambda_amps, swap):
    owners = len(tiles)
    pairs, tile_rows, cols = lambda_amps.shape[2:]
    rows = tile_rows // owners
    smem = pl.BlockSpec(memory_space=pltpu.SMEM)
    vmem = pl.BlockSpec(memory_space=pltpu.VMEM)
    count = sum(len(group) for group in groups)
    return pl.pallas_call(
        functools.partial(dress_kernel, owners, rows, groups),
        in_specs=[smem] * 3 + [vmem] * (owners + 2),
        out_specs=[vmem] * len(groups),
        out_shape=[
            jax.ShapeDtypeStruct((len(group), ROWS, pairs, cols), jnp.bfloat16)
            for group in groups
        ],
        scratch_shapes=[
            pltpu.VMEM((owners, count * ROWS, 2 * tile_rows), jnp.bfloat16),
            pltpu.VMEM((pairs // ROWS, count, ROWS * ROWS, cols), jnp.bfloat16),
        ],
        compiler_params=pltpu.CompilerParams(vmem_limit_bytes=VMEM_BYTES),
        cost_estimate=pl.CostEstimate(
            flops=2 * pairs * count * ROWS * tile_rows * cols,
            bytes_accessed=3 * pairs * tile_rows * cols,
            transcendentals=0,
        ),
    )(
        place,
        in_hbm(tile_of),
        in_hbm(jnp.swapaxes(tile_mask, 2, 3)),
        in_hbm(tiles[0]),
        *tiles[2:],
        tiles[1],
        lambda_amps,
        swap,
    )


def finish_blocks(indices, chunk, swap_ref, w_ref, inverse_ref, piece_refs, done, ys, then):
    groups, _, rows, _ = done.shape
    mine = groups * ROWS
    weights = w_ref[...]
    for a in range(rows):
        amps = jnp.concatenate([ref[index, a] for ref, index in zip(piece_refs, indices)], axis=0)
        cycle = jnp.dot(weights, amps, preferred_element_type=jnp.float32)
        total = amps[:mine].astype(jnp.float32) + cycle
        value = (total * inverse_ref[chunk * rows + a]).astype(jnp.bfloat16)
        for g in range(groups):
            ys[g, pl.ds(a * ROWS, ROWS), :] = value[g * ROWS : (g + 1) * ROWS]
    swap = swap_ref[...]
    for g in range(groups):
        turned = jnp.dot(swap, ys[g], preferred_element_type=jnp.float32)
        done[g] = turned.astype(jnp.bfloat16).reshape(done.shape[1:])
        then(g)


def early_kernel(indices, chunk, swap_ref, w_ref, inverse_ref, *refs):
    piece_refs, (done, ys) = refs[:-2], refs[-2:]
    finish_blocks(
        indices, chunk, swap_ref, w_ref, inverse_ref, piece_refs, done, ys, lambda g: None
    )


def last_kernel(indices, chunk, swap_ref, w_ref, inverse_ref, place_ref, *refs):
    ready_refs, piece_refs, (out_ref, done, ys, sems) = refs[:chunk], refs[chunk:-4], refs[-4:]
    groups, _, rows, _ = done.shape
    halves = 2 * groups // len(indices)
    me = place_ref[0]
    leaving = []

    def write(source, c, g):
        k, h = g // halves, g % halves
        copy = pltpu.make_async_copy(
            source.at[g],
            out_ref.at[me ^ k, 0, pl.ds(h * ROWS, ROWS), pl.ds(c * rows, rows), :],
            sems.at[c, g],
        )
        copy.start()
        leaving.append(copy)

    for c, ref in enumerate(ready_refs):
        for g in range(groups):
            write(ref, c, g)
    finish_blocks(
        indices,
        chunk,
        swap_ref,
        w_ref,
        inverse_ref,
        piece_refs,
        done,
        ys,
        lambda g: write(done, chunk, g),
    )
    for copy in leaving:
        copy.wait()


def finish(chunk, swap, weights, inverse, pieces, place=None, ready=(), shape=None):
    _, rows, pairs, cols = pieces[0][0].shape
    groups = len(pieces) // 2 * (pairs // ROWS)
    indices = [index for _, index in pieces]
    vmem, anywhere = pl.BlockSpec(memory_space=pltpu.VMEM), pl.BlockSpec(memory_space=pl.ANY)
    block = (groups, ROWS, rows, cols)
    ys = pltpu.VMEM((groups, ROWS * rows, cols), jnp.bfloat16)
    args, in_specs = [swap, weights, inverse], [vmem] * 3
    if shape is None:
        kernel = functools.partial(early_kernel, indices, chunk)
        out_spec, out_shape = vmem, jax.ShapeDtypeStruct(block, jnp.bfloat16)
        scratch = [ys]
    else:
        kernel = functools.partial(last_kernel, indices, chunk)
        out_spec, out_shape = anywhere, jax.ShapeDtypeStruct(shape, jnp.bfloat16)
        scratch = [pltpu.VMEM(block, jnp.bfloat16), ys]
        scratch += [pltpu.SemaphoreType.DMA((chunk + 1, groups))]
        args += [place, *ready]
        in_specs += [pl.BlockSpec(memory_space=pltpu.SMEM)] + [anywhere] * len(ready)
    return pl.pallas_call(
        kernel,
        in_specs=in_specs + [vmem] * len(pieces),
        out_specs=out_spec,
        out_shape=out_shape,
        scratch_shapes=scratch,
        compiler_params=pltpu.CompilerParams(vmem_limit_bytes=VMEM_BYTES),
        cost_estimate=pl.CostEstimate(flops=0, bytes_accessed=0, transcendentals=0),
    )(*args, *[piece for piece, _ in pieces])


def local_chunked(
    lambda_amps,
    integral_tiles,
    tile_of,
    tile_mask,
    pair_list,
    coupling,
    pair_gap,
    row_energy,
    col_energy,
):
    pairs, tile_rows, cols = lambda_amps.shape[2:]
    owners = lax.axis_size("pair")
    rows = tile_rows // owners
    chunks = rows // ROWS
    me = lax.axis_index("pair").astype(jnp.int32)
    sub = lax.axis_index("sub").astype(jnp.int32)
    place = jnp.stack([me, sub])

    def to_owner(value, k):
        return lax.ppermute(value, "pair", [(o, o ^ k) for o in range(owners)])

    def to_sibling(value):
        return lax.ppermute(value, "sub", [(0, 1), (1, 0)])

    def after(value, earlier):
        return value if earlier is None else lax.optimization_barrier((value, earlier))[0]

    tiles = [integral_tiles] + [to_owner(integral_tiles, k) for k in range(1, owners)]

    far = list(range(2, owners))
    last = far[-1]
    groups = [((k, c),) for c in range(chunks) for k in far[::-1]]
    groups += [tuple((k, c) for c in range(chunks)) for k in (1, 0)]
    held, swap = hold(lambda_amps)
    sent = dict(zip(groups, dress(groups, place, tile_of, tile_mask, tiles, held, swap)))
    weights, inverse = make_weights(
        after(pair_list, sent[groups[0]]), coupling, pair_gap, place, row_energy, col_energy
    )
    own, near = sent[groups[-1]], to_owner(sent[groups[-2]], 1)
    direct, other = {}, {}
    for k in far:
        for c in range(chunks):
            earlier = direct[k, c - 1] if c and k == last else None
            direct[k, c] = to_owner(after(sent[((k, c),)], earlier), k)
    own_passed = to_sibling(after(own, direct[last, 0]))
    near_passed = to_sibling(after(near, (weights, direct[far[0], 0])))
    for k in far:
        for c in range(chunks):
            earlier = other[k, c - 1] if c else None
            other[k, c] = to_sibling(after(direct[k, c], earlier))

    ready = []
    for c in range(chunks):
        pieces = [(own, c), (near, c)] + [(direct[k, c], 0) for k in far]
        pieces += [(own_passed, c), (near_passed, c)] + [(other[k, c], 0) for k in far]
        if c + 1 < chunks:
            ready.append(finish(c, swap, weights, inverse, pieces))
    shape = (owners, 1, pairs, rows, cols)
    return finish(c, swap, weights, inverse, pieces, place, ready, shape)


def solution(mesh):
    placed = (
        P(("mol", "pair"), "sub", None, None, "tile"),
        P(("mol", "pair"), None, None),
        P(("mol", "pair"), "sub", None),
        P(("mol", "pair"), "sub", None, "tile"),
        P("mol", None),
        P("mol", None),
        P("mol", "sub", None),
        P(("mol", "pair")),
        P(("mol", "tile")),
    )
    owners, subs = mesh.shape["pair"], mesh.shape["sub"]

    def local(*args):
        tile_rows, cols = args[0].shape[3:]
        rows = tile_rows // owners
        power = owners >= 4 and owners & (owners - 1) == 0
        fits = rows % ROWS == 0 and cols % LANES == 0 and args[1].shape[0] == 1
        if power and fits and subs == 2 and args[0].shape[2] % ROWS == 0:
            return local_chunked(*args)
        return local_general(*args)

    return jax.shard_map(
        local,
        mesh=mesh,
        in_specs=placed,
        out_specs=P("mol", "sub", None, "pair", "tile"),
        check_vma=False,
    )
```

```python
import functools
import math

import jax
import jax.numpy as jnp
from jax import lax
from jax.experimental import pallas as pl
from jax.experimental.pallas import tpu as pltpu
from jax.sharding import PartitionSpec as P

ROWS = 16
LANES = 128
VMEM_BYTES = 24 * 2**20


def column_tables(coupling, col_pairs):
    left_table = jnp.take(coupling.T, col_pairs[:, 0], axis=0).T
    right_table = jnp.take(coupling.T, col_pairs[:, 1], axis=0).T
    return (left_table, right_table)


def cycle_rows(left_table, right_table, row_pairs):
    left_part = jnp.take(left_table, row_pairs[:, 0], axis=0)
    right_part = jnp.take(right_table, row_pairs[:, 1], axis=0)
    return (left_part * right_part).astype(jnp.bfloat16)


def cycle_all(coupling, pair_list, col_pairs, flat_rhs):
    total_pairs = pair_list.shape[0]
    step_rows = math.gcd(total_pairs, 512)
    row_blocks = pair_list.reshape(total_pairs // step_rows, step_rows, 2)
    left_table, right_table = column_tables(coupling, col_pairs)

    def one_block(row_pairs):
        weights = cycle_rows(left_table, right_table, row_pairs)
        return jnp.dot(weights, flat_rhs, preferred_element_type=jnp.float32)

    return lax.map(one_block, row_blocks).reshape(total_pairs, -1)


def local_general(
    lambda_amps,
    integral_tiles,
    tile_of,
    tile_mask,
    pair_list,
    coupling,
    pair_gap,
    row_energy,
    col_energy,
):
    pair_count = lambda_amps.shape[2]
    tile_rows = lambda_amps.shape[3]
    col_count = lambda_amps.shape[4]
    owners = lax.axis_size("pair")
    sub_count = lax.axis_size("sub")
    wanted = tile_of.reshape(pair_count)
    empty_tiles = jnp.zeros((pair_count, tile_rows, tile_rows), integral_tiles.dtype)
    shard_piece = lax.all_gather(integral_tiles, "pair", axis=0, tiled=True)
    inside = (wanted >= 0) & (wanted < shard_piece.shape[0])
    taken_rows = shard_piece[jnp.clip(wanted, 0, shard_piece.shape[0] - 1)]
    chosen = jnp.where(inside[:, None, None], taken_rows, empty_tiles)
    amplitudes = lambda_amps.reshape(pair_count, tile_rows, col_count)
    ladder = jnp.einsum("pac,pcb->pab", chosen, amplitudes, preferred_element_type=jnp.float32)
    blocks = tile_mask.shape[3]
    keep_mask = tile_mask.reshape(pair_count, 1, blocks, 1).astype(jnp.float32)
    ladder = (
        ladder.reshape(pair_count, tile_rows, blocks, col_count // blocks) * keep_mask
    ).reshape(pair_count, tile_rows, col_count)
    dressed = (amplitudes.astype(jnp.float32) + ladder).astype(jnp.bfloat16)
    dressed = dressed.reshape(1, 1, pair_count, tile_rows, col_count)
    relayed = lax.all_to_all(dressed, "pair", split_axis=3, concat_axis=0, tiled=True)
    sub_index = lax.axis_index("sub")
    block_ids = jnp.arange(owners, dtype=jnp.int32) * sub_count + sub_index
    mine_ids = (
        block_ids[:, None] * pair_count + jnp.arange(pair_count, dtype=jnp.int32)[None, :]
    ).reshape(-1)
    col_pairs = pair_list[mine_ids]
    flat_rhs = relayed.reshape(owners * pair_count, -1)
    partial_value = cycle_all(coupling, pair_list, col_pairs, flat_rhs)
    partial_value = partial_value.reshape(
        owners, sub_count, pair_count, relayed.shape[3], col_count
    )
    cycle_term = lax.psum_scatter(
        partial_value.astype(jnp.bfloat16), "sub", scatter_dimension=1, tiled=True
    ).astype(jnp.float32)
    total_sum = relayed.astype(jnp.float32) + cycle_term
    energy_gap = (
        pair_gap[:, :, :, None, None]
        + row_energy[None, None, None, :, None]
        + col_energy[None, None, None, None, :]
    )
    return (-total_sum / energy_gap).astype(jnp.bfloat16)


def in_hbm(value):
    return pltpu.with_memory_space_constraint(value, pltpu.HBM)


def in_smem(value):
    return pltpu.with_memory_space_constraint(value, pltpu.SMEM)


def one_hot(hits):
    return jnp.where(hits, 1.0, 0.0).astype(jnp.bfloat16)


def square_iotas(size):
    return (lax.broadcasted_iota(jnp.int32, (size, size), axis) for axis in range(2))


def split3(value):
    high = value.astype(jnp.bfloat16)
    rest = value - high.astype(jnp.float32)
    mid = rest.astype(jnp.bfloat16)
    low = (rest - mid.astype(jnp.float32)).astype(jnp.bfloat16)
    return high, mid, low


def pick_columns(value, columns):
    high, mid, low = (
        jnp.dot(part, columns, preferred_element_type=jnp.float32) for part in split3(value)
    )
    return high + (mid + low)


def pick_rows(columns, value):
    dims = (((0,), (0,)), ((), ()))
    high, mid, low = (
        lax.dot_general(columns, part, dims, preferred_element_type=jnp.float32)
        for part in split3(value)
    )
    return high + (mid + low)


def hold_kernel(lam_ref, held_ref, swap_ref, sems):
    step = lam_ref.shape[2] // sems.shape[0]
    copies = []
    for i in range(sems.shape[0]):
        block = pl.ds(i * step, step)
        copy = pltpu.make_async_copy(
            lam_ref.at[:, :, block], held_ref.at[:, :, block], sems.at[i]
        )
        copy.start()
        copies.append(copy)
    to, frm = square_iotas(ROWS * ROWS)
    swap_ref[...] = one_hot(to == (frm % ROWS) * ROWS + frm // ROWS)
    for copy in copies:
        copy.wait()


def hold(lambda_amps):
    anywhere = pl.BlockSpec(memory_space=pl.ANY)
    return pl.pallas_call(
        hold_kernel,
        in_specs=[anywhere],
        out_specs=[anywhere, pl.BlockSpec(memory_space=pltpu.VMEM)],
        out_shape=[
            jax.ShapeDtypeStruct(lambda_amps.shape, lambda_amps.dtype),
            jax.ShapeDtypeStruct((ROWS * ROWS, ROWS * ROWS), jnp.bfloat16),
        ],
        scratch_shapes=[pltpu.SemaphoreType.DMA((8,))],
        compiler_params=pltpu.CompilerParams(vmem_limit_bytes=VMEM_BYTES),
        cost_estimate=pl.CostEstimate(
            flops=0, bytes_accessed=4 * lambda_amps.size, transcendentals=0
        ),
    )(in_hbm(lambda_amps))


def weights_kernel(
    pair_ref, coupling_ref, gap_ref, place_ref, row_ref, col_ref, w_ref, inverse_ref, full
):
    total = pair_ref.shape[1]
    depth = coupling_ref.shape[0]
    owners, _, pairs = gap_ref.shape
    me, sub = place_ref[0], place_ref[1]
    orbital = lax.broadcasted_iota(jnp.int32, (depth, total), 0)
    coupling = coupling_ref[...]
    product = None
    for side in range(2):
        columns = one_hot(orbital == pair_ref[side : side + 1, :])
        picked = pick_rows(columns, pick_columns(coupling, columns))
        product = picked if product is None else product * picked
    frm, to = square_iotas(total)
    block, within = to // pairs, to % pairs
    source = ((me ^ (block % owners)) * 2 + (sub ^ (block // owners))) * pairs + within
    full[...] = jnp.dot(
        product.astype(jnp.bfloat16), one_hot(frm == source), preferred_element_type=jnp.float32
    )
    row, column = square_iotas(pairs)
    for k in range(owners):
        start = pl.multiple_of(((me ^ k) * 2 + sub) * pairs, pairs)
        rows = pl.ds(k * pairs, pairs)
        w_ref[rows, :] = full[pl.ds(start, pairs), :].astype(jnp.bfloat16)
        gap = jnp.sum(jnp.where(row == column, gap_ref[me ^ k], 0.0), axis=1, keepdims=True)
        for a in range(inverse_ref.shape[0]):
            inverse_ref[a, rows, :] = -1.0 / ((gap + row_ref[a]) + col_ref[...])


def make_weights(pair_list, coupling, pair_gap, place, row_energy, col_energy):
    owners, _, pairs = pair_gap.shape
    total = pair_list.shape[0]
    mine = owners * pairs
    rows, cols = row_energy.shape[0], col_energy.shape[0]
    smem = pl.BlockSpec(memory_space=pltpu.SMEM)
    vmem = pl.BlockSpec(memory_space=pltpu.VMEM)
    return pl.pallas_call(
        weights_kernel,
        in_specs=[vmem, vmem, vmem, smem, smem, vmem],
        out_specs=[vmem, vmem],
        out_shape=[
            jax.ShapeDtypeStruct((mine, total), jnp.bfloat16),
            jax.ShapeDtypeStruct((rows, mine, cols), jnp.float32),
        ],
        scratch_shapes=[pltpu.VMEM((total, total), jnp.float32)],
        compiler_params=pltpu.CompilerParams(vmem_limit_bytes=VMEM_BYTES),
        cost_estimate=pl.CostEstimate(
            flops=12 * total * coupling.size, bytes_accessed=4 * coupling.size, transcendentals=0
        ),
    )(pair_list.T, coupling, pair_gap, place, row_energy, col_energy.reshape(1, cols))


def dress_kernel(owners, rows, groups, place_ref, tile_of_ref, mask_ref, *refs):
    tile_refs, lam_ref = (refs[0], *refs[2:owners], refs[1]), refs[owners]
    swap_ref = refs[owners + 1]
    out_refs = refs[owners + 2 : -2]
    tiles, stage = refs[-2:]
    me = place_ref[0]
    flat = [(k, c, out, j) for out, group in zip(out_refs, groups) for j, (k, c) in enumerate(group)]
    starts = [pl.multiple_of((me ^ k) * rows + c * ROWS, ROWS) for k, c, _, _ in flat]
    tile_rows, cols = lam_ref.shape[3:]
    row = lax.broadcasted_iota(jnp.int32, (ROWS, tile_rows), 0)
    column = lax.broadcasted_iota(jnp.int32, (ROWS, tile_rows), 1)
    for n, start in enumerate(starts):
        block = pl.ds(n * ROWS, ROWS)
        own_row = one_hot(column == row + start)
        for k in range(owners):
            tiles[k, block, :tile_rows] = tile_refs[k][0, pl.ds(start, ROWS), :]
            tiles[k, block, tile_rows:] = own_row
    swap = swap_ref[...]
    parts = mask_ref.shape[2]
    width = cols // parts
    for g in range(lam_ref.shape[2] // ROWS):
        for i in range(ROWS):
            pair = g * ROWS + i
            amps = lam_ref[0, 0, pair]
            kept = [
                amps[:, part * width : (part + 1) * width]
                * mask_ref[0, 0, part, pair].astype(jnp.float32).astype(jnp.bfloat16)
                for part in range(parts)
            ]
            both = jnp.concatenate([jnp.concatenate(kept, axis=1), amps], axis=0)
            full = jnp.dot(
                tiles[tile_of_ref[0, 0, pair] ^ me], both, preferred_element_type=jnp.float32
            ).astype(jnp.bfloat16)
            for n in range(len(flat)):
                stage[g, n, pl.ds(i * ROWS, ROWS), :] = full[n * ROWS : (n + 1) * ROWS]
        for n, (_, _, out, j) in enumerate(flat):
            turned = jnp.dot(swap, stage[g, n], preferred_element_type=jnp.float32)
            out[j, :, pl.ds(g * ROWS, ROWS), :] = turned.astype(jnp.bfloat16).reshape(
                ROWS, ROWS, turned.shape[1]
            )


def dress(groups, place, tile_of, tile_mask, tiles, lambda_amps, swap):
    owners = len(tiles)
    pairs, tile_rows, cols = lambda_amps.shape[2:]
    rows = tile_rows // owners
    smem = pl.BlockSpec(memory_space=pltpu.SMEM)
    vmem = pl.BlockSpec(memory_space=pltpu.VMEM)
    count = sum(len(group) for group in groups)
    return pl.pallas_call(
        functools.partial(dress_kernel, owners, rows, groups),
        in_specs=[smem] * 3 + [vmem] * (owners + 2),
        out_specs=[vmem] * len(groups),
        out_shape=[
            jax.ShapeDtypeStruct((len(group), ROWS, pairs, cols), jnp.bfloat16)
            for group in groups
        ],
        scratch_shapes=[
            pltpu.VMEM((owners, count * ROWS, 2 * tile_rows), jnp.bfloat16),
            pltpu.VMEM((pairs // ROWS, count, ROWS * ROWS, cols), jnp.bfloat16),
        ],
        compiler_params=pltpu.CompilerParams(vmem_limit_bytes=VMEM_BYTES),
        cost_estimate=pl.CostEstimate(
            flops=2 * pairs * count * ROWS * tile_rows * cols,
            bytes_accessed=3 * pairs * tile_rows * cols,
            transcendentals=0,
        ),
    )(
        in_smem(place),
        in_smem(tile_of),
        in_smem(jnp.swapaxes(tile_mask, 2, 3)),
        tiles[0],
        tiles[-1],
        *tiles[1:-1],
        lambda_amps,
        swap,
    )


def finish_blocks(indices, chunk, swap_ref, w_ref, inverse_ref, piece_refs, done, ys, then):
    groups, _, rows, _ = done.shape
    mine = groups * ROWS
    weights = w_ref[...]
    for a in range(rows):
        amps = jnp.concatenate([ref[index, a] for ref, index in zip(piece_refs, indices)], axis=0)
        cycle = jnp.dot(weights, amps, preferred_element_type=jnp.float32)
        total = amps[:mine].astype(jnp.float32) + cycle
        value = (total * inverse_ref[chunk * rows + a]).astype(jnp.bfloat16)
        for g in range(groups):
            ys[g, pl.ds(a * ROWS, ROWS), :] = value[g * ROWS : (g + 1) * ROWS]
    swap = swap_ref[...]
    for g in range(groups):
        turned = jnp.dot(swap, ys[g], preferred_element_type=jnp.float32)
        done[g] = turned.astype(jnp.bfloat16).reshape(done.shape[1:])
        then(g)


def early_kernel(indices, chunk, swap_ref, w_ref, inverse_ref, *refs):
    piece_refs, (done, ys) = refs[:-2], refs[-2:]
    finish_blocks(
        indices, chunk, swap_ref, w_ref, inverse_ref, piece_refs, done, ys, lambda g: None
    )


def last_kernel(indices, chunk, swap_ref, w_ref, inverse_ref, place_ref, *refs):
    ready_refs, piece_refs, (out_ref, done, ys, sems) = refs[:chunk], refs[chunk:-4], refs[-4:]
    groups, _, rows, _ = done.shape
    halves = 2 * groups // len(indices)
    me = place_ref[0]
    leaving = []

    def write(source, c, g):
        k, h = g // halves, g % halves
        copy = pltpu.make_async_copy(
            source.at[g],
            out_ref.at[me ^ k, 0, pl.ds(h * ROWS, ROWS), pl.ds(c * rows, rows), :],
            sems.at[c, g],
        )
        copy.start()
        leaving.append(copy)

    for c, ref in enumerate(ready_refs):
        for g in range(groups):
            write(ref, c, g)
    finish_blocks(
        indices,
        chunk,
        swap_ref,
        w_ref,
        inverse_ref,
        piece_refs,
        done,
        ys,
        lambda g: write(done, chunk, g),
    )
    for copy in leaving:
        copy.wait()


def finish(chunk, swap, weights, inverse, pieces, place=None, ready=(), shape=None):
    _, rows, pairs, cols = pieces[0][0].shape
    groups = len(pieces) // 2 * (pairs // ROWS)
    indices = [index for _, index in pieces]
    vmem, anywhere = pl.BlockSpec(memory_space=pltpu.VMEM), pl.BlockSpec(memory_space=pl.ANY)
    block = (groups, ROWS, rows, cols)
    ys = pltpu.VMEM((groups, ROWS * rows, cols), jnp.bfloat16)
    args, in_specs = [swap, weights, inverse], [vmem] * 3
    if shape is None:
        kernel = functools.partial(early_kernel, indices, chunk)
        out_spec, out_shape = vmem, jax.ShapeDtypeStruct(block, jnp.bfloat16)
        scratch = [ys]
    else:
        kernel = functools.partial(last_kernel, indices, chunk)
        out_spec, out_shape = anywhere, jax.ShapeDtypeStruct(shape, jnp.bfloat16)
        scratch = [pltpu.VMEM(block, jnp.bfloat16), ys]
        scratch += [pltpu.SemaphoreType.DMA((chunk + 1, groups))]
        args += [place, *ready]
        in_specs += [pl.BlockSpec(memory_space=pltpu.SMEM)] + [anywhere] * len(ready)
    return pl.pallas_call(
        kernel,
        in_specs=in_specs + [vmem] * len(pieces),
        out_specs=out_spec,
        out_shape=out_shape,
        scratch_shapes=scratch,
        compiler_params=pltpu.CompilerParams(vmem_limit_bytes=VMEM_BYTES),
        cost_estimate=pl.CostEstimate(flops=0, bytes_accessed=0, transcendentals=0),
    )(*args, *[piece for piece, _ in pieces])


def local_chunked(
    lambda_amps,
    integral_tiles,
    tile_of,
    tile_mask,
    pair_list,
    coupling,
    pair_gap,
    row_energy,
    col_energy,
):
    pairs, tile_rows, cols = lambda_amps.shape[2:]
    owners = lax.axis_size("pair")
    rows = tile_rows // owners
    chunks = rows // ROWS
    me = lax.axis_index("pair").astype(jnp.int32)
    sub = lax.axis_index("sub").astype(jnp.int32)
    place = jnp.stack([me, sub])

    def to_owner(value, k):
        return lax.ppermute(value, "pair", [(o, o ^ k) for o in range(owners)])

    def to_sibling(value):
        return lax.ppermute(value, "sub", [(0, 1), (1, 0)])

    def after(value, earlier):
        return value if earlier is None else lax.optimization_barrier((value, earlier))[0]

    tiles = [integral_tiles] + [to_owner(integral_tiles, k) for k in range(1, owners)]

    far = list(range(2, owners))
    last = far[-1]
    groups = [((k, c),) for c in range(chunks) for k in far[::-1]]
    groups += [tuple((k, c) for c in range(chunks)) for k in (1, 0)]
    held, swap = hold(lambda_amps)
    sent = dict(zip(groups, dress(groups, place, tile_of, tile_mask, tiles, held, swap)))
    weights, inverse = make_weights(
        after(pair_list, sent[groups[0]]), coupling, pair_gap, place, row_energy, col_energy
    )
    own, near = sent[groups[-1]], to_owner(sent[groups[-2]], 1)
    direct, other = {}, {}
    for k in far:
        for c in range(chunks):
            earlier = direct[k, c - 1] if c and k == last else None
            direct[k, c] = to_owner(after(sent[((k, c),)], earlier), k)
    own_passed = to_sibling(after(own, direct[last, 0]))
    near_passed = to_sibling(after(near, (weights, direct[far[0], 0])))
    for k in far:
        for c in range(chunks):
            earlier = other[k, c - 1] if c else None
            other[k, c] = to_sibling(after(direct[k, c], earlier))

    ready = []
    for c in range(chunks):
        pieces = [(own, c), (near, c)] + [(direct[k, c], 0) for k in far]
        pieces += [(own_passed, c), (near_passed, c)] + [(other[k, c], 0) for k in far]
        if c + 1 < chunks:
            ready.append(finish(c, swap, weights, inverse, pieces))
    shape = (owners, 1, pairs, rows, cols)
    return finish(c, swap, weights, inverse, pieces, place, ready, shape)


def solution(mesh):
    placed = (
        P(("mol", "pair"), "sub", None, None, "tile"),
        P(("mol", "pair"), None, None),
        P(("mol", "pair"), "sub", None),
        P(("mol", "pair"), "sub", None, "tile"),
        P("mol", None),
        P("mol", None),
        P("mol", "sub", None),
        P(("mol", "pair")),
        P(("mol", "tile")),
    )
    owners, subs = mesh.shape["pair"], mesh.shape["sub"]

    def local(*args):
        tile_rows, cols = args[0].shape[3:]
        rows = tile_rows // owners
        power = owners >= 4 and owners & (owners - 1) == 0
        fits = rows % ROWS == 0 and cols % LANES == 0 and args[1].shape[0] == 1
        if power and fits and subs == 2 and args[0].shape[2] % ROWS == 0:
            return local_chunked(*args)
        return local_general(*args)

    return jax.shard_map(
        local,
        mesh=mesh,
        in_specs=placed,
        out_specs=P("mol", "sub", None, "pair", "tile"),
        check_vma=False,
    )
```

```python
import functools
import math

import jax
import jax.numpy as jnp
from jax import lax
from jax.experimental import pallas as pl
from jax.experimental.pallas import tpu as pltpu
from jax.sharding import PartitionSpec as P

ROWS = 16
LANES = 128
VMEM_BYTES = 24 * 2**20


def column_tables(coupling, col_pairs):
    left_table = jnp.take(coupling.T, col_pairs[:, 0], axis=0).T
    right_table = jnp.take(coupling.T, col_pairs[:, 1], axis=0).T
    return (left_table, right_table)


def cycle_rows(left_table, right_table, row_pairs):
    left_part = jnp.take(left_table, row_pairs[:, 0], axis=0)
    right_part = jnp.take(right_table, row_pairs[:, 1], axis=0)
    return (left_part * right_part).astype(jnp.bfloat16)


def cycle_all(coupling, pair_list, col_pairs, flat_rhs):
    total_pairs = pair_list.shape[0]
    step_rows = math.gcd(total_pairs, 512)
    row_blocks = pair_list.reshape(total_pairs // step_rows, step_rows, 2)
    left_table, right_table = column_tables(coupling, col_pairs)

    def one_block(row_pairs):
        weights = cycle_rows(left_table, right_table, row_pairs)
        return jnp.dot(weights, flat_rhs, preferred_element_type=jnp.float32)

    return lax.map(one_block, row_blocks).reshape(total_pairs, -1)


def local_general(
    lambda_amps,
    integral_tiles,
    tile_of,
    tile_mask,
    pair_list,
    coupling,
    pair_gap,
    row_energy,
    col_energy,
):
    pair_count = lambda_amps.shape[2]
    tile_rows = lambda_amps.shape[3]
    col_count = lambda_amps.shape[4]
    owners = lax.axis_size("pair")
    sub_count = lax.axis_size("sub")
    wanted = tile_of.reshape(pair_count)
    empty_tiles = jnp.zeros((pair_count, tile_rows, tile_rows), integral_tiles.dtype)
    shard_piece = lax.all_gather(integral_tiles, "pair", axis=0, tiled=True)
    inside = (wanted >= 0) & (wanted < shard_piece.shape[0])
    taken_rows = shard_piece[jnp.clip(wanted, 0, shard_piece.shape[0] - 1)]
    chosen = jnp.where(inside[:, None, None], taken_rows, empty_tiles)
    amplitudes = lambda_amps.reshape(pair_count, tile_rows, col_count)
    ladder = jnp.einsum("pac,pcb->pab", chosen, amplitudes, preferred_element_type=jnp.float32)
    blocks = tile_mask.shape[3]
    keep_mask = tile_mask.reshape(pair_count, 1, blocks, 1).astype(jnp.float32)
    ladder = (
        ladder.reshape(pair_count, tile_rows, blocks, col_count // blocks) * keep_mask
    ).reshape(pair_count, tile_rows, col_count)
    dressed = (amplitudes.astype(jnp.float32) + ladder).astype(jnp.bfloat16)
    dressed = dressed.reshape(1, 1, pair_count, tile_rows, col_count)
    relayed = lax.all_to_all(dressed, "pair", split_axis=3, concat_axis=0, tiled=True)
    sub_index = lax.axis_index("sub")
    block_ids = jnp.arange(owners, dtype=jnp.int32) * sub_count + sub_index
    mine_ids = (
        block_ids[:, None] * pair_count + jnp.arange(pair_count, dtype=jnp.int32)[None, :]
    ).reshape(-1)
    col_pairs = pair_list[mine_ids]
    flat_rhs = relayed.reshape(owners * pair_count, -1)
    partial_value = cycle_all(coupling, pair_list, col_pairs, flat_rhs)
    partial_value = partial_value.reshape(
        owners, sub_count, pair_count, relayed.shape[3], col_count
    )
    cycle_term = lax.psum_scatter(
        partial_value.astype(jnp.bfloat16), "sub", scatter_dimension=1, tiled=True
    ).astype(jnp.float32)
    total_sum = relayed.astype(jnp.float32) + cycle_term
    energy_gap = (
        pair_gap[:, :, :, None, None]
        + row_energy[None, None, None, :, None]
        + col_energy[None, None, None, None, :]
    )
    return (-total_sum / energy_gap).astype(jnp.bfloat16)


def in_hbm(value):
    return pltpu.with_memory_space_constraint(value, pltpu.HBM)


def in_smem(value):
    return pltpu.with_memory_space_constraint(value, pltpu.SMEM)


def one_hot(hits):
    return jnp.where(hits, 1.0, 0.0).astype(jnp.bfloat16)


def square_iotas(size):
    return (lax.broadcasted_iota(jnp.int32, (size, size), axis) for axis in range(2))


def split3(value):
    high = value.astype(jnp.bfloat16)
    rest = value - high.astype(jnp.float32)
    mid = rest.astype(jnp.bfloat16)
    low = (rest - mid.astype(jnp.float32)).astype(jnp.bfloat16)
    return high, mid, low


def pick_columns(value, columns):
    high, mid, low = (
        jnp.dot(part, columns, preferred_element_type=jnp.float32) for part in split3(value)
    )
    return high + (mid + low)


def pick_rows(columns, value):
    dims = (((0,), (0,)), ((), ()))
    high, mid, low = (
        lax.dot_general(columns, part, dims, preferred_element_type=jnp.float32)
        for part in split3(value)
    )
    return high + (mid + low)


def hold_kernel(lam_ref, held_ref, swap_ref, sems):
    step = lam_ref.shape[2] // sems.shape[0]
    copies = []
    for i in range(sems.shape[0]):
        block = pl.ds(i * step, step)
        copy = pltpu.make_async_copy(
            lam_ref.at[:, :, block], held_ref.at[:, :, block], sems.at[i]
        )
        copy.start()
        copies.append(copy)
    to, frm = square_iotas(ROWS * ROWS)
    swap_ref[...] = one_hot(to == (frm % ROWS) * ROWS + frm // ROWS)
    for copy in copies:
        copy.wait()


def hold(lambda_amps):
    anywhere = pl.BlockSpec(memory_space=pl.ANY)
    return pl.pallas_call(
        hold_kernel,
        in_specs=[anywhere],
        out_specs=[anywhere, pl.BlockSpec(memory_space=pltpu.VMEM)],
        out_shape=[
            jax.ShapeDtypeStruct(lambda_amps.shape, lambda_amps.dtype),
            jax.ShapeDtypeStruct((ROWS * ROWS, ROWS * ROWS), jnp.bfloat16),
        ],
        scratch_shapes=[pltpu.SemaphoreType.DMA((8,))],
        compiler_params=pltpu.CompilerParams(vmem_limit_bytes=VMEM_BYTES),
        cost_estimate=pl.CostEstimate(
            flops=0, bytes_accessed=4 * lambda_amps.size, transcendentals=0
        ),
    )(in_hbm(lambda_amps))


def weights_kernel(
    pair_ref, coupling_ref, gap_ref, place_ref, row_ref, col_ref, w_ref, inverse_ref, full
):
    total = pair_ref.shape[1]
    depth = coupling_ref.shape[0]
    owners, _, pairs = gap_ref.shape
    me, sub = place_ref[0], place_ref[1]
    orbital = lax.broadcasted_iota(jnp.int32, (depth, total), 0)
    coupling = coupling_ref[...]
    product = None
    for side in range(2):
        columns = one_hot(orbital == pair_ref[side : side + 1, :])
        picked = pick_rows(columns, pick_columns(coupling, columns))
        product = picked if product is None else product * picked
    frm, to = square_iotas(total)
    block, within = to // pairs, to % pairs
    source = ((me ^ (block % owners)) * 2 + (sub ^ (block // owners))) * pairs + within
    full[...] = jnp.dot(
        product.astype(jnp.bfloat16), one_hot(frm == source), preferred_element_type=jnp.float32
    )
    row, column = square_iotas(pairs)
    for k in range(owners):
        start = pl.multiple_of(((me ^ k) * 2 + sub) * pairs, pairs)
        rows = pl.ds(k * pairs, pairs)
        w_ref[rows, :] = full[pl.ds(start, pairs), :].astype(jnp.bfloat16)
        gap = jnp.sum(jnp.where(row == column, gap_ref[me ^ k], 0.0), axis=1, keepdims=True)
        for a in range(inverse_ref.shape[0]):
            inverse_ref[a, rows, :] = -1.0 / ((gap + row_ref[a]) + col_ref[...])


def make_weights(pair_list, coupling, pair_gap, place, row_energy, col_energy):
    owners, _, pairs = pair_gap.shape
    total = pair_list.shape[0]
    mine = owners * pairs
    rows, cols = row_energy.shape[0], col_energy.shape[0]
    smem = pl.BlockSpec(memory_space=pltpu.SMEM)
    vmem = pl.BlockSpec(memory_space=pltpu.VMEM)
    return pl.pallas_call(
        weights_kernel,
        in_specs=[vmem, vmem, vmem, smem, smem, vmem],
        out_specs=[vmem, vmem],
        out_shape=[
            jax.ShapeDtypeStruct((mine, total), jnp.bfloat16),
            jax.ShapeDtypeStruct((rows, mine, cols), jnp.float32),
        ],
        scratch_shapes=[pltpu.VMEM((total, total), jnp.float32)],
        compiler_params=pltpu.CompilerParams(vmem_limit_bytes=VMEM_BYTES),
        cost_estimate=pl.CostEstimate(
            flops=12 * total * coupling.size, bytes_accessed=4 * coupling.size, transcendentals=0
        ),
    )(pair_list.T, coupling, pair_gap, place, row_energy, col_energy.reshape(1, cols))


def dress_kernel(owners, rows, groups, place_ref, tile_of_ref, mask_ref, *refs):
    tile_refs, lam_ref = (refs[0], refs[owners - 1], *refs[1 : owners - 1]), refs[owners]
    swap_ref = refs[owners + 1]
    out_refs = refs[owners + 2 : -2]
    tiles, stage = refs[-2:]
    me = place_ref[0]
    flat = [(k, c, out, j) for out, group in zip(out_refs, groups) for j, (k, c) in enumerate(group)]
    starts = [pl.multiple_of((me ^ k) * rows + c * ROWS, ROWS) for k, c, _, _ in flat]
    tile_rows, cols = lam_ref.shape[3:]
    row = lax.broadcasted_iota(jnp.int32, (ROWS, tile_rows), 0)
    column = lax.broadcasted_iota(jnp.int32, (ROWS, tile_rows), 1)
    for n, start in enumerate(starts):
        block = pl.ds(n * ROWS, ROWS)
        own_row = one_hot(column == row + start)
        for k in range(owners):
            tiles[k, block, :tile_rows] = tile_refs[k][0, pl.ds(start, ROWS), :]
            tiles[k, block, tile_rows:] = own_row
    swap = swap_ref[...]
    parts = mask_ref.shape[2]
    width = cols // parts
    for g in range(lam_ref.shape[2] // ROWS):
        for i in range(ROWS):
            pair = g * ROWS + i
            amps = lam_ref[0, 0, pair]
            kept = [
                amps[:, part * width : (part + 1) * width]
                * mask_ref[0, 0, part, pair].astype(jnp.float32).astype(jnp.bfloat16)
                for part in range(parts)
            ]
            both = jnp.concatenate([jnp.concatenate(kept, axis=1), amps], axis=0)
            full = jnp.dot(
                tiles[tile_of_ref[0, 0, pair] ^ me], both, preferred_element_type=jnp.float32
            ).astype(jnp.bfloat16)
            for n in range(len(flat)):
                stage[g, n, pl.ds(i * ROWS, ROWS), :] = full[n * ROWS : (n + 1) * ROWS]
        for n, (_, _, out, j) in enumerate(flat):
            turned = jnp.dot(swap, stage[g, n], preferred_element_type=jnp.float32)
            out[j, :, pl.ds(g * ROWS, ROWS), :] = turned.astype(jnp.bfloat16).reshape(
                ROWS, ROWS, turned.shape[1]
            )


def dress(groups, place, tile_of, tile_mask, tiles, lambda_amps, swap):
    owners = len(tiles)
    pairs, tile_rows, cols = lambda_amps.shape[2:]
    rows = tile_rows // owners
    smem = pl.BlockSpec(memory_space=pltpu.SMEM)
    vmem = pl.BlockSpec(memory_space=pltpu.VMEM)
    count = sum(len(group) for group in groups)
    return pl.pallas_call(
        functools.partial(dress_kernel, owners, rows, groups),
        in_specs=[smem] * 3 + [vmem] * (owners + 2),
        out_specs=[vmem] * len(groups),
        out_shape=[
            jax.ShapeDtypeStruct((len(group), ROWS, pairs, cols), jnp.bfloat16)
            for group in groups
        ],
        scratch_shapes=[
            pltpu.VMEM((owners, count * ROWS, 2 * tile_rows), jnp.bfloat16),
            pltpu.VMEM((pairs // ROWS, count, ROWS * ROWS, cols), jnp.bfloat16),
        ],
        compiler_params=pltpu.CompilerParams(vmem_limit_bytes=VMEM_BYTES),
        cost_estimate=pl.CostEstimate(
            flops=2 * pairs * count * ROWS * tile_rows * cols,
            bytes_accessed=3 * pairs * tile_rows * cols,
            transcendentals=0,
        ),
    )(
        in_smem(place),
        in_smem(tile_of),
        in_smem(jnp.swapaxes(tile_mask, 2, 3)),
        tiles[0],
        *tiles[2:],
        tiles[1],
        lambda_amps,
        swap,
    )


def finish_blocks(indices, chunk, swap_ref, w_ref, inverse_ref, piece_refs, done, ys, then):
    groups, _, rows, _ = done.shape
    mine = groups * ROWS
    weights = w_ref[...]
    for a in range(rows):
        amps = jnp.concatenate([ref[index, a] for ref, index in zip(piece_refs, indices)], axis=0)
        cycle = jnp.dot(weights, amps, preferred_element_type=jnp.float32)
        total = amps[:mine].astype(jnp.float32) + cycle
        value = (total * inverse_ref[chunk * rows + a]).astype(jnp.bfloat16)
        for g in range(groups):
            ys[g, pl.ds(a * ROWS, ROWS), :] = value[g * ROWS : (g + 1) * ROWS]
    swap = swap_ref[...]
    for g in range(groups):
        turned = jnp.dot(swap, ys[g], preferred_element_type=jnp.float32)
        done[g] = turned.astype(jnp.bfloat16).reshape(done.shape[1:])
        then(g)


def early_kernel(indices, chunk, swap_ref, w_ref, inverse_ref, *refs):
    piece_refs, (done, ys) = refs[:-2], refs[-2:]
    finish_blocks(
        indices, chunk, swap_ref, w_ref, inverse_ref, piece_refs, done, ys, lambda g: None
    )


def last_kernel(indices, chunk, swap_ref, w_ref, inverse_ref, place_ref, *refs):
    ready_refs, piece_refs, (out_ref, done, ys, sems) = refs[:chunk], refs[chunk:-4], refs[-4:]
    groups, _, rows, _ = done.shape
    halves = 2 * groups // len(indices)
    me = place_ref[0]
    leaving = []

    def write(source, c, g):
        k, h = g // halves, g % halves
        copy = pltpu.make_async_copy(
            source.at[g],
            out_ref.at[me ^ k, 0, pl.ds(h * ROWS, ROWS), pl.ds(c * rows, rows), :],
            sems.at[c, g],
        )
        copy.start()
        leaving.append(copy)

    for c, ref in enumerate(ready_refs):
        for g in range(groups):
            write(ref, c, g)
    finish_blocks(
        indices,
        chunk,
        swap_ref,
        w_ref,
        inverse_ref,
        piece_refs,
        done,
        ys,
        lambda g: write(done, chunk, g),
    )
    for copy in leaving:
        copy.wait()


def finish(chunk, swap, weights, inverse, pieces, place=None, ready=(), shape=None):
    _, rows, pairs, cols = pieces[0][0].shape
    groups = len(pieces) // 2 * (pairs // ROWS)
    indices = [index for _, index in pieces]
    vmem, anywhere = pl.BlockSpec(memory_space=pltpu.VMEM), pl.BlockSpec(memory_space=pl.ANY)
    block = (groups, ROWS, rows, cols)
    ys = pltpu.VMEM((groups, ROWS * rows, cols), jnp.bfloat16)
    args, in_specs = [swap, weights, inverse], [vmem] * 3
    if shape is None:
        kernel = functools.partial(early_kernel, indices, chunk)
        out_spec, out_shape = vmem, jax.ShapeDtypeStruct(block, jnp.bfloat16)
        scratch = [ys]
    else:
        kernel = functools.partial(last_kernel, indices, chunk)
        out_spec, out_shape = anywhere, jax.ShapeDtypeStruct(shape, jnp.bfloat16)
        scratch = [pltpu.VMEM(block, jnp.bfloat16), ys]
        scratch += [pltpu.SemaphoreType.DMA((chunk + 1, groups))]
        args += [place, *ready]
        in_specs += [pl.BlockSpec(memory_space=pltpu.SMEM)] + [anywhere] * len(ready)
    return pl.pallas_call(
        kernel,
        in_specs=in_specs + [vmem] * len(pieces),
        out_specs=out_spec,
        out_shape=out_shape,
        scratch_shapes=scratch,
        compiler_params=pltpu.CompilerParams(vmem_limit_bytes=VMEM_BYTES),
        cost_estimate=pl.CostEstimate(flops=0, bytes_accessed=0, transcendentals=0),
    )(*args, *[piece for piece, _ in pieces])


def local_chunked(
    lambda_amps,
    integral_tiles,
    tile_of,
    tile_mask,
    pair_list,
    coupling,
    pair_gap,
    row_energy,
    col_energy,
):
    pairs, tile_rows, cols = lambda_amps.shape[2:]
    owners = lax.axis_size("pair")
    rows = tile_rows // owners
    chunks = rows // ROWS
    me = lax.axis_index("pair").astype(jnp.int32)
    sub = lax.axis_index("sub").astype(jnp.int32)
    place = jnp.stack([me, sub])

    def to_owner(value, k):
        return lax.ppermute(value, "pair", [(o, o ^ k) for o in range(owners)])

    def to_sibling(value):
        return lax.ppermute(value, "sub", [(0, 1), (1, 0)])

    def after(value, earlier):
        return value if earlier is None else lax.optimization_barrier((value, earlier))[0]

    tiles = [integral_tiles] + [to_owner(integral_tiles, k) for k in range(1, owners)]

    far = list(range(2, owners))
    last = far[-1]
    groups = [((k, c),) for c in range(chunks) for k in far[::-1]]
    groups += [tuple((k, c) for c in range(chunks)) for k in (1, 0)]
    held, swap = hold(lambda_amps)
    sent = dict(zip(groups, dress(groups, place, tile_of, tile_mask, tiles, held, swap)))
    weights, inverse = make_weights(
        after(pair_list, sent[groups[0]]), coupling, pair_gap, place, row_energy, col_energy
    )
    own, near = sent[groups[-1]], to_owner(sent[groups[-2]], 1)
    direct, other = {}, {}
    for k in far:
        for c in range(chunks):
            earlier = direct[k, c - 1] if c and k == last else None
            direct[k, c] = to_owner(after(sent[((k, c),)], earlier), k)
    own_passed = to_sibling(after(own, direct[last, 0]))
    near_passed = to_sibling(after(near, (weights, direct[far[0], 0])))
    for k in far:
        for c in range(chunks):
            earlier = other[k, c - 1] if c else None
            other[k, c] = to_sibling(after(direct[k, c], earlier))

    ready = []
    for c in range(chunks):
        pieces = [(own, c), (near, c)] + [(direct[k, c], 0) for k in far]
        pieces += [(own_passed, c), (near_passed, c)] + [(other[k, c], 0) for k in far]
        if c + 1 < chunks:
            ready.append(finish(c, swap, weights, inverse, pieces))
    shape = (owners, 1, pairs, rows, cols)
    return finish(c, swap, weights, inverse, pieces, place, ready, shape)


def solution(mesh):
    placed = (
        P(("mol", "pair"), "sub", None, None, "tile"),
        P(("mol", "pair"), None, None),
        P(("mol", "pair"), "sub", None),
        P(("mol", "pair"), "sub", None, "tile"),
        P("mol", None),
        P("mol", None),
        P("mol", "sub", None),
        P(("mol", "pair")),
        P(("mol", "tile")),
    )
    owners, subs = mesh.shape["pair"], mesh.shape["sub"]

    def local(*args):
        tile_rows, cols = args[0].shape[3:]
        rows = tile_rows // owners
        power = owners >= 4 and owners & (owners - 1) == 0
        fits = rows % ROWS == 0 and cols % LANES == 0 and args[1].shape[0] == 1
        if power and fits and subs == 2 and args[0].shape[2] % ROWS == 0:
            return local_chunked(*args)
        return local_general(*args)

    return jax.shard_map(
        local,
        mesh=mesh,
        in_specs=placed,
        out_specs=P("mol", "sub", None, "pair", "tile"),
        check_vma=False,
    )
```

```python
import functools
import math

import jax
import jax.numpy as jnp
from jax import lax
from jax.experimental import pallas as pl
from jax.experimental.pallas import tpu as pltpu
from jax.sharding import PartitionSpec as P

ROWS = 16
LANES = 128
VMEM_BYTES = 24 * 2**20


def column_tables(coupling, col_pairs):
    left_table = jnp.take(coupling.T, col_pairs[:, 0], axis=0).T
    right_table = jnp.take(coupling.T, col_pairs[:, 1], axis=0).T
    return (left_table, right_table)


def cycle_rows(left_table, right_table, row_pairs):
    left_part = jnp.take(left_table, row_pairs[:, 0], axis=0)
    right_part = jnp.take(right_table, row_pairs[:, 1], axis=0)
    return (left_part * right_part).astype(jnp.bfloat16)


def cycle_all(coupling, pair_list, col_pairs, flat_rhs):
    total_pairs = pair_list.shape[0]
    step_rows = math.gcd(total_pairs, 512)
    row_blocks = pair_list.reshape(total_pairs // step_rows, step_rows, 2)
    left_table, right_table = column_tables(coupling, col_pairs)

    def one_block(row_pairs):
        weights = cycle_rows(left_table, right_table, row_pairs)
        return jnp.dot(weights, flat_rhs, preferred_element_type=jnp.float32)

    return lax.map(one_block, row_blocks).reshape(total_pairs, -1)


def local_general(
    lambda_amps,
    integral_tiles,
    tile_of,
    tile_mask,
    pair_list,
    coupling,
    pair_gap,
    row_energy,
    col_energy,
):
    pair_count = lambda_amps.shape[2]
    tile_rows = lambda_amps.shape[3]
    col_count = lambda_amps.shape[4]
    owners = lax.axis_size("pair")
    sub_count = lax.axis_size("sub")
    wanted = tile_of.reshape(pair_count)
    empty_tiles = jnp.zeros((pair_count, tile_rows, tile_rows), integral_tiles.dtype)
    shard_piece = lax.all_gather(integral_tiles, "pair", axis=0, tiled=True)
    inside = (wanted >= 0) & (wanted < shard_piece.shape[0])
    taken_rows = shard_piece[jnp.clip(wanted, 0, shard_piece.shape[0] - 1)]
    chosen = jnp.where(inside[:, None, None], taken_rows, empty_tiles)
    amplitudes = lambda_amps.reshape(pair_count, tile_rows, col_count)
    ladder = jnp.einsum("pac,pcb->pab", chosen, amplitudes, preferred_element_type=jnp.float32)
    blocks = tile_mask.shape[3]
    keep_mask = tile_mask.reshape(pair_count, 1, blocks, 1).astype(jnp.float32)
    ladder = (
        ladder.reshape(pair_count, tile_rows, blocks, col_count // blocks) * keep_mask
    ).reshape(pair_count, tile_rows, col_count)
    dressed = (amplitudes.astype(jnp.float32) + ladder).astype(jnp.bfloat16)
    dressed = dressed.reshape(1, 1, pair_count, tile_rows, col_count)
    relayed = lax.all_to_all(dressed, "pair", split_axis=3, concat_axis=0, tiled=True)
    sub_index = lax.axis_index("sub")
    block_ids = jnp.arange(owners, dtype=jnp.int32) * sub_count + sub_index
    mine_ids = (
        block_ids[:, None] * pair_count + jnp.arange(pair_count, dtype=jnp.int32)[None, :]
    ).reshape(-1)
    col_pairs = pair_list[mine_ids]
    flat_rhs = relayed.reshape(owners * pair_count, -1)
    partial_value = cycle_all(coupling, pair_list, col_pairs, flat_rhs)
    partial_value = partial_value.reshape(
        owners, sub_count, pair_count, relayed.shape[3], col_count
    )
    cycle_term = lax.psum_scatter(
        partial_value.astype(jnp.bfloat16), "sub", scatter_dimension=1, tiled=True
    ).astype(jnp.float32)
    total_sum = relayed.astype(jnp.float32) + cycle_term
    energy_gap = (
        pair_gap[:, :, :, None, None]
        + row_energy[None, None, None, :, None]
        + col_energy[None, None, None, None, :]
    )
    return (-total_sum / energy_gap).astype(jnp.bfloat16)


def in_hbm(value):
    return pltpu.with_memory_space_constraint(value, pltpu.HBM)


def in_smem(value):
    return pltpu.with_memory_space_constraint(value, pltpu.SMEM)


def one_hot(hits):
    return jnp.where(hits, 1.0, 0.0).astype(jnp.bfloat16)


def square_iotas(size):
    return (lax.broadcasted_iota(jnp.int32, (size, size), axis) for axis in range(2))


def split3(value):
    high = value.astype(jnp.bfloat16)
    rest = value - high.astype(jnp.float32)
    mid = rest.astype(jnp.bfloat16)
    low = (rest - mid.astype(jnp.float32)).astype(jnp.bfloat16)
    return high, mid, low


def pick_columns(value, columns):
    high, mid, low = (
        jnp.dot(part, columns, preferred_element_type=jnp.float32) for part in split3(value)
    )
    return high + (mid + low)


def pick_rows(columns, value):
    dims = (((0,), (0,)), ((), ()))
    high, mid, low = (
        lax.dot_general(columns, part, dims, preferred_element_type=jnp.float32)
        for part in split3(value)
    )
    return high + (mid + low)


def hold_kernel(lam_ref, held_ref, swap_ref, sems):
    step = lam_ref.shape[2] // sems.shape[0]
    copies = []
    for i in range(sems.shape[0]):
        block = pl.ds(i * step, step)
        copy = pltpu.make_async_copy(
            lam_ref.at[:, :, block], held_ref.at[:, :, block], sems.at[i]
        )
        copy.start()
        copies.append(copy)
    to, frm = square_iotas(ROWS * ROWS)
    swap_ref[...] = one_hot(to == (frm % ROWS) * ROWS + frm // ROWS)
    for copy in copies:
        copy.wait()


def hold(lambda_amps):
    anywhere = pl.BlockSpec(memory_space=pl.ANY)
    return pl.pallas_call(
        hold_kernel,
        in_specs=[anywhere],
        out_specs=[anywhere, pl.BlockSpec(memory_space=pltpu.VMEM)],
        out_shape=[
            jax.ShapeDtypeStruct(lambda_amps.shape, lambda_amps.dtype),
            jax.ShapeDtypeStruct((ROWS * ROWS, ROWS * ROWS), jnp.bfloat16),
        ],
        scratch_shapes=[pltpu.SemaphoreType.DMA((8,))],
        compiler_params=pltpu.CompilerParams(vmem_limit_bytes=VMEM_BYTES),
        cost_estimate=pl.CostEstimate(
            flops=0, bytes_accessed=4 * lambda_amps.size, transcendentals=0
        ),
    )(in_hbm(lambda_amps))


def weights_kernel(
    pair_ref, coupling_ref, gap_ref, place_ref, row_ref, col_ref, w_ref, inverse_ref, full
):
    total = pair_ref.shape[1]
    depth = coupling_ref.shape[0]
    owners, _, pairs = gap_ref.shape
    me, sub = place_ref[0], place_ref[1]
    orbital = lax.broadcasted_iota(jnp.int32, (depth, total), 0)
    coupling = coupling_ref[...]
    product = None
    for side in range(2):
        columns = one_hot(orbital == pair_ref[side : side + 1, :])
        picked = pick_rows(columns, pick_columns(coupling, columns))
        product = picked if product is None else product * picked
    frm, to = square_iotas(total)
    block, within = to // pairs, to % pairs
    source = ((me ^ (block % owners)) * 2 + (sub ^ (block // owners))) * pairs + within
    full[...] = jnp.dot(
        product.astype(jnp.bfloat16), one_hot(frm == source), preferred_element_type=jnp.float32
    )
    row, column = square_iotas(pairs)
    for k in range(owners):
        start = pl.multiple_of(((me ^ k) * 2 + sub) * pairs, pairs)
        rows = pl.ds(k * pairs, pairs)
        w_ref[rows, :] = full[pl.ds(start, pairs), :].astype(jnp.bfloat16)
        gap = jnp.sum(jnp.where(row == column, gap_ref[me ^ k], 0.0), axis=1, keepdims=True)
        for a in range(inverse_ref.shape[0]):
            inverse_ref[a, rows, :] = -1.0 / ((gap + row_ref[a]) + col_ref[...])


def make_weights(pair_list, coupling, pair_gap, place, row_energy, col_energy):
    owners, _, pairs = pair_gap.shape
    total = pair_list.shape[0]
    mine = owners * pairs
    rows, cols = row_energy.shape[0], col_energy.shape[0]
    smem = pl.BlockSpec(memory_space=pltpu.SMEM)
    vmem = pl.BlockSpec(memory_space=pltpu.VMEM)
    return pl.pallas_call(
        weights_kernel,
        in_specs=[vmem, vmem, vmem, smem, smem, vmem],
        out_specs=[vmem, vmem],
        out_shape=[
            jax.ShapeDtypeStruct((mine, total), jnp.bfloat16),
            jax.ShapeDtypeStruct((rows, mine, cols), jnp.float32),
        ],
        scratch_shapes=[pltpu.VMEM((total, total), jnp.float32)],
        compiler_params=pltpu.CompilerParams(vmem_limit_bytes=VMEM_BYTES),
        cost_estimate=pl.CostEstimate(
            flops=12 * total * coupling.size, bytes_accessed=4 * coupling.size, transcendentals=0
        ),
    )(pair_list.T, coupling, pair_gap, place, row_energy, col_energy.reshape(1, cols))


def dress_kernel(owners, rows, groups, place_ref, tile_of_ref, mask_ref, *refs):
    tile_refs, lam_ref = (refs[0], refs[owners - 1], *refs[1 : owners - 1]), refs[owners]
    swap_ref = refs[owners + 1]
    out_refs = refs[owners + 2 : -2]
    tiles, stage = refs[-2:]
    me = place_ref[0]
    flat = [(k, c, out, j) for out, group in zip(out_refs, groups) for j, (k, c) in enumerate(group)]
    starts = [pl.multiple_of((me ^ k) * rows + c * ROWS, ROWS) for k, c, _, _ in flat]
    tile_rows, cols = lam_ref.shape[3:]
    row = lax.broadcasted_iota(jnp.int32, (ROWS, tile_rows), 0)
    column = lax.broadcasted_iota(jnp.int32, (ROWS, tile_rows), 1)
    for n, start in enumerate(starts):
        block = pl.ds(n * ROWS, ROWS)
        own_row = one_hot(column == row + start)
        for k in range(owners):
            tiles[k, block, :tile_rows] = tile_refs[k][0, pl.ds(start, ROWS), :]
            tiles[k, block, tile_rows:] = own_row
    swap = swap_ref[...]
    parts = mask_ref.shape[2]
    width = cols // parts
    for g in range(lam_ref.shape[2] // ROWS):
        for i in range(ROWS):
            pair = g * ROWS + i
            amps = lam_ref[0, 0, pair]
            kept = [
                amps[:, part * width : (part + 1) * width]
                * mask_ref[0, 0, part, pair].astype(jnp.float32).astype(jnp.bfloat16)
                for part in range(parts)
            ]
            both = jnp.concatenate([jnp.concatenate(kept, axis=1), amps], axis=0)
            full = jnp.dot(
                tiles[tile_of_ref[0, 0, pair] ^ me], both, preferred_element_type=jnp.float32
            ).astype(jnp.bfloat16)
            for n in range(len(flat)):
                stage[g, n, pl.ds(i * ROWS, ROWS), :] = full[n * ROWS : (n + 1) * ROWS]
        for n, (_, _, out, j) in enumerate(flat):
            turned = jnp.dot(swap, stage[g, n], preferred_element_type=jnp.float32)
            out[j, :, pl.ds(g * ROWS, ROWS), :] = turned.astype(jnp.bfloat16).reshape(
                ROWS, ROWS, turned.shape[1]
            )


def dress(groups, place, tile_of, tile_mask, tiles, lambda_amps, swap):
    owners = len(tiles)
    pairs, tile_rows, cols = lambda_amps.shape[2:]
    rows = tile_rows // owners
    smem = pl.BlockSpec(memory_space=pltpu.SMEM)
    vmem = pl.BlockSpec(memory_space=pltpu.VMEM)
    count = sum(len(group) for group in groups)
    return pl.pallas_call(
        functools.partial(dress_kernel, owners, rows, groups),
        in_specs=[smem] * 3 + [vmem] * (owners + 2),
        out_specs=[vmem] * len(groups),
        out_shape=[
            jax.ShapeDtypeStruct((len(group), ROWS, pairs, cols), jnp.bfloat16)
            for group in groups
        ],
        scratch_shapes=[
            pltpu.VMEM((owners, count * ROWS, 2 * tile_rows), jnp.bfloat16),
            pltpu.VMEM((pairs // ROWS, count, ROWS * ROWS, cols), jnp.bfloat16),
        ],
        compiler_params=pltpu.CompilerParams(vmem_limit_bytes=VMEM_BYTES),
        cost_estimate=pl.CostEstimate(
            flops=2 * pairs * count * ROWS * tile_rows * cols,
            bytes_accessed=3 * pairs * tile_rows * cols,
            transcendentals=0,
        ),
    )(
        in_smem(place),
        in_smem(tile_of),
        in_smem(jnp.swapaxes(tile_mask, 2, 3)),
        tiles[0],
        *tiles[2:],
        tiles[1],
        lambda_amps,
        swap,
    )


def finish_kernel(indices, chunk, kept, last, swap_ref, w_ref, inverse_ref, place_ref, *refs):
    pieces = len(indices)
    piece_refs, refs = refs[:pieces], refs[pieces:]
    ready_refs, refs = (refs[:chunk], refs[chunk:]) if last else ((), refs)
    out_ref, *left_ref, done, ys, sems = refs[1 if chunk else 0 :]
    groups, _, rows, _ = done.shape
    halves = 2 * groups // pieces
    mine = groups * ROWS
    me = place_ref[0]
    leaving = []

    def write(source, c, g, at):
        k, h = g // halves, g % halves
        copy = pltpu.make_async_copy(
            source.at[at],
            out_ref.at[me ^ k, 0, pl.ds(h * ROWS, ROWS), pl.ds(c * rows, rows), :],
            sems.at[c, g],
        )
        copy.start()
        leaving.append(copy)

    for c, ref in enumerate(ready_refs):
        for at in range(kept):
            write(ref, c, groups - kept + at, at)
    weights = w_ref[...]
    for a in range(rows):
        amps = jnp.concatenate([ref[index, a] for ref, index in zip(piece_refs, indices)], axis=0)
        cycle = jnp.dot(weights, amps, preferred_element_type=jnp.float32)
        total = amps[:mine].astype(jnp.float32) + cycle
        value = (total * inverse_ref[chunk * rows + a]).astype(jnp.bfloat16)
        for g in range(groups):
            ys[g, pl.ds(a * ROWS, ROWS), :] = value[g * ROWS : (g + 1) * ROWS]
    swap = swap_ref[...]
    for g in range(groups):
        turned = jnp.dot(swap, ys[g], preferred_element_type=jnp.float32)
        turned = turned.astype(jnp.bfloat16).reshape(done.shape[1:])
        if last or g < groups - kept:
            done[g] = turned
            write(done, chunk, g, g)
        else:
            left_ref[0][g - (groups - kept)] = turned
    for copy in leaving:
        copy.wait()


def finish(chunk, place, swap, weights, inverse, pieces, before, ready, shape):
    _, rows, pairs, cols = pieces[0][0].shape
    groups = len(pieces) // 2 * (pairs // ROWS)
    kept = groups // 2
    last = chunk + 1 == shape[3] // rows
    vmem, anywhere = pl.BlockSpec(memory_space=pltpu.VMEM), pl.BlockSpec(memory_space=pl.ANY)
    args = [swap, weights, inverse, place, *[piece for piece, _ in pieces]]
    in_specs = [vmem] * 3 + [pl.BlockSpec(memory_space=pltpu.SMEM)] + [vmem] * len(pieces)
    if last:
        args += ready
        in_specs += [anywhere] * len(ready)
    aliases = {}
    if before is not None:
        aliases = {len(args): 0}
        args.append(before)
        in_specs.append(anywhere)
    out_specs, out_shape = [anywhere], [jax.ShapeDtypeStruct(shape, jnp.bfloat16)]
    if not last:
        out_specs.append(vmem)
        out_shape.append(jax.ShapeDtypeStruct((kept, ROWS, rows, cols), jnp.bfloat16))
    return pl.pallas_call(
        functools.partial(finish_kernel, [index for _, index in pieces], chunk, kept, last),
        in_specs=in_specs,
        out_specs=out_specs,
        out_shape=out_shape,
        scratch_shapes=[
            pltpu.VMEM((groups, ROWS, rows, cols), jnp.bfloat16),
            pltpu.VMEM((groups, ROWS * rows, cols), jnp.bfloat16),
            pltpu.SemaphoreType.DMA((chunk + 1, groups)),
        ],
        input_output_aliases=aliases,
        compiler_params=pltpu.CompilerParams(vmem_limit_bytes=VMEM_BYTES),
        cost_estimate=pl.CostEstimate(flops=0, bytes_accessed=0, transcendentals=0),
    )(*args)


def local_chunked(
    lambda_amps,
    integral_tiles,
    tile_of,
    tile_mask,
    pair_list,
    coupling,
    pair_gap,
    row_energy,
    col_energy,
):
    pairs, tile_rows, cols = lambda_amps.shape[2:]
    owners = lax.axis_size("pair")
    rows = tile_rows // owners
    chunks = rows // ROWS
    me = lax.axis_index("pair").astype(jnp.int32)
    sub = lax.axis_index("sub").astype(jnp.int32)
    place = jnp.stack([me, sub])

    def to_owner(value, k):
        return lax.ppermute(value, "pair", [(o, o ^ k) for o in range(owners)])

    def to_sibling(value):
        return lax.ppermute(value, "sub", [(0, 1), (1, 0)])

    def after(value, earlier):
        return value if earlier is None else lax.optimization_barrier((value, earlier))[0]

    tiles = [integral_tiles] + [to_owner(integral_tiles, k) for k in range(1, owners)]

    far = list(range(2, owners))
    last = far[-1]
    groups = [((k, c),) for c in range(chunks) for k in far[::-1]]
    groups += [tuple((k, c) for c in range(chunks)) for k in (1, 0)]
    held, swap = hold(lambda_amps)
    sent = dict(zip(groups, dress(groups, place, tile_of, tile_mask, tiles, held, swap)))
    weights, inverse = make_weights(
        after(pair_list, sent[groups[0]]), coupling, pair_gap, place, row_energy, col_energy
    )
    own, near = sent[groups[-1]], to_owner(sent[groups[-2]], 1)
    direct, other = {}, {}
    for k in far:
        for c in range(chunks):
            earlier = direct[k, c - 1] if c and k == last else None
            direct[k, c] = to_owner(after(sent[((k, c),)], earlier), k)
    own_passed = to_sibling(after(own, weights))
    near_passed = to_sibling(after(near, (weights, direct[far[0], 0])))
    for k in far:
        for c in range(chunks):
            earlier = None
            if k == last:
                earlier = other[far[0], c - 1] if c else weights
            other[k, c] = to_sibling(after(direct[k, c], earlier))

    result, ready = None, []
    for c in range(chunks):
        pieces = [(own, c), (near, c)] + [(direct[k, c], 0) for k in far]
        pieces += [(own_passed, c), (near_passed, c)] + [(other[k, c], 0) for k in far]
        shape = (owners, 1, pairs, rows, cols)
        result, *left = finish(c, place, swap, weights, inverse, pieces, result, ready, shape)
        ready += left
    return result


def solution(mesh):
    placed = (
        P(("mol", "pair"), "sub", None, None, "tile"),
        P(("mol", "pair"), None, None),
        P(("mol", "pair"), "sub", None),
        P(("mol", "pair"), "sub", None, "tile"),
        P("mol", None),
        P("mol", None),
        P("mol", "sub", None),
        P(("mol", "pair")),
        P(("mol", "tile")),
    )
    owners, subs = mesh.shape["pair"], mesh.shape["sub"]

    def local(*args):
        tile_rows, cols = args[0].shape[3:]
        rows = tile_rows // owners
        power = owners >= 4 and owners & (owners - 1) == 0
        fits = rows % ROWS == 0 and cols % LANES == 0 and args[1].shape[0] == 1
        if power and fits and subs == 2 and args[0].shape[2] % ROWS == 0:
            return local_chunked(*args)
        return local_general(*args)

    return jax.shard_map(
        local,
        mesh=mesh,
        in_specs=placed,
        out_specs=P("mol", "sub", None, "pair", "tile"),
        check_vma=False,
    )
```

```python
import functools
import math

import jax
import jax.numpy as jnp
from jax import lax
from jax.experimental import pallas as pl
from jax.experimental.pallas import tpu as pltpu
from jax.sharding import PartitionSpec as P

ROWS = 16
LANES = 128
VMEM_BYTES = 24 * 2**20


def column_tables(coupling, col_pairs):
    left_table = jnp.take(coupling.T, col_pairs[:, 0], axis=0).T
    right_table = jnp.take(coupling.T, col_pairs[:, 1], axis=0).T
    return (left_table, right_table)


def cycle_rows(left_table, right_table, row_pairs):
    left_part = jnp.take(left_table, row_pairs[:, 0], axis=0)
    right_part = jnp.take(right_table, row_pairs[:, 1], axis=0)
    return (left_part * right_part).astype(jnp.bfloat16)


def cycle_all(coupling, pair_list, col_pairs, flat_rhs):
    total_pairs = pair_list.shape[0]
    step_rows = math.gcd(total_pairs, 512)
    row_blocks = pair_list.reshape(total_pairs // step_rows, step_rows, 2)
    left_table, right_table = column_tables(coupling, col_pairs)

    def one_block(row_pairs):
        weights = cycle_rows(left_table, right_table, row_pairs)
        return jnp.dot(weights, flat_rhs, preferred_element_type=jnp.float32)

    return lax.map(one_block, row_blocks).reshape(total_pairs, -1)


def local_general(
    lambda_amps,
    integral_tiles,
    tile_of,
    tile_mask,
    pair_list,
    coupling,
    pair_gap,
    row_energy,
    col_energy,
):
    pair_count = lambda_amps.shape[2]
    tile_rows = lambda_amps.shape[3]
    col_count = lambda_amps.shape[4]
    owners = lax.axis_size("pair")
    sub_count = lax.axis_size("sub")
    wanted = tile_of.reshape(pair_count)
    empty_tiles = jnp.zeros((pair_count, tile_rows, tile_rows), integral_tiles.dtype)
    shard_piece = lax.all_gather(integral_tiles, "pair", axis=0, tiled=True)
    inside = (wanted >= 0) & (wanted < shard_piece.shape[0])
    taken_rows = shard_piece[jnp.clip(wanted, 0, shard_piece.shape[0] - 1)]
    chosen = jnp.where(inside[:, None, None], taken_rows, empty_tiles)
    amplitudes = lambda_amps.reshape(pair_count, tile_rows, col_count)
    ladder = jnp.einsum("pac,pcb->pab", chosen, amplitudes, preferred_element_type=jnp.float32)
    blocks = tile_mask.shape[3]
    keep_mask = tile_mask.reshape(pair_count, 1, blocks, 1).astype(jnp.float32)
    ladder = (
        ladder.reshape(pair_count, tile_rows, blocks, col_count // blocks) * keep_mask
    ).reshape(pair_count, tile_rows, col_count)
    dressed = (amplitudes.astype(jnp.float32) + ladder).astype(jnp.bfloat16)
    dressed = dressed.reshape(1, 1, pair_count, tile_rows, col_count)
    relayed = lax.all_to_all(dressed, "pair", split_axis=3, concat_axis=0, tiled=True)
    sub_index = lax.axis_index("sub")
    block_ids = jnp.arange(owners, dtype=jnp.int32) * sub_count + sub_index
    mine_ids = (
        block_ids[:, None] * pair_count + jnp.arange(pair_count, dtype=jnp.int32)[None, :]
    ).reshape(-1)
    col_pairs = pair_list[mine_ids]
    flat_rhs = relayed.reshape(owners * pair_count, -1)
    partial_value = cycle_all(coupling, pair_list, col_pairs, flat_rhs)
    partial_value = partial_value.reshape(
        owners, sub_count, pair_count, relayed.shape[3], col_count
    )
    cycle_term = lax.psum_scatter(
        partial_value.astype(jnp.bfloat16), "sub", scatter_dimension=1, tiled=True
    ).astype(jnp.float32)
    total_sum = relayed.astype(jnp.float32) + cycle_term
    energy_gap = (
        pair_gap[:, :, :, None, None]
        + row_energy[None, None, None, :, None]
        + col_energy[None, None, None, None, :]
    )
    return (-total_sum / energy_gap).astype(jnp.bfloat16)


def in_hbm(value):
    return pltpu.with_memory_space_constraint(value, pltpu.HBM)


def in_smem(value):
    return pltpu.with_memory_space_constraint(value, pltpu.SMEM)


def one_hot(hits):
    return jnp.where(hits, 1.0, 0.0).astype(jnp.bfloat16)


def square_iotas(size):
    return (lax.broadcasted_iota(jnp.int32, (size, size), axis) for axis in range(2))


def split3(value):
    high = value.astype(jnp.bfloat16)
    rest = value - high.astype(jnp.float32)
    mid = rest.astype(jnp.bfloat16)
    low = (rest - mid.astype(jnp.float32)).astype(jnp.bfloat16)
    return high, mid, low


def pick_columns(value, columns):
    high, mid, low = (
        jnp.dot(part, columns, preferred_element_type=jnp.float32) for part in split3(value)
    )
    return high + (mid + low)


def pick_rows(columns, value):
    dims = (((0,), (0,)), ((), ()))
    high, mid, low = (
        lax.dot_general(columns, part, dims, preferred_element_type=jnp.float32)
        for part in split3(value)
    )
    return high + (mid + low)


def hold_kernel(lam_ref, held_ref, swap_ref, sems):
    step = lam_ref.shape[2] // sems.shape[0]
    copies = []
    for i in range(sems.shape[0]):
        block = pl.ds(i * step, step)
        copy = pltpu.make_async_copy(
            lam_ref.at[:, :, block], held_ref.at[:, :, block], sems.at[i]
        )
        copy.start()
        copies.append(copy)
    to, frm = square_iotas(ROWS * ROWS)
    swap_ref[...] = one_hot(to == (frm % ROWS) * ROWS + frm // ROWS)
    for copy in copies:
        copy.wait()


def hold(lambda_amps):
    anywhere = pl.BlockSpec(memory_space=pl.ANY)
    return pl.pallas_call(
        hold_kernel,
        in_specs=[anywhere],
        out_specs=[anywhere, pl.BlockSpec(memory_space=pltpu.VMEM)],
        out_shape=[
            jax.ShapeDtypeStruct(lambda_amps.shape, lambda_amps.dtype),
            jax.ShapeDtypeStruct((ROWS * ROWS, ROWS * ROWS), jnp.bfloat16),
        ],
        scratch_shapes=[pltpu.SemaphoreType.DMA((8,))],
        compiler_params=pltpu.CompilerParams(vmem_limit_bytes=VMEM_BYTES),
        cost_estimate=pl.CostEstimate(
            flops=0, bytes_accessed=4 * lambda_amps.size, transcendentals=0
        ),
    )(in_hbm(lambda_amps))


def weights_kernel(
    pair_ref, coupling_ref, gap_ref, place_ref, row_ref, col_ref, w_ref, inverse_ref, full
):
    total = pair_ref.shape[1]
    depth = coupling_ref.shape[0]
    owners, _, pairs = gap_ref.shape
    me, sub = place_ref[0], place_ref[1]
    orbital = lax.broadcasted_iota(jnp.int32, (depth, total), 0)
    coupling = coupling_ref[...]
    product = None
    for side in range(2):
        columns = one_hot(orbital == pair_ref[side : side + 1, :])
        picked = pick_rows(columns, pick_columns(coupling, columns))
        product = picked if product is None else product * picked
    frm, to = square_iotas(total)
    block, within = to // pairs, to % pairs
    source = ((me ^ (block % owners)) * 2 + (sub ^ (block // owners))) * pairs + within
    full[...] = jnp.dot(
        product.astype(jnp.bfloat16), one_hot(frm == source), preferred_element_type=jnp.float32
    )
    row, column = square_iotas(pairs)
    for k in range(owners):
        start = pl.multiple_of(((me ^ k) * 2 + sub) * pairs, pairs)
        rows = pl.ds(k * pairs, pairs)
        w_ref[rows, :] = full[pl.ds(start, pairs), :].astype(jnp.bfloat16)
        gap = jnp.sum(jnp.where(row == column, gap_ref[me ^ k], 0.0), axis=1, keepdims=True)
        for a in range(inverse_ref.shape[0]):
            inverse_ref[a, rows, :] = -1.0 / ((gap + row_ref[a]) + col_ref[...])


def make_weights(pair_list, coupling, pair_gap, place, row_energy, col_energy):
    owners, _, pairs = pair_gap.shape
    total = pair_list.shape[0]
    mine = owners * pairs
    rows, cols = row_energy.shape[0], col_energy.shape[0]
    smem = pl.BlockSpec(memory_space=pltpu.SMEM)
    vmem = pl.BlockSpec(memory_space=pltpu.VMEM)
    return pl.pallas_call(
        weights_kernel,
        in_specs=[vmem, vmem, vmem, smem, smem, vmem],
        out_specs=[vmem, vmem],
        out_shape=[
            jax.ShapeDtypeStruct((mine, total), jnp.bfloat16),
            jax.ShapeDtypeStruct((rows, mine, cols), jnp.float32),
        ],
        scratch_shapes=[pltpu.VMEM((total, total), jnp.float32)],
        compiler_params=pltpu.CompilerParams(vmem_limit_bytes=VMEM_BYTES),
        cost_estimate=pl.CostEstimate(
            flops=12 * total * coupling.size, bytes_accessed=4 * coupling.size, transcendentals=0
        ),
    )(pair_list.T, coupling, pair_gap, place, row_energy, col_energy.reshape(1, cols))


def dress_kernel(owners, rows, groups, place_ref, tile_of_ref, mask_ref, *refs):
    tile_refs, lam_ref = (refs[0], refs[owners - 1], *refs[1 : owners - 1]), refs[owners]
    swap_ref = refs[owners + 1]
    out_refs = refs[owners + 2 : -2]
    tiles, stage = refs[-2:]
    me = place_ref[0]
    flat = [(k, c, out, j) for out, group in zip(out_refs, groups) for j, (k, c) in enumerate(group)]
    starts = [pl.multiple_of((me ^ k) * rows + c * ROWS, ROWS) for k, c, _, _ in flat]
    tile_rows, cols = lam_ref.shape[3:]
    row = lax.broadcasted_iota(jnp.int32, (ROWS, tile_rows), 0)
    column = lax.broadcasted_iota(jnp.int32, (ROWS, tile_rows), 1)
    for n, start in enumerate(starts):
        block = pl.ds(n * ROWS, ROWS)
        own_row = one_hot(column == row + start)
        for k in range(owners):
            tiles[k, block, :tile_rows] = tile_refs[k][0, pl.ds(start, ROWS), :]
            tiles[k, block, tile_rows:] = own_row
    swap = swap_ref[...]
    parts = mask_ref.shape[2]
    width = cols // parts
    for g in range(lam_ref.shape[2] // ROWS):
        for i in range(ROWS):
            pair = g * ROWS + i
            amps = lam_ref[0, 0, pair]
            kept = [
                amps[:, part * width : (part + 1) * width]
                * mask_ref[0, 0, part, pair].astype(jnp.float32).astype(jnp.bfloat16)
                for part in range(parts)
            ]
            both = jnp.concatenate([jnp.concatenate(kept, axis=1), amps], axis=0)
            full = jnp.dot(
                tiles[tile_of_ref[0, 0, pair] ^ me], both, preferred_element_type=jnp.float32
            ).astype(jnp.bfloat16)
            for n in range(len(flat)):
                stage[g, n, pl.ds(i * ROWS, ROWS), :] = full[n * ROWS : (n + 1) * ROWS]
        for n, (_, _, out, j) in enumerate(flat):
            turned = jnp.dot(swap, stage[g, n], preferred_element_type=jnp.float32)
            out[j, :, pl.ds(g * ROWS, ROWS), :] = turned.astype(jnp.bfloat16).reshape(
                ROWS, ROWS, turned.shape[1]
            )


def dress(groups, place, tile_of, tile_mask, tiles, lambda_amps, swap):
    owners = len(tiles)
    pairs, tile_rows, cols = lambda_amps.shape[2:]
    rows = tile_rows // owners
    smem = pl.BlockSpec(memory_space=pltpu.SMEM)
    vmem = pl.BlockSpec(memory_space=pltpu.VMEM)
    count = sum(len(group) for group in groups)
    return pl.pallas_call(
        functools.partial(dress_kernel, owners, rows, groups),
        in_specs=[smem] * 3 + [vmem] * (owners + 2),
        out_specs=[vmem] * len(groups),
        out_shape=[
            jax.ShapeDtypeStruct((len(group), ROWS, pairs, cols), jnp.bfloat16)
            for group in groups
        ],
        scratch_shapes=[
            pltpu.VMEM((owners, count * ROWS, 2 * tile_rows), jnp.bfloat16),
            pltpu.VMEM((pairs // ROWS, count, ROWS * ROWS, cols), jnp.bfloat16),
        ],
        compiler_params=pltpu.CompilerParams(vmem_limit_bytes=VMEM_BYTES),
        cost_estimate=pl.CostEstimate(
            flops=2 * pairs * count * ROWS * tile_rows * cols,
            bytes_accessed=3 * pairs * tile_rows * cols,
            transcendentals=0,
        ),
    )(
        in_smem(place),
        in_smem(tile_of),
        in_smem(jnp.swapaxes(tile_mask, 2, 3)),
        tiles[0],
        *tiles[2:],
        tiles[1],
        lambda_amps,
        swap,
    )


def finish_blocks(indices, chunk, swap_ref, w_ref, inverse_ref, piece_refs, done, ys, then):
    groups, _, rows, _ = done.shape
    mine = groups * ROWS
    weights = w_ref[...]
    for a in range(rows):
        amps = jnp.concatenate([ref[index, a] for ref, index in zip(piece_refs, indices)], axis=0)
        cycle = jnp.dot(weights, amps, preferred_element_type=jnp.float32)
        total = amps[:mine].astype(jnp.float32) + cycle
        value = (total * inverse_ref[chunk * rows + a]).astype(jnp.bfloat16)
        for g in range(groups):
            ys[g, pl.ds(a * ROWS, ROWS), :] = value[g * ROWS : (g + 1) * ROWS]
    swap = swap_ref[...]
    for g in range(groups):
        turned = jnp.dot(swap, ys[g], preferred_element_type=jnp.float32)
        done[g] = turned.astype(jnp.bfloat16).reshape(done.shape[1:])
        then(g)


def early_kernel(indices, chunk, swap_ref, w_ref, inverse_ref, *refs):
    piece_refs, (done, ys) = refs[:-2], refs[-2:]
    finish_blocks(
        indices, chunk, swap_ref, w_ref, inverse_ref, piece_refs, done, ys, lambda g: None
    )


def last_kernel(indices, chunk, swap_ref, w_ref, inverse_ref, place_ref, *refs):
    ready_refs, piece_refs, (out_ref, done, ys, sems) = refs[:chunk], refs[chunk:-4], refs[-4:]
    groups, _, rows, _ = done.shape
    halves = 2 * groups // len(indices)
    me = place_ref[0]
    leaving = []

    def write(source, c, g):
        k, h = g // halves, g % halves
        copy = pltpu.make_async_copy(
            source.at[g],
            out_ref.at[me ^ k, 0, pl.ds(h * ROWS, ROWS), pl.ds(c * rows, rows), :],
            sems.at[c, g],
        )
        copy.start()
        leaving.append(copy)

    for c, ref in enumerate(ready_refs):
        for g in range(groups):
            write(ref, c, g)
    finish_blocks(
        indices,
        chunk,
        swap_ref,
        w_ref,
        inverse_ref,
        piece_refs,
        done,
        ys,
        lambda g: write(done, chunk, g),
    )
    for copy in leaving:
        copy.wait()


def finish(chunk, swap, weights, inverse, pieces, place=None, ready=(), shape=None):
    _, rows, pairs, cols = pieces[0][0].shape
    groups = len(pieces) // 2 * (pairs // ROWS)
    indices = [index for _, index in pieces]
    vmem, anywhere = pl.BlockSpec(memory_space=pltpu.VMEM), pl.BlockSpec(memory_space=pl.ANY)
    block = (groups, ROWS, rows, cols)
    ys = pltpu.VMEM((groups, ROWS * rows, cols), jnp.bfloat16)
    args, in_specs = [swap, weights, inverse], [vmem] * 3
    if shape is None:
        kernel = functools.partial(early_kernel, indices, chunk)
        out_spec, out_shape = vmem, jax.ShapeDtypeStruct(block, jnp.bfloat16)
        scratch = [ys]
    else:
        kernel = functools.partial(last_kernel, indices, chunk)
        out_spec, out_shape = anywhere, jax.ShapeDtypeStruct(shape, jnp.bfloat16)
        scratch = [pltpu.VMEM(block, jnp.bfloat16), ys]
        scratch += [pltpu.SemaphoreType.DMA((chunk + 1, groups))]
        args += [place, *ready]
        in_specs += [pl.BlockSpec(memory_space=pltpu.SMEM)] + [anywhere] * len(ready)
    return pl.pallas_call(
        kernel,
        in_specs=in_specs + [vmem] * len(pieces),
        out_specs=out_spec,
        out_shape=out_shape,
        scratch_shapes=scratch,
        compiler_params=pltpu.CompilerParams(vmem_limit_bytes=VMEM_BYTES),
        cost_estimate=pl.CostEstimate(flops=0, bytes_accessed=0, transcendentals=0),
    )(*args, *[piece for piece, _ in pieces])


def local_chunked(
    lambda_amps,
    integral_tiles,
    tile_of,
    tile_mask,
    pair_list,
    coupling,
    pair_gap,
    row_energy,
    col_energy,
):
    pairs, tile_rows, cols = lambda_amps.shape[2:]
    owners = lax.axis_size("pair")
    rows = tile_rows // owners
    chunks = rows // ROWS
    me = lax.axis_index("pair").astype(jnp.int32)
    sub = lax.axis_index("sub").astype(jnp.int32)
    place = jnp.stack([me, sub])

    def to_owner(value, k):
        return lax.ppermute(value, "pair", [(o, o ^ k) for o in range(owners)])

    def to_sibling(value):
        return lax.ppermute(value, "sub", [(0, 1), (1, 0)])

    def after(value, earlier):
        return value if earlier is None else lax.optimization_barrier((value, earlier))[0]

    tiles = [integral_tiles] + [to_owner(integral_tiles, k) for k in range(1, owners)]

    far = list(range(2, owners))
    last = far[-1]
    groups = [((k, c),) for c in range(chunks) for k in far[::-1]]
    groups += [tuple((k, c) for c in range(chunks)) for k in (1, 0)]
    held, swap = hold(lambda_amps)
    sent = dict(zip(groups, dress(groups, place, tile_of, tile_mask, tiles, held, swap)))
    weights, inverse = make_weights(
        after(pair_list, sent[groups[0]]), coupling, pair_gap, place, row_energy, col_energy
    )
    own, near = sent[groups[-1]], to_owner(sent[groups[-2]], 1)
    direct, other = {}, {}
    for k in far:
        for c in range(chunks):
            earlier = direct[k, c - 1] if c and k == last else None
            direct[k, c] = to_owner(after(sent[((k, c),)], earlier), k)
    own_passed = to_sibling(after(own, weights))
    near_passed = to_sibling(after(near, (weights, direct[far[0], 0])))
    for k in far:
        for c in range(chunks):
            earlier = None
            if k == last:
                earlier = other[far[0], c - 1] if c else weights
            other[k, c] = to_sibling(after(direct[k, c], earlier))

    ready = []
    for c in range(chunks):
        pieces = [(own, c), (near, c)] + [(direct[k, c], 0) for k in far]
        pieces += [(own_passed, c), (near_passed, c)] + [(other[k, c], 0) for k in far]
        if c + 1 < chunks:
            ready.append(finish(c, swap, weights, inverse, pieces))
    shape = (owners, 1, pairs, rows, cols)
    return finish(c, swap, weights, inverse, pieces, place, ready, shape)


def solution(mesh):
    placed = (
        P(("mol", "pair"), "sub", None, None, "tile"),
        P(("mol", "pair"), None, None),
        P(("mol", "pair"), "sub", None),
        P(("mol", "pair"), "sub", None, "tile"),
        P("mol", None),
        P("mol", None),
        P("mol", "sub", None),
        P(("mol", "pair")),
        P(("mol", "tile")),
    )
    owners, subs = mesh.shape["pair"], mesh.shape["sub"]

    def local(*args):
        tile_rows, cols = args[0].shape[3:]
        rows = tile_rows // owners
        power = owners >= 4 and owners & (owners - 1) == 0
        fits = rows % ROWS == 0 and cols % LANES == 0 and args[1].shape[0] == 1
        if power and fits and subs == 2 and args[0].shape[2] % ROWS == 0:
            return local_chunked(*args)
        return local_general(*args)

    return jax.shard_map(
        local,
        mesh=mesh,
        in_specs=placed,
        out_specs=P("mol", "sub", None, "pair", "tile"),
        check_vma=False,
    )
```

```python
import functools
import math

import jax
import jax.numpy as jnp
from jax import lax
from jax.experimental import pallas as pl
from jax.experimental.pallas import tpu as pltpu
from jax.sharding import PartitionSpec as P

ROWS = 16
LANES = 128
VMEM_BYTES = 24 * 2**20


def column_tables(coupling, col_pairs):
    left_table = jnp.take(coupling.T, col_pairs[:, 0], axis=0).T
    right_table = jnp.take(coupling.T, col_pairs[:, 1], axis=0).T
    return (left_table, right_table)


def cycle_rows(left_table, right_table, row_pairs):
    left_part = jnp.take(left_table, row_pairs[:, 0], axis=0)
    right_part = jnp.take(right_table, row_pairs[:, 1], axis=0)
    return (left_part * right_part).astype(jnp.bfloat16)


def cycle_all(coupling, pair_list, col_pairs, flat_rhs):
    total_pairs = pair_list.shape[0]
    step_rows = math.gcd(total_pairs, 512)
    row_blocks = pair_list.reshape(total_pairs // step_rows, step_rows, 2)
    left_table, right_table = column_tables(coupling, col_pairs)

    def one_block(row_pairs):
        weights = cycle_rows(left_table, right_table, row_pairs)
        return jnp.dot(weights, flat_rhs, preferred_element_type=jnp.float32)

    return lax.map(one_block, row_blocks).reshape(total_pairs, -1)


def local_general(
    lambda_amps,
    integral_tiles,
    tile_of,
    tile_mask,
    pair_list,
    coupling,
    pair_gap,
    row_energy,
    col_energy,
):
    pair_count = lambda_amps.shape[2]
    tile_rows = lambda_amps.shape[3]
    col_count = lambda_amps.shape[4]
    owners = lax.axis_size("pair")
    sub_count = lax.axis_size("sub")
    wanted = tile_of.reshape(pair_count)
    empty_tiles = jnp.zeros((pair_count, tile_rows, tile_rows), integral_tiles.dtype)
    shard_piece = lax.all_gather(integral_tiles, "pair", axis=0, tiled=True)
    inside = (wanted >= 0) & (wanted < shard_piece.shape[0])
    taken_rows = shard_piece[jnp.clip(wanted, 0, shard_piece.shape[0] - 1)]
    chosen = jnp.where(inside[:, None, None], taken_rows, empty_tiles)
    amplitudes = lambda_amps.reshape(pair_count, tile_rows, col_count)
    ladder = jnp.einsum("pac,pcb->pab", chosen, amplitudes, preferred_element_type=jnp.float32)
    blocks = tile_mask.shape[3]
    keep_mask = tile_mask.reshape(pair_count, 1, blocks, 1).astype(jnp.float32)
    ladder = (
        ladder.reshape(pair_count, tile_rows, blocks, col_count // blocks) * keep_mask
    ).reshape(pair_count, tile_rows, col_count)
    dressed = (amplitudes.astype(jnp.float32) + ladder).astype(jnp.bfloat16)
    dressed = dressed.reshape(1, 1, pair_count, tile_rows, col_count)
    relayed = lax.all_to_all(dressed, "pair", split_axis=3, concat_axis=0, tiled=True)
    sub_index = lax.axis_index("sub")
    block_ids = jnp.arange(owners, dtype=jnp.int32) * sub_count + sub_index
    mine_ids = (
        block_ids[:, None] * pair_count + jnp.arange(pair_count, dtype=jnp.int32)[None, :]
    ).reshape(-1)
    col_pairs = pair_list[mine_ids]
    flat_rhs = relayed.reshape(owners * pair_count, -1)
    partial_value = cycle_all(coupling, pair_list, col_pairs, flat_rhs)
    partial_value = partial_value.reshape(
        owners, sub_count, pair_count, relayed.shape[3], col_count
    )
    cycle_term = lax.psum_scatter(
        partial_value.astype(jnp.bfloat16), "sub", scatter_dimension=1, tiled=True
    ).astype(jnp.float32)
    total_sum = relayed.astype(jnp.float32) + cycle_term
    energy_gap = (
        pair_gap[:, :, :, None, None]
        + row_energy[None, None, None, :, None]
        + col_energy[None, None, None, None, :]
    )
    return (-total_sum / energy_gap).astype(jnp.bfloat16)


def in_hbm(value):
    return pltpu.with_memory_space_constraint(value, pltpu.HBM)


def in_smem(value):
    return pltpu.with_memory_space_constraint(value, pltpu.SMEM)


def one_hot(hits):
    return jnp.where(hits, 1.0, 0.0).astype(jnp.bfloat16)


def square_iotas(size):
    return (lax.broadcasted_iota(jnp.int32, (size, size), axis) for axis in range(2))


def split3(value):
    high = value.astype(jnp.bfloat16)
    rest = value - high.astype(jnp.float32)
    mid = rest.astype(jnp.bfloat16)
    low = (rest - mid.astype(jnp.float32)).astype(jnp.bfloat16)
    return high, mid, low


def pick_columns(value, columns):
    high, mid, low = (
        jnp.dot(part, columns, preferred_element_type=jnp.float32) for part in split3(value)
    )
    return high + (mid + low)


def pick_rows(columns, value):
    dims = (((0,), (0,)), ((), ()))
    high, mid, low = (
        lax.dot_general(columns, part, dims, preferred_element_type=jnp.float32)
        for part in split3(value)
    )
    return high + (mid + low)


def hold_kernel(lam_ref, held_ref, swap_ref, sems):
    step = lam_ref.shape[2] // sems.shape[0]
    copies = []
    for i in range(sems.shape[0]):
        block = pl.ds(i * step, step)
        copy = pltpu.make_async_copy(
            lam_ref.at[:, :, block], held_ref.at[:, :, block], sems.at[i]
        )
        copy.start()
        copies.append(copy)
    to, frm = square_iotas(ROWS * ROWS)
    swap_ref[...] = one_hot(to == (frm % ROWS) * ROWS + frm // ROWS)
    for copy in copies:
        copy.wait()


def hold(lambda_amps):
    anywhere = pl.BlockSpec(memory_space=pl.ANY)
    return pl.pallas_call(
        hold_kernel,
        in_specs=[anywhere],
        out_specs=[anywhere, pl.BlockSpec(memory_space=pltpu.VMEM)],
        out_shape=[
            jax.ShapeDtypeStruct(lambda_amps.shape, lambda_amps.dtype),
            jax.ShapeDtypeStruct((ROWS * ROWS, ROWS * ROWS), jnp.bfloat16),
        ],
        scratch_shapes=[pltpu.SemaphoreType.DMA((8,))],
        compiler_params=pltpu.CompilerParams(vmem_limit_bytes=VMEM_BYTES),
        cost_estimate=pl.CostEstimate(
            flops=0, bytes_accessed=4 * lambda_amps.size, transcendentals=0
        ),
    )(in_hbm(lambda_amps))


def weights_kernel(
    pair_ref, coupling_ref, gap_ref, place_ref, row_ref, col_ref, w_ref, inverse_ref, full
):
    total = pair_ref.shape[1]
    depth = coupling_ref.shape[0]
    owners, _, pairs = gap_ref.shape
    me, sub = place_ref[0], place_ref[1]
    orbital = lax.broadcasted_iota(jnp.int32, (depth, total), 0)
    coupling = coupling_ref[...]
    product = None
    for side in range(2):
        columns = one_hot(orbital == pair_ref[side : side + 1, :])
        picked = pick_rows(columns, pick_columns(coupling, columns))
        product = picked if product is None else product * picked
    frm, to = square_iotas(total)
    block, within = to // pairs, to % pairs
    source = ((me ^ (block % owners)) * 2 + (sub ^ (block // owners))) * pairs + within
    full[...] = jnp.dot(
        product.astype(jnp.bfloat16), one_hot(frm == source), preferred_element_type=jnp.float32
    )
    row, column = square_iotas(pairs)
    for k in range(owners):
        start = pl.multiple_of(((me ^ k) * 2 + sub) * pairs, pairs)
        rows = pl.ds(k * pairs, pairs)
        w_ref[rows, :] = full[pl.ds(start, pairs), :].astype(jnp.bfloat16)
        gap = jnp.sum(jnp.where(row == column, gap_ref[me ^ k], 0.0), axis=1, keepdims=True)
        for a in range(inverse_ref.shape[0]):
            inverse_ref[a, rows, :] = -1.0 / ((gap + row_ref[a]) + col_ref[...])


def make_weights(pair_list, coupling, pair_gap, place, row_energy, col_energy):
    owners, _, pairs = pair_gap.shape
    total = pair_list.shape[0]
    mine = owners * pairs
    rows, cols = row_energy.shape[0], col_energy.shape[0]
    smem = pl.BlockSpec(memory_space=pltpu.SMEM)
    vmem = pl.BlockSpec(memory_space=pltpu.VMEM)
    return pl.pallas_call(
        weights_kernel,
        in_specs=[vmem, vmem, vmem, smem, smem, vmem],
        out_specs=[vmem, vmem],
        out_shape=[
            jax.ShapeDtypeStruct((mine, total), jnp.bfloat16),
            jax.ShapeDtypeStruct((rows, mine, cols), jnp.float32),
        ],
        scratch_shapes=[pltpu.VMEM((total, total), jnp.float32)],
        compiler_params=pltpu.CompilerParams(vmem_limit_bytes=VMEM_BYTES),
        cost_estimate=pl.CostEstimate(
            flops=12 * total * coupling.size, bytes_accessed=4 * coupling.size, transcendentals=0
        ),
    )(pair_list.T, coupling, pair_gap, place, row_energy, col_energy.reshape(1, cols))


def dress_kernel(owners, rows, groups, place_ref, tile_of_ref, mask_ref, *refs):
    tile_refs, lam_ref = (refs[0], refs[owners - 1], *refs[1 : owners - 1]), refs[owners]
    swap_ref = refs[owners + 1]
    out_refs = refs[owners + 2 : -2]
    tiles, stage = refs[-2:]
    me = place_ref[0]
    flat = [(k, c, out, j) for out, group in zip(out_refs, groups) for j, (k, c) in enumerate(group)]
    starts = [pl.multiple_of((me ^ k) * rows + c * ROWS, ROWS) for k, c, _, _ in flat]
    tile_rows, cols = lam_ref.shape[3:]
    row = lax.broadcasted_iota(jnp.int32, (ROWS, tile_rows), 0)
    column = lax.broadcasted_iota(jnp.int32, (ROWS, tile_rows), 1)
    for n, start in enumerate(starts):
        block = pl.ds(n * ROWS, ROWS)
        own_row = one_hot(column == row + start)
        for k in range(owners):
            tiles[k, block, :tile_rows] = tile_refs[k][0, pl.ds(start, ROWS), :]
            tiles[k, block, tile_rows:] = own_row
    swap = swap_ref[...]
    parts = mask_ref.shape[2]
    width = cols // parts
    for g in range(lam_ref.shape[2] // ROWS):
        for i in range(ROWS):
            pair = g * ROWS + i
            amps = lam_ref[0, 0, pair]
            kept = [
                amps[:, part * width : (part + 1) * width]
                * mask_ref[0, 0, part, pair].astype(jnp.float32).astype(jnp.bfloat16)
                for part in range(parts)
            ]
            both = jnp.concatenate([jnp.concatenate(kept, axis=1), amps], axis=0)
            full = jnp.dot(
                tiles[tile_of_ref[0, 0, pair] ^ me], both, preferred_element_type=jnp.float32
            ).astype(jnp.bfloat16)
            for n in range(len(flat)):
                stage[g, n, pl.ds(i * ROWS, ROWS), :] = full[n * ROWS : (n + 1) * ROWS]
        for n, (_, _, out, j) in enumerate(flat):
            turned = jnp.dot(swap, stage[g, n], preferred_element_type=jnp.float32)
            out[j, :, pl.ds(g * ROWS, ROWS), :] = turned.astype(jnp.bfloat16).reshape(
                ROWS, ROWS, turned.shape[1]
            )


def dress(groups, place, tile_of, tile_mask, tiles, lambda_amps, swap):
    owners = len(tiles)
    pairs, tile_rows, cols = lambda_amps.shape[2:]
    rows = tile_rows // owners
    smem = pl.BlockSpec(memory_space=pltpu.SMEM)
    vmem = pl.BlockSpec(memory_space=pltpu.VMEM)
    count = sum(len(group) for group in groups)
    return pl.pallas_call(
        functools.partial(dress_kernel, owners, rows, groups),
        in_specs=[smem] * 3 + [vmem] * (owners + 2),
        out_specs=[vmem] * len(groups),
        out_shape=[
            jax.ShapeDtypeStruct((len(group), ROWS, pairs, cols), jnp.bfloat16)
            for group in groups
        ],
        scratch_shapes=[
            pltpu.VMEM((owners, count * ROWS, 2 * tile_rows), jnp.bfloat16),
            pltpu.VMEM((pairs // ROWS, count, ROWS * ROWS, cols), jnp.bfloat16),
        ],
        compiler_params=pltpu.CompilerParams(vmem_limit_bytes=VMEM_BYTES),
        cost_estimate=pl.CostEstimate(
            flops=2 * pairs * count * ROWS * tile_rows * cols,
            bytes_accessed=3 * pairs * tile_rows * cols,
            transcendentals=0,
        ),
    )(
        in_smem(place),
        in_smem(tile_of),
        in_smem(jnp.swapaxes(tile_mask, 2, 3)),
        tiles[0],
        *tiles[2:],
        tiles[1],
        lambda_amps,
        swap,
    )


def finish_blocks(indices, chunk, swap_ref, w_ref, inverse_ref, piece_refs, done, ys, then):
    groups, _, rows, _ = done.shape
    mine = groups * ROWS
    weights = w_ref[...]
    for a in range(rows):
        amps = jnp.concatenate([ref[index, a] for ref, index in zip(piece_refs, indices)], axis=0)
        cycle = jnp.dot(weights, amps, preferred_element_type=jnp.float32)
        total = amps[:mine].astype(jnp.float32) + cycle
        value = (total * inverse_ref[chunk * rows + a]).astype(jnp.bfloat16)
        for g in range(groups):
            ys[g, pl.ds(a * ROWS, ROWS), :] = value[g * ROWS : (g + 1) * ROWS]
    swap = swap_ref[...]
    for g in range(groups):
        turned = jnp.dot(swap, ys[g], preferred_element_type=jnp.float32)
        done[g] = turned.astype(jnp.bfloat16).reshape(done.shape[1:])
        then(g)


def early_kernel(indices, chunk, swap_ref, w_ref, inverse_ref, *refs):
    piece_refs, (done, ys) = refs[:-2], refs[-2:]
    finish_blocks(
        indices, chunk, swap_ref, w_ref, inverse_ref, piece_refs, done, ys, lambda g: None
    )


def last_kernel(indices, chunk, swap_ref, w_ref, inverse_ref, place_ref, *refs):
    ready_refs, piece_refs, (out_ref, done, ys, sems) = refs[:chunk], refs[chunk:-4], refs[-4:]
    groups, _, rows, _ = done.shape
    halves = 2 * groups // len(indices)
    me = place_ref[0]
    leaving = []

    def write(source, c, g):
        k, h = g // halves, g % halves
        copy = pltpu.make_async_copy(
            source.at[g],
            out_ref.at[me ^ k, 0, pl.ds(h * ROWS, ROWS), pl.ds(c * rows, rows), :],
            sems.at[c, g],
        )
        copy.start()
        leaving.append(copy)

    for c, ref in enumerate(ready_refs):
        for g in range(groups):
            write(ref, c, g)
    finish_blocks(
        indices,
        chunk,
        swap_ref,
        w_ref,
        inverse_ref,
        piece_refs,
        done,
        ys,
        lambda g: write(done, chunk, g),
    )
    for copy in leaving:
        copy.wait()


def finish(chunk, swap, weights, inverse, pieces, place=None, ready=(), shape=None):
    _, rows, pairs, cols = pieces[0][0].shape
    groups = len(pieces) // 2 * (pairs // ROWS)
    indices = [index for _, index in pieces]
    vmem, anywhere = pl.BlockSpec(memory_space=pltpu.VMEM), pl.BlockSpec(memory_space=pl.ANY)
    block = (groups, ROWS, rows, cols)
    ys = pltpu.VMEM((groups, ROWS * rows, cols), jnp.bfloat16)
    args, in_specs = [swap, weights, inverse], [vmem] * 3
    if shape is None:
        kernel = functools.partial(early_kernel, indices, chunk)
        out_spec, out_shape = vmem, jax.ShapeDtypeStruct(block, jnp.bfloat16)
        scratch = [ys]
    else:
        kernel = functools.partial(last_kernel, indices, chunk)
        out_spec, out_shape = anywhere, jax.ShapeDtypeStruct(shape, jnp.bfloat16)
        scratch = [pltpu.VMEM(block, jnp.bfloat16), ys]
        scratch += [pltpu.SemaphoreType.DMA((chunk + 1, groups))]
        args += [place, *ready]
        in_specs += [pl.BlockSpec(memory_space=pltpu.SMEM)] + [anywhere] * len(ready)
    return pl.pallas_call(
        kernel,
        in_specs=in_specs + [vmem] * len(pieces),
        out_specs=out_spec,
        out_shape=out_shape,
        scratch_shapes=scratch,
        compiler_params=pltpu.CompilerParams(vmem_limit_bytes=VMEM_BYTES),
        cost_estimate=pl.CostEstimate(flops=0, bytes_accessed=0, transcendentals=0),
    )(*args, *[piece for piece, _ in pieces])


def local_chunked(
    lambda_amps,
    integral_tiles,
    tile_of,
    tile_mask,
    pair_list,
    coupling,
    pair_gap,
    row_energy,
    col_energy,
):
    pairs, tile_rows, cols = lambda_amps.shape[2:]
    owners = lax.axis_size("pair")
    rows = tile_rows // owners
    chunks = rows // ROWS
    me = lax.axis_index("pair").astype(jnp.int32)
    sub = lax.axis_index("sub").astype(jnp.int32)
    place = jnp.stack([me, sub])

    def to_owner(value, k):
        return lax.ppermute(value, "pair", [(o, o ^ k) for o in range(owners)])

    def to_sibling(value):
        return lax.ppermute(value, "sub", [(0, 1), (1, 0)])

    def after(value, earlier):
        return value if earlier is None else lax.optimization_barrier((value, earlier))[0]

    tiles = [integral_tiles] + [to_owner(integral_tiles, k) for k in range(1, owners)]

    far = list(range(2, owners))
    last = far[-1]
    groups = [((k, c),) for c in range(chunks) for k in far[::-1]]
    groups += [tuple((k, c) for c in range(chunks)) for k in (1, 0)]
    held, swap = hold(lambda_amps)
    sent = dict(zip(groups, dress(groups, place, tile_of, tile_mask, tiles, held, swap)))
    weights, inverse = make_weights(
        after(pair_list, sent[groups[0]]), coupling, pair_gap, place, row_energy, col_energy
    )
    own, near = sent[groups[-1]], to_owner(sent[groups[-2]], 1)

    @functools.cache
    def landed(k, c):
        earlier = landed(k, c - 1) if c and k == last else None
        return to_owner(after(sent[((k, c),)], earlier), k)

    @functools.cache
    def passed(k, c):
        earlier = passed(far[0], c - 1) if c else (weights, inverse) if k == last else None
        return to_sibling(after(landed(k, c), earlier))

    @functools.cache
    def passed_whole(k):
        return to_sibling(after(near, (weights, inverse, passed(last, 0))) if k else after(own, near))

    chunk_pieces = []
    for c in range(chunks - 1, -1, -1):
        pieces = [(own, c), (near, c)] + [(landed(k, c), 0) for k in far]
        pieces += [(passed_whole(k), c) for k in (0, 1)] + [(passed(k, c), 0) for k in far]
        chunk_pieces.insert(0, pieces)
    ready = [finish(c, swap, weights, inverse, chunk_pieces[c]) for c in range(chunks - 1)]
    shape = (owners, 1, pairs, rows, cols)
    return finish(chunks - 1, swap, weights, inverse, chunk_pieces[-1], place, ready, shape)


def solution(mesh):
    placed = (
        P(("mol", "pair"), "sub", None, None, "tile"),
        P(("mol", "pair"), None, None),
        P(("mol", "pair"), "sub", None),
        P(("mol", "pair"), "sub", None, "tile"),
        P("mol", None),
        P("mol", None),
        P("mol", "sub", None),
        P(("mol", "pair")),
        P(("mol", "tile")),
    )
    owners, subs = mesh.shape["pair"], mesh.shape["sub"]

    def local(*args):
        tile_rows, cols = args[0].shape[3:]
        rows = tile_rows // owners
        power = owners >= 4 and owners & (owners - 1) == 0
        fits = rows % ROWS == 0 and cols % LANES == 0 and args[1].shape[0] == 1
        if power and fits and subs == 2 and args[0].shape[2] % ROWS == 0:
            return local_chunked(*args)
        return local_general(*args)

    return jax.shard_map(
        local,
        mesh=mesh,
        in_specs=placed,
        out_specs=P("mol", "sub", None, "pair", "tile"),
        check_vma=False,
    )
```

```python
import functools
import math

import jax
import jax.numpy as jnp
from jax import lax
from jax.experimental import pallas as pl
from jax.experimental.pallas import tpu as pltpu
from jax.sharding import PartitionSpec as P

ROWS = 16
LANES = 128
VMEM_BYTES = 24 * 2**20


def column_tables(coupling, col_pairs):
    left_table = jnp.take(coupling.T, col_pairs[:, 0], axis=0).T
    right_table = jnp.take(coupling.T, col_pairs[:, 1], axis=0).T
    return (left_table, right_table)


def cycle_rows(left_table, right_table, row_pairs):
    left_part = jnp.take(left_table, row_pairs[:, 0], axis=0)
    right_part = jnp.take(right_table, row_pairs[:, 1], axis=0)
    return (left_part * right_part).astype(jnp.bfloat16)


def cycle_all(coupling, pair_list, col_pairs, flat_rhs):
    total_pairs = pair_list.shape[0]
    step_rows = math.gcd(total_pairs, 512)
    row_blocks = pair_list.reshape(total_pairs // step_rows, step_rows, 2)
    left_table, right_table = column_tables(coupling, col_pairs)

    def one_block(row_pairs):
        weights = cycle_rows(left_table, right_table, row_pairs)
        return jnp.dot(weights, flat_rhs, preferred_element_type=jnp.float32)

    return lax.map(one_block, row_blocks).reshape(total_pairs, -1)


def local_general(
    lambda_amps,
    integral_tiles,
    tile_of,
    tile_mask,
    pair_list,
    coupling,
    pair_gap,
    row_energy,
    col_energy,
):
    pair_count = lambda_amps.shape[2]
    tile_rows = lambda_amps.shape[3]
    col_count = lambda_amps.shape[4]
    owners = lax.axis_size("pair")
    sub_count = lax.axis_size("sub")
    wanted = tile_of.reshape(pair_count)
    empty_tiles = jnp.zeros((pair_count, tile_rows, tile_rows), integral_tiles.dtype)
    shard_piece = lax.all_gather(integral_tiles, "pair", axis=0, tiled=True)
    inside = (wanted >= 0) & (wanted < shard_piece.shape[0])
    taken_rows = shard_piece[jnp.clip(wanted, 0, shard_piece.shape[0] - 1)]
    chosen = jnp.where(inside[:, None, None], taken_rows, empty_tiles)
    amplitudes = lambda_amps.reshape(pair_count, tile_rows, col_count)
    ladder = jnp.einsum("pac,pcb->pab", chosen, amplitudes, preferred_element_type=jnp.float32)
    blocks = tile_mask.shape[3]
    keep_mask = tile_mask.reshape(pair_count, 1, blocks, 1).astype(jnp.float32)
    ladder = (
        ladder.reshape(pair_count, tile_rows, blocks, col_count // blocks) * keep_mask
    ).reshape(pair_count, tile_rows, col_count)
    dressed = (amplitudes.astype(jnp.float32) + ladder).astype(jnp.bfloat16)
    dressed = dressed.reshape(1, 1, pair_count, tile_rows, col_count)
    relayed = lax.all_to_all(dressed, "pair", split_axis=3, concat_axis=0, tiled=True)
    sub_index = lax.axis_index("sub")
    block_ids = jnp.arange(owners, dtype=jnp.int32) * sub_count + sub_index
    mine_ids = (
        block_ids[:, None] * pair_count + jnp.arange(pair_count, dtype=jnp.int32)[None, :]
    ).reshape(-1)
    col_pairs = pair_list[mine_ids]
    flat_rhs = relayed.reshape(owners * pair_count, -1)
    partial_value = cycle_all(coupling, pair_list, col_pairs, flat_rhs)
    partial_value = partial_value.reshape(
        owners, sub_count, pair_count, relayed.shape[3], col_count
    )
    cycle_term = lax.psum_scatter(
        partial_value.astype(jnp.bfloat16), "sub", scatter_dimension=1, tiled=True
    ).astype(jnp.float32)
    total_sum = relayed.astype(jnp.float32) + cycle_term
    energy_gap = (
        pair_gap[:, :, :, None, None]
        + row_energy[None, None, None, :, None]
        + col_energy[None, None, None, None, :]
    )
    return (-total_sum / energy_gap).astype(jnp.bfloat16)


def in_hbm(value):
    return pltpu.with_memory_space_constraint(value, pltpu.HBM)


def in_smem(value):
    return pltpu.with_memory_space_constraint(value, pltpu.SMEM)


def one_hot(hits):
    return jnp.where(hits, 1.0, 0.0).astype(jnp.bfloat16)


def square_iotas(size):
    return (lax.broadcasted_iota(jnp.int32, (size, size), axis) for axis in range(2))


def split3(value):
    high = value.astype(jnp.bfloat16)
    rest = value - high.astype(jnp.float32)
    mid = rest.astype(jnp.bfloat16)
    low = (rest - mid.astype(jnp.float32)).astype(jnp.bfloat16)
    return high, mid, low


def pick_columns(value, columns):
    high, mid, low = (
        jnp.dot(part, columns, preferred_element_type=jnp.float32) for part in split3(value)
    )
    return high + (mid + low)


def pick_rows(columns, value):
    dims = (((0,), (0,)), ((), ()))
    high, mid, low = (
        lax.dot_general(columns, part, dims, preferred_element_type=jnp.float32)
        for part in split3(value)
    )
    return high + (mid + low)


def hold_kernel(lam_ref, held_ref, swap_ref, sems):
    step = lam_ref.shape[2] // sems.shape[0]
    copies = []
    for i in range(sems.shape[0]):
        block = pl.ds(i * step, step)
        copy = pltpu.make_async_copy(
            lam_ref.at[:, :, block], held_ref.at[:, :, block], sems.at[i]
        )
        copy.start()
        copies.append(copy)
    to, frm = square_iotas(ROWS * ROWS)
    swap_ref[...] = one_hot(to == (frm % ROWS) * ROWS + frm // ROWS)
    for copy in copies:
        copy.wait()


def hold(lambda_amps):
    anywhere = pl.BlockSpec(memory_space=pl.ANY)
    return pl.pallas_call(
        hold_kernel,
        in_specs=[anywhere],
        out_specs=[anywhere, pl.BlockSpec(memory_space=pltpu.VMEM)],
        out_shape=[
            jax.ShapeDtypeStruct(lambda_amps.shape, lambda_amps.dtype),
            jax.ShapeDtypeStruct((ROWS * ROWS, ROWS * ROWS), jnp.bfloat16),
        ],
        scratch_shapes=[pltpu.SemaphoreType.DMA((8,))],
        compiler_params=pltpu.CompilerParams(vmem_limit_bytes=VMEM_BYTES),
        cost_estimate=pl.CostEstimate(
            flops=0, bytes_accessed=4 * lambda_amps.size, transcendentals=0
        ),
    )(in_hbm(lambda_amps))


def weights_kernel(
    pair_ref, coupling_ref, gap_ref, place_ref, row_ref, col_ref, w_ref, inverse_ref, full
):
    total = pair_ref.shape[1]
    depth = coupling_ref.shape[0]
    owners, _, pairs = gap_ref.shape
    me, sub = place_ref[0], place_ref[1]
    orbital = lax.broadcasted_iota(jnp.int32, (depth, total), 0)
    coupling = coupling_ref[...]
    product = None
    for side in range(2):
        columns = one_hot(orbital == pair_ref[side : side + 1, :])
        picked = pick_rows(columns, pick_columns(coupling, columns))
        product = picked if product is None else product * picked
    frm, to = square_iotas(total)
    block, within = to // pairs, to % pairs
    source = ((me ^ (block % owners)) * 2 + (sub ^ (block // owners))) * pairs + within
    full[...] = jnp.dot(
        product.astype(jnp.bfloat16), one_hot(frm == source), preferred_element_type=jnp.float32
    )
    row, column = square_iotas(pairs)
    for k in range(owners):
        start = pl.multiple_of(((me ^ k) * 2 + sub) * pairs, pairs)
        rows = pl.ds(k * pairs, pairs)
        w_ref[rows, :] = full[pl.ds(start, pairs), :].astype(jnp.bfloat16)
        gap = jnp.sum(jnp.where(row == column, gap_ref[me ^ k], 0.0), axis=1, keepdims=True)
        for a in range(inverse_ref.shape[0]):
            inverse_ref[a, rows, :] = -1.0 / ((gap + row_ref[a]) + col_ref[...])


def make_weights(pair_list, coupling, pair_gap, place, row_energy, col_energy):
    owners, _, pairs = pair_gap.shape
    total = pair_list.shape[0]
    mine = owners * pairs
    rows, cols = row_energy.shape[0], col_energy.shape[0]
    smem = pl.BlockSpec(memory_space=pltpu.SMEM)
    vmem = pl.BlockSpec(memory_space=pltpu.VMEM)
    return pl.pallas_call(
        weights_kernel,
        in_specs=[vmem, vmem, vmem, smem, smem, vmem],
        out_specs=[vmem, vmem],
        out_shape=[
            jax.ShapeDtypeStruct((mine, total), jnp.bfloat16),
            jax.ShapeDtypeStruct((rows, mine, cols), jnp.float32),
        ],
        scratch_shapes=[pltpu.VMEM((total, total), jnp.float32)],
        compiler_params=pltpu.CompilerParams(vmem_limit_bytes=VMEM_BYTES),
        cost_estimate=pl.CostEstimate(
            flops=12 * total * coupling.size, bytes_accessed=4 * coupling.size, transcendentals=0
        ),
    )(pair_list.T, coupling, pair_gap, place, row_energy, col_energy.reshape(1, cols))


def dress_kernel(owners, rows, groups, place_ref, tile_of_ref, mask_ref, *refs):
    tile_refs, lam_ref = (refs[0], refs[owners - 1], *refs[1 : owners - 1]), refs[owners]
    swap_ref = refs[owners + 1]
    out_refs = refs[owners + 2 : -2]
    tiles, stage = refs[-2:]
    me = place_ref[0]
    flat = [(k, c, out, j) for out, group in zip(out_refs, groups) for j, (k, c) in enumerate(group)]
    starts = [pl.multiple_of((me ^ k) * rows + c * ROWS, ROWS) for k, c, _, _ in flat]
    tile_rows, cols = lam_ref.shape[3:]
    row = lax.broadcasted_iota(jnp.int32, (ROWS, tile_rows), 0)
    column = lax.broadcasted_iota(jnp.int32, (ROWS, tile_rows), 1)
    for n, start in enumerate(starts):
        block = pl.ds(n * ROWS, ROWS)
        own_row = one_hot(column == row + start)
        for k in range(owners):
            tiles[k, block, :tile_rows] = tile_refs[k][0, pl.ds(start, ROWS), :]
            tiles[k, block, tile_rows:] = own_row
    swap = swap_ref[...]
    parts = mask_ref.shape[2]
    width = cols // parts
    for g in range(lam_ref.shape[2] // ROWS):
        for i in range(ROWS):
            pair = g * ROWS + i
            amps = lam_ref[0, 0, pair]
            kept = [
                amps[:, part * width : (part + 1) * width]
                * mask_ref[0, 0, part, pair].astype(jnp.float32).astype(jnp.bfloat16)
                for part in range(parts)
            ]
            both = jnp.concatenate([jnp.concatenate(kept, axis=1), amps], axis=0)
            full = jnp.dot(
                tiles[tile_of_ref[0, 0, pair] ^ me], both, preferred_element_type=jnp.float32
            ).astype(jnp.bfloat16)
            for n in range(len(flat)):
                stage[g, n, pl.ds(i * ROWS, ROWS), :] = full[n * ROWS : (n + 1) * ROWS]
        for n, (_, _, out, j) in enumerate(flat):
            turned = jnp.dot(swap, stage[g, n], preferred_element_type=jnp.float32)
            out[j, :, pl.ds(g * ROWS, ROWS), :] = turned.astype(jnp.bfloat16).reshape(
                ROWS, ROWS, turned.shape[1]
            )


def dress(groups, place, tile_of, tile_mask, tiles, lambda_amps, swap):
    owners = len(tiles)
    pairs, tile_rows, cols = lambda_amps.shape[2:]
    rows = tile_rows // owners
    smem = pl.BlockSpec(memory_space=pltpu.SMEM)
    vmem = pl.BlockSpec(memory_space=pltpu.VMEM)
    count = sum(len(group) for group in groups)
    return pl.pallas_call(
        functools.partial(dress_kernel, owners, rows, groups),
        in_specs=[smem] * 3 + [vmem] * (owners + 2),
        out_specs=[vmem] * len(groups),
        out_shape=[
            jax.ShapeDtypeStruct((len(group), ROWS, pairs, cols), jnp.bfloat16)
            for group in groups
        ],
        scratch_shapes=[
            pltpu.VMEM((owners, count * ROWS, 2 * tile_rows), jnp.bfloat16),
            pltpu.VMEM((pairs // ROWS, count, ROWS * ROWS, cols), jnp.bfloat16),
        ],
        compiler_params=pltpu.CompilerParams(vmem_limit_bytes=VMEM_BYTES),
        cost_estimate=pl.CostEstimate(
            flops=2 * pairs * count * ROWS * tile_rows * cols,
            bytes_accessed=3 * pairs * tile_rows * cols,
            transcendentals=0,
        ),
    )(
        in_smem(place),
        in_smem(tile_of),
        in_smem(jnp.swapaxes(tile_mask, 2, 3)),
        tiles[0],
        *tiles[2:],
        tiles[1],
        lambda_amps,
        swap,
    )


def finish_blocks(indices, chunk, swap_ref, w_ref, inverse_ref, piece_refs, done, ys, then):
    groups, _, rows, _ = done.shape
    mine = groups * ROWS
    weights = w_ref[...]
    for a in range(rows):
        amps = jnp.concatenate([ref[index, a] for ref, index in zip(piece_refs, indices)], axis=0)
        cycle = jnp.dot(weights, amps, preferred_element_type=jnp.float32)
        total = amps[:mine].astype(jnp.float32) + cycle
        value = (total * inverse_ref[chunk * rows + a]).astype(jnp.bfloat16)
        for g in range(groups):
            ys[g, pl.ds(a * ROWS, ROWS), :] = value[g * ROWS : (g + 1) * ROWS]
    swap = swap_ref[...]
    for g in range(groups):
        turned = jnp.dot(swap, ys[g], preferred_element_type=jnp.float32)
        done[g] = turned.astype(jnp.bfloat16).reshape(done.shape[1:])
        then(g)


def early_kernel(indices, chunk, swap_ref, w_ref, inverse_ref, *refs):
    piece_refs, (done, ys) = refs[:-2], refs[-2:]
    finish_blocks(
        indices, chunk, swap_ref, w_ref, inverse_ref, piece_refs, done, ys, lambda g: None
    )


def last_kernel(indices, chunk, swap_ref, w_ref, inverse_ref, place_ref, *refs):
    ready_refs, piece_refs, (out_ref, done, ys, sems) = refs[:chunk], refs[chunk:-4], refs[-4:]
    groups, _, rows, _ = done.shape
    halves = 2 * groups // len(indices)
    me = place_ref[0]
    leaving = []

    def write(source, c, g):
        k, h = g // halves, g % halves
        copy = pltpu.make_async_copy(
            source.at[g],
            out_ref.at[me ^ k, 0, pl.ds(h * ROWS, ROWS), pl.ds(c * rows, rows), :],
            sems.at[c, g],
        )
        copy.start()
        leaving.append(copy)

    for c, ref in enumerate(ready_refs):
        for g in range(groups):
            write(ref, c, g)
    finish_blocks(
        indices,
        chunk,
        swap_ref,
        w_ref,
        inverse_ref,
        piece_refs,
        done,
        ys,
        lambda g: write(done, chunk, g),
    )
    for copy in leaving:
        copy.wait()


def finish(chunk, swap, weights, inverse, pieces, place=None, ready=(), shape=None):
    _, rows, pairs, cols = pieces[0][0].shape
    groups = len(pieces) // 2 * (pairs // ROWS)
    indices = [index for _, index in pieces]
    vmem, anywhere = pl.BlockSpec(memory_space=pltpu.VMEM), pl.BlockSpec(memory_space=pl.ANY)
    block = (groups, ROWS, rows, cols)
    ys = pltpu.VMEM((groups, ROWS * rows, cols), jnp.bfloat16)
    args, in_specs = [swap, weights, inverse], [vmem] * 3
    if shape is None:
        kernel = functools.partial(early_kernel, indices, chunk)
        out_spec, out_shape = vmem, jax.ShapeDtypeStruct(block, jnp.bfloat16)
        scratch = [ys]
    else:
        kernel = functools.partial(last_kernel, indices, chunk)
        out_spec, out_shape = anywhere, jax.ShapeDtypeStruct(shape, jnp.bfloat16)
        scratch = [pltpu.VMEM(block, jnp.bfloat16), ys]
        scratch += [pltpu.SemaphoreType.DMA((chunk + 1, groups))]
        args += [place, *ready]
        in_specs += [pl.BlockSpec(memory_space=pltpu.SMEM)] + [anywhere] * len(ready)
    return pl.pallas_call(
        kernel,
        in_specs=in_specs + [vmem] * len(pieces),
        out_specs=out_spec,
        out_shape=out_shape,
        scratch_shapes=scratch,
        compiler_params=pltpu.CompilerParams(vmem_limit_bytes=VMEM_BYTES),
        cost_estimate=pl.CostEstimate(flops=0, bytes_accessed=0, transcendentals=0),
    )(*args, *[piece for piece, _ in pieces])


def local_chunked(
    lambda_amps,
    integral_tiles,
    tile_of,
    tile_mask,
    pair_list,
    coupling,
    pair_gap,
    row_energy,
    col_energy,
):
    pairs, tile_rows, cols = lambda_amps.shape[2:]
    owners = lax.axis_size("pair")
    rows = tile_rows // owners
    chunks = rows // ROWS
    me = lax.axis_index("pair").astype(jnp.int32)
    sub = lax.axis_index("sub").astype(jnp.int32)
    place = jnp.stack([me, sub])

    def to_owner(value, k):
        return lax.ppermute(value, "pair", [(o, o ^ k) for o in range(owners)])

    def to_sibling(value):
        return lax.ppermute(value, "sub", [(0, 1), (1, 0)])

    def after(value, earlier):
        return value if earlier is None else lax.optimization_barrier((value, earlier))[0]

    tiles = [integral_tiles] + [to_owner(integral_tiles, k) for k in range(1, owners)]

    far = list(range(2, owners))
    lead, last = far[0], far[-1]
    groups = [((k, c),) for c in range(chunks) for k in far[::-1]]
    groups += [tuple((k, c) for c in range(chunks)) for k in (1, 0)]
    held, swap = hold(lambda_amps)
    sent = dict(zip(groups, dress(groups, place, tile_of, tile_mask, tiles, held, swap)))
    weights, inverse = make_weights(
        after(pair_list, sent[groups[0]]), coupling, pair_gap, place, row_energy, col_energy
    )
    own, near = sent[groups[-1]], to_owner(sent[groups[-2]], 1)

    @functools.cache
    def landed(k, c):
        earlier = landed(k, c - 1) if c and k == lead else None
        return to_owner(after(sent[((k, c),)], earlier), k)

    @functools.cache
    def passed(k, c):
        earlier = passed(last, c - 1) if c else (weights, inverse) if k == lead else None
        return to_sibling(after(landed(k, c), earlier))

    @functools.cache
    def passed_whole(k):
        return to_sibling(after(near, (weights, inverse, passed(lead, 0))) if k else after(own, near))

    chunk_pieces = []
    for c in range(chunks - 1, -1, -1):
        pieces = [(own, c), (near, c)] + [(landed(k, c), 0) for k in far]
        pieces += [(passed_whole(k), c) for k in (0, 1)] + [(passed(k, c), 0) for k in far]
        chunk_pieces.insert(0, pieces)
    ready = [finish(c, swap, weights, inverse, chunk_pieces[c]) for c in range(chunks - 1)]
    shape = (owners, 1, pairs, rows, cols)
    return finish(chunks - 1, swap, weights, inverse, chunk_pieces[-1], place, ready, shape)


def solution(mesh):
    placed = (
        P(("mol", "pair"), "sub", None, None, "tile"),
        P(("mol", "pair"), None, None),
        P(("mol", "pair"), "sub", None),
        P(("mol", "pair"), "sub", None, "tile"),
        P("mol", None),
        P("mol", None),
        P("mol", "sub", None),
        P(("mol", "pair")),
        P(("mol", "tile")),
    )
    owners, subs = mesh.shape["pair"], mesh.shape["sub"]

    def local(*args):
        tile_rows, cols = args[0].shape[3:]
        rows = tile_rows // owners
        power = owners >= 4 and owners & (owners - 1) == 0
        fits = rows % ROWS == 0 and cols % LANES == 0 and args[1].shape[0] == 1
        if power and fits and subs == 2 and args[0].shape[2] % ROWS == 0:
            return local_chunked(*args)
        return local_general(*args)

    return jax.shard_map(
        local,
        mesh=mesh,
        in_specs=placed,
        out_specs=P("mol", "sub", None, "pair", "tile"),
        check_vma=False,
    )
```

```python
import functools
import math

import jax
import jax.numpy as jnp
from jax import lax
from jax.experimental import pallas as pl
from jax.experimental.pallas import tpu as pltpu
from jax.sharding import PartitionSpec as P

ROWS = 16
LANES = 128
VMEM_BYTES = 24 * 2**20


def column_tables(coupling, col_pairs):
    left_table = jnp.take(coupling.T, col_pairs[:, 0], axis=0).T
    right_table = jnp.take(coupling.T, col_pairs[:, 1], axis=0).T
    return (left_table, right_table)


def cycle_rows(left_table, right_table, row_pairs):
    left_part = jnp.take(left_table, row_pairs[:, 0], axis=0)
    right_part = jnp.take(right_table, row_pairs[:, 1], axis=0)
    return (left_part * right_part).astype(jnp.bfloat16)


def cycle_all(coupling, pair_list, col_pairs, flat_rhs):
    total_pairs = pair_list.shape[0]
    step_rows = math.gcd(total_pairs, 512)
    row_blocks = pair_list.reshape(total_pairs // step_rows, step_rows, 2)
    left_table, right_table = column_tables(coupling, col_pairs)

    def one_block(row_pairs):
        weights = cycle_rows(left_table, right_table, row_pairs)
        return jnp.dot(weights, flat_rhs, preferred_element_type=jnp.float32)

    return lax.map(one_block, row_blocks).reshape(total_pairs, -1)


def local_general(
    lambda_amps,
    integral_tiles,
    tile_of,
    tile_mask,
    pair_list,
    coupling,
    pair_gap,
    row_energy,
    col_energy,
):
    pair_count = lambda_amps.shape[2]
    tile_rows = lambda_amps.shape[3]
    col_count = lambda_amps.shape[4]
    owners = lax.axis_size("pair")
    sub_count = lax.axis_size("sub")
    wanted = tile_of.reshape(pair_count)
    empty_tiles = jnp.zeros((pair_count, tile_rows, tile_rows), integral_tiles.dtype)
    shard_piece = lax.all_gather(integral_tiles, "pair", axis=0, tiled=True)
    inside = (wanted >= 0) & (wanted < shard_piece.shape[0])
    taken_rows = shard_piece[jnp.clip(wanted, 0, shard_piece.shape[0] - 1)]
    chosen = jnp.where(inside[:, None, None], taken_rows, empty_tiles)
    amplitudes = lambda_amps.reshape(pair_count, tile_rows, col_count)
    ladder = jnp.einsum("pac,pcb->pab", chosen, amplitudes, preferred_element_type=jnp.float32)
    blocks = tile_mask.shape[3]
    keep_mask = tile_mask.reshape(pair_count, 1, blocks, 1).astype(jnp.float32)
    ladder = (
        ladder.reshape(pair_count, tile_rows, blocks, col_count // blocks) * keep_mask
    ).reshape(pair_count, tile_rows, col_count)
    dressed = (amplitudes.astype(jnp.float32) + ladder).astype(jnp.bfloat16)
    dressed = dressed.reshape(1, 1, pair_count, tile_rows, col_count)
    relayed = lax.all_to_all(dressed, "pair", split_axis=3, concat_axis=0, tiled=True)
    sub_index = lax.axis_index("sub")
    block_ids = jnp.arange(owners, dtype=jnp.int32) * sub_count + sub_index
    mine_ids = (
        block_ids[:, None] * pair_count + jnp.arange(pair_count, dtype=jnp.int32)[None, :]
    ).reshape(-1)
    col_pairs = pair_list[mine_ids]
    flat_rhs = relayed.reshape(owners * pair_count, -1)
    partial_value = cycle_all(coupling, pair_list, col_pairs, flat_rhs)
    partial_value = partial_value.reshape(
        owners, sub_count, pair_count, relayed.shape[3], col_count
    )
    cycle_term = lax.psum_scatter(
        partial_value.astype(jnp.bfloat16), "sub", scatter_dimension=1, tiled=True
    ).astype(jnp.float32)
    total_sum = relayed.astype(jnp.float32) + cycle_term
    energy_gap = (
        pair_gap[:, :, :, None, None]
        + row_energy[None, None, None, :, None]
        + col_energy[None, None, None, None, :]
    )
    return (-total_sum / energy_gap).astype(jnp.bfloat16)


def in_hbm(value):
    return pltpu.with_memory_space_constraint(value, pltpu.HBM)


def in_smem(value):
    return pltpu.with_memory_space_constraint(value, pltpu.SMEM)


def one_hot(hits):
    return jnp.where(hits, 1.0, 0.0).astype(jnp.bfloat16)


def square_iotas(size):
    return (lax.broadcasted_iota(jnp.int32, (size, size), axis) for axis in range(2))


def split3(value):
    high = value.astype(jnp.bfloat16)
    rest = value - high.astype(jnp.float32)
    mid = rest.astype(jnp.bfloat16)
    low = (rest - mid.astype(jnp.float32)).astype(jnp.bfloat16)
    return high, mid, low


def pick_columns(value, columns):
    high, mid, low = (
        jnp.dot(part, columns, preferred_element_type=jnp.float32) for part in split3(value)
    )
    return high + (mid + low)


def pick_rows(columns, value):
    dims = (((0,), (0,)), ((), ()))
    high, mid, low = (
        lax.dot_general(columns, part, dims, preferred_element_type=jnp.float32)
        for part in split3(value)
    )
    return high + (mid + low)


def hold_kernel(lam_ref, held_ref, swap_ref, sems):
    step = lam_ref.shape[2] // sems.shape[0]
    copies = []
    for i in range(sems.shape[0]):
        block = pl.ds(i * step, step)
        copy = pltpu.make_async_copy(
            lam_ref.at[:, :, block], held_ref.at[:, :, block], sems.at[i]
        )
        copy.start()
        copies.append(copy)
    to, frm = square_iotas(ROWS * ROWS)
    swap_ref[...] = one_hot(to == (frm % ROWS) * ROWS + frm // ROWS)
    for copy in copies:
        copy.wait()


def hold(lambda_amps):
    anywhere = pl.BlockSpec(memory_space=pl.ANY)
    return pl.pallas_call(
        hold_kernel,
        in_specs=[anywhere],
        out_specs=[anywhere, pl.BlockSpec(memory_space=pltpu.VMEM)],
        out_shape=[
            jax.ShapeDtypeStruct(lambda_amps.shape, lambda_amps.dtype),
            jax.ShapeDtypeStruct((ROWS * ROWS, ROWS * ROWS), jnp.bfloat16),
        ],
        scratch_shapes=[pltpu.SemaphoreType.DMA((8,))],
        compiler_params=pltpu.CompilerParams(vmem_limit_bytes=VMEM_BYTES),
        cost_estimate=pl.CostEstimate(
            flops=0, bytes_accessed=4 * lambda_amps.size, transcendentals=0
        ),
    )(in_hbm(lambda_amps))


def weights_kernel(
    pair_ref, coupling_ref, gap_ref, place_ref, row_ref, col_ref, w_ref, inverse_ref, full
):
    total = pair_ref.shape[1]
    depth = coupling_ref.shape[0]
    owners, _, pairs = gap_ref.shape
    me, sub = place_ref[0], place_ref[1]
    orbital = lax.broadcasted_iota(jnp.int32, (depth, total), 0)
    coupling = coupling_ref[...]
    product = None
    for side in range(2):
        columns = one_hot(orbital == pair_ref[side : side + 1, :])
        picked = pick_rows(columns, pick_columns(coupling, columns))
        product = picked if product is None else product * picked
    frm, to = square_iotas(total)
    block, within = to // pairs, to % pairs
    source = ((me ^ (block % owners)) * 2 + (sub ^ (block // owners))) * pairs + within
    full[...] = jnp.dot(
        product.astype(jnp.bfloat16), one_hot(frm == source), preferred_element_type=jnp.float32
    )
    row, column = square_iotas(pairs)
    for k in range(owners):
        start = pl.multiple_of(((me ^ k) * 2 + sub) * pairs, pairs)
        rows = pl.ds(k * pairs, pairs)
        w_ref[rows, :] = full[pl.ds(start, pairs), :].astype(jnp.bfloat16)
        gap = jnp.sum(jnp.where(row == column, gap_ref[me ^ k], 0.0), axis=1, keepdims=True)
        for a in range(inverse_ref.shape[0]):
            inverse_ref[a, rows, :] = -1.0 / ((gap + row_ref[a]) + col_ref[...])


def make_weights(pair_list, coupling, pair_gap, place, row_energy, col_energy):
    owners, _, pairs = pair_gap.shape
    total = pair_list.shape[0]
    mine = owners * pairs
    rows, cols = row_energy.shape[0], col_energy.shape[0]
    smem = pl.BlockSpec(memory_space=pltpu.SMEM)
    vmem = pl.BlockSpec(memory_space=pltpu.VMEM)
    return pl.pallas_call(
        weights_kernel,
        in_specs=[vmem, vmem, vmem, smem, smem, vmem],
        out_specs=[vmem, vmem],
        out_shape=[
            jax.ShapeDtypeStruct((mine, total), jnp.bfloat16),
            jax.ShapeDtypeStruct((rows, mine, cols), jnp.float32),
        ],
        scratch_shapes=[pltpu.VMEM((total, total), jnp.float32)],
        compiler_params=pltpu.CompilerParams(vmem_limit_bytes=VMEM_BYTES),
        cost_estimate=pl.CostEstimate(
            flops=12 * total * coupling.size, bytes_accessed=4 * coupling.size, transcendentals=0
        ),
    )(pair_list.T, coupling, pair_gap, place, row_energy, col_energy.reshape(1, cols))


def dress_kernel(owners, rows, groups, place_ref, tile_of_ref, mask_ref, *refs):
    tile_refs, lam_ref = (refs[0], refs[owners - 1], *refs[1 : owners - 1]), refs[owners]
    swap_ref = refs[owners + 1]
    out_refs = refs[owners + 2 : -2]
    tiles, stage = refs[-2:]
    me = place_ref[0]
    flat = [(k, c, out, j) for out, group in zip(out_refs, groups) for j, (k, c) in enumerate(group)]
    starts = [pl.multiple_of((me ^ k) * rows + c * ROWS, ROWS) for k, c, _, _ in flat]
    tile_rows, cols = lam_ref.shape[3:]
    row = lax.broadcasted_iota(jnp.int32, (ROWS, tile_rows), 0)
    column = lax.broadcasted_iota(jnp.int32, (ROWS, tile_rows), 1)
    for n, start in enumerate(starts):
        block = pl.ds(n * ROWS, ROWS)
        own_row = one_hot(column == row + start)
        for k in range(owners):
            tiles[k, block, :tile_rows] = tile_refs[k][0, pl.ds(start, ROWS), :]
            tiles[k, block, tile_rows:] = own_row
    swap = swap_ref[...]
    parts = mask_ref.shape[2]
    width = cols // parts
    for g in range(lam_ref.shape[2] // ROWS):
        for i in range(ROWS):
            pair = g * ROWS + i
            amps = lam_ref[0, 0, pair]
            kept = [
                amps[:, part * width : (part + 1) * width]
                * mask_ref[0, 0, part, pair].astype(jnp.float32).astype(jnp.bfloat16)
                for part in range(parts)
            ]
            both = jnp.concatenate([jnp.concatenate(kept, axis=1), amps], axis=0)
            full = jnp.dot(
                tiles[tile_of_ref[0, 0, pair] ^ me], both, preferred_element_type=jnp.float32
            ).astype(jnp.bfloat16)
            for n in range(len(flat)):
                stage[g, n, pl.ds(i * ROWS, ROWS), :] = full[n * ROWS : (n + 1) * ROWS]
        for n, (_, _, out, j) in enumerate(flat):
            turned = jnp.dot(swap, stage[g, n], preferred_element_type=jnp.float32)
            out[j, :, pl.ds(g * ROWS, ROWS), :] = turned.astype(jnp.bfloat16).reshape(
                ROWS, ROWS, turned.shape[1]
            )


def dress(groups, place, tile_of, tile_mask, tiles, lambda_amps, swap):
    owners = len(tiles)
    pairs, tile_rows, cols = lambda_amps.shape[2:]
    rows = tile_rows // owners
    smem = pl.BlockSpec(memory_space=pltpu.SMEM)
    vmem = pl.BlockSpec(memory_space=pltpu.VMEM)
    count = sum(len(group) for group in groups)
    return pl.pallas_call(
        functools.partial(dress_kernel, owners, rows, groups),
        in_specs=[smem] * 3 + [vmem] * (owners + 2),
        out_specs=[vmem] * len(groups),
        out_shape=[
            jax.ShapeDtypeStruct((len(group), ROWS, pairs, cols), jnp.bfloat16)
            for group in groups
        ],
        scratch_shapes=[
            pltpu.VMEM((owners, count * ROWS, 2 * tile_rows), jnp.bfloat16),
            pltpu.VMEM((pairs // ROWS, count, ROWS * ROWS, cols), jnp.bfloat16),
        ],
        compiler_params=pltpu.CompilerParams(vmem_limit_bytes=VMEM_BYTES),
        cost_estimate=pl.CostEstimate(
            flops=2 * pairs * count * ROWS * tile_rows * cols,
            bytes_accessed=3 * pairs * tile_rows * cols,
            transcendentals=0,
        ),
    )(
        in_smem(place),
        in_smem(tile_of),
        in_smem(jnp.swapaxes(tile_mask, 2, 3)),
        tiles[0],
        *tiles[2:],
        tiles[1],
        lambda_amps,
        swap,
    )


def finish_blocks(indices, chunk, swap_ref, w_ref, inverse_ref, piece_refs, done, ys, then):
    groups, _, rows, _ = done.shape
    mine = groups * ROWS
    weights = w_ref[...]
    for a in range(rows):
        amps = jnp.concatenate([ref[index, a] for ref, index in zip(piece_refs, indices)], axis=0)
        cycle = jnp.dot(weights, amps, preferred_element_type=jnp.float32)
        total = amps[:mine].astype(jnp.float32) + cycle
        value = (total * inverse_ref[chunk * rows + a]).astype(jnp.bfloat16)
        for g in range(groups):
            ys[g, pl.ds(a * ROWS, ROWS), :] = value[g * ROWS : (g + 1) * ROWS]
    swap = swap_ref[...]
    for g in range(groups):
        turned = jnp.dot(swap, ys[g], preferred_element_type=jnp.float32)
        done[g] = turned.astype(jnp.bfloat16).reshape(done.shape[1:])
        then(g)


def early_kernel(indices, chunk, swap_ref, w_ref, inverse_ref, *refs):
    piece_refs, (done, ys) = refs[:-2], refs[-2:]
    finish_blocks(
        indices, chunk, swap_ref, w_ref, inverse_ref, piece_refs, done, ys, lambda g: None
    )


def last_kernel(indices, chunk, swap_ref, w_ref, inverse_ref, place_ref, *refs):
    ready_refs, piece_refs, (out_ref, done, ys, sems) = refs[:chunk], refs[chunk:-4], refs[-4:]
    groups, _, rows, _ = done.shape
    halves = 2 * groups // len(indices)
    me = place_ref[0]
    leaving = []

    def write(source, c, g):
        k, h = g // halves, g % halves
        copy = pltpu.make_async_copy(
            source.at[g],
            out_ref.at[me ^ k, 0, pl.ds(h * ROWS, ROWS), pl.ds(c * rows, rows), :],
            sems.at[c, g],
        )
        copy.start()
        leaving.append(copy)

    for c, ref in enumerate(ready_refs):
        for g in range(groups):
            write(ref, c, g)
    finish_blocks(
        indices,
        chunk,
        swap_ref,
        w_ref,
        inverse_ref,
        piece_refs,
        done,
        ys,
        lambda g: write(done, chunk, g),
    )
    for copy in leaving:
        copy.wait()


def finish(chunk, swap, weights, inverse, pieces, place=None, ready=(), shape=None):
    _, rows, pairs, cols = pieces[0][0].shape
    groups = len(pieces) // 2 * (pairs // ROWS)
    indices = [index for _, index in pieces]
    vmem, anywhere = pl.BlockSpec(memory_space=pltpu.VMEM), pl.BlockSpec(memory_space=pl.ANY)
    block = (groups, ROWS, rows, cols)
    ys = pltpu.VMEM((groups, ROWS * rows, cols), jnp.bfloat16)
    args, in_specs = [swap, weights, inverse], [vmem] * 3
    if shape is None:
        kernel = functools.partial(early_kernel, indices, chunk)
        out_spec, out_shape = vmem, jax.ShapeDtypeStruct(block, jnp.bfloat16)
        scratch = [ys]
    else:
        kernel = functools.partial(last_kernel, indices, chunk)
        out_spec, out_shape = anywhere, jax.ShapeDtypeStruct(shape, jnp.bfloat16)
        scratch = [pltpu.VMEM(block, jnp.bfloat16), ys]
        scratch += [pltpu.SemaphoreType.DMA((chunk + 1, groups))]
        args += [place, *ready]
        in_specs += [pl.BlockSpec(memory_space=pltpu.SMEM)] + [anywhere] * len(ready)
    return pl.pallas_call(
        kernel,
        in_specs=in_specs + [vmem] * len(pieces),
        out_specs=out_spec,
        out_shape=out_shape,
        scratch_shapes=scratch,
        compiler_params=pltpu.CompilerParams(vmem_limit_bytes=VMEM_BYTES),
        cost_estimate=pl.CostEstimate(flops=0, bytes_accessed=0, transcendentals=0),
    )(*args, *[piece for piece, _ in pieces])


def local_chunked(
    lambda_amps,
    integral_tiles,
    tile_of,
    tile_mask,
    pair_list,
    coupling,
    pair_gap,
    row_energy,
    col_energy,
):
    pairs, tile_rows, cols = lambda_amps.shape[2:]
    owners = lax.axis_size("pair")
    rows = tile_rows // owners
    chunks = rows // ROWS
    me = lax.axis_index("pair").astype(jnp.int32)
    sub = lax.axis_index("sub").astype(jnp.int32)
    place = jnp.stack([me, sub])

    def to_owner(value, k):
        return lax.ppermute(value, "pair", [(o, o ^ k) for o in range(owners)])

    def to_sibling(value):
        return lax.ppermute(value, "sub", [(0, 1), (1, 0)])

    def after(value, earlier):
        return value if earlier is None else lax.optimization_barrier((value, earlier))[0]

    tiles = [integral_tiles] + [to_owner(integral_tiles, k) for k in range(1, owners)]

    far = list(range(2, owners))
    last = far[-1]
    groups = [((k, c),) for c in range(chunks) for k in far[::-1]]
    groups += [tuple((k, c) for c in range(chunks)) for k in (1, 0)]
    held, swap = hold(lambda_amps)
    sent = dict(zip(groups, dress(groups, place, tile_of, tile_mask, tiles, held, swap)))
    weights, inverse = make_weights(
        after(pair_list, sent[groups[0]]), coupling, pair_gap, place, row_energy, col_energy
    )
    own, near = sent[groups[-1]], to_owner(sent[groups[-2]], 1)

    @functools.cache
    def landed(k, c):
        earlier = None
        if c:
            earlier = landed(k, c - 1) if k == last else passed(last, c - 1)
        return to_owner(after(sent[((k, c),)], earlier), k)

    @functools.cache
    def passed(k, c):
        earlier = passed(far[0], c - 1) if c else (weights, inverse) if k == last else None
        return to_sibling(after(landed(k, c), earlier))

    @functools.cache
    def passed_whole(k):
        return to_sibling(after(near, (weights, inverse, passed(last, 0))) if k else after(own, near))

    chunk_pieces = []
    for c in range(chunks - 1, -1, -1):
        pieces = [(own, c), (near, c)] + [(landed(k, c), 0) for k in far]
        pieces += [(passed_whole(k), c) for k in (0, 1)] + [(passed(k, c), 0) for k in far]
        chunk_pieces.insert(0, pieces)
    ready = [finish(c, swap, weights, inverse, chunk_pieces[c]) for c in range(chunks - 1)]
    shape = (owners, 1, pairs, rows, cols)
    return finish(chunks - 1, swap, weights, inverse, chunk_pieces[-1], place, ready, shape)


def solution(mesh):
    placed = (
        P(("mol", "pair"), "sub", None, None, "tile"),
        P(("mol", "pair"), None, None),
        P(("mol", "pair"), "sub", None),
        P(("mol", "pair"), "sub", None, "tile"),
        P("mol", None),
        P("mol", None),
        P("mol", "sub", None),
        P(("mol", "pair")),
        P(("mol", "tile")),
    )
    owners, subs = mesh.shape["pair"], mesh.shape["sub"]

    def local(*args):
        tile_rows, cols = args[0].shape[3:]
        rows = tile_rows // owners
        power = owners >= 4 and owners & (owners - 1) == 0
        fits = rows % ROWS == 0 and cols % LANES == 0 and args[1].shape[0] == 1
        if power and fits and subs == 2 and args[0].shape[2] % ROWS == 0:
            return local_chunked(*args)
        return local_general(*args)

    return jax.shard_map(
        local,
        mesh=mesh,
        in_specs=placed,
        out_specs=P("mol", "sub", None, "pair", "tile"),
        check_vma=False,
    )
```

```python
import functools
import math

import jax
import jax.numpy as jnp
from jax import lax
from jax.experimental import pallas as pl
from jax.experimental.pallas import tpu as pltpu
from jax.sharding import PartitionSpec as P

ROWS = 16
LANES = 128
VMEM_BYTES = 24 * 2**20


def column_tables(coupling, col_pairs):
    left_table = jnp.take(coupling.T, col_pairs[:, 0], axis=0).T
    right_table = jnp.take(coupling.T, col_pairs[:, 1], axis=0).T
    return (left_table, right_table)


def cycle_rows(left_table, right_table, row_pairs):
    left_part = jnp.take(left_table, row_pairs[:, 0], axis=0)
    right_part = jnp.take(right_table, row_pairs[:, 1], axis=0)
    return (left_part * right_part).astype(jnp.bfloat16)


def cycle_all(coupling, pair_list, col_pairs, flat_rhs):
    total_pairs = pair_list.shape[0]
    step_rows = math.gcd(total_pairs, 512)
    row_blocks = pair_list.reshape(total_pairs // step_rows, step_rows, 2)
    left_table, right_table = column_tables(coupling, col_pairs)

    def one_block(row_pairs):
        weights = cycle_rows(left_table, right_table, row_pairs)
        return jnp.dot(weights, flat_rhs, preferred_element_type=jnp.float32)

    return lax.map(one_block, row_blocks).reshape(total_pairs, -1)


def local_general(
    lambda_amps,
    integral_tiles,
    tile_of,
    tile_mask,
    pair_list,
    coupling,
    pair_gap,
    row_energy,
    col_energy,
):
    pair_count = lambda_amps.shape[2]
    tile_rows = lambda_amps.shape[3]
    col_count = lambda_amps.shape[4]
    owners = lax.axis_size("pair")
    sub_count = lax.axis_size("sub")
    wanted = tile_of.reshape(pair_count)
    empty_tiles = jnp.zeros((pair_count, tile_rows, tile_rows), integral_tiles.dtype)
    shard_piece = lax.all_gather(integral_tiles, "pair", axis=0, tiled=True)
    inside = (wanted >= 0) & (wanted < shard_piece.shape[0])
    taken_rows = shard_piece[jnp.clip(wanted, 0, shard_piece.shape[0] - 1)]
    chosen = jnp.where(inside[:, None, None], taken_rows, empty_tiles)
    amplitudes = lambda_amps.reshape(pair_count, tile_rows, col_count)
    ladder = jnp.einsum("pac,pcb->pab", chosen, amplitudes, preferred_element_type=jnp.float32)
    blocks = tile_mask.shape[3]
    keep_mask = tile_mask.reshape(pair_count, 1, blocks, 1).astype(jnp.float32)
    ladder = (
        ladder.reshape(pair_count, tile_rows, blocks, col_count // blocks) * keep_mask
    ).reshape(pair_count, tile_rows, col_count)
    dressed = (amplitudes.astype(jnp.float32) + ladder).astype(jnp.bfloat16)
    dressed = dressed.reshape(1, 1, pair_count, tile_rows, col_count)
    relayed = lax.all_to_all(dressed, "pair", split_axis=3, concat_axis=0, tiled=True)
    sub_index = lax.axis_index("sub")
    block_ids = jnp.arange(owners, dtype=jnp.int32) * sub_count + sub_index
    mine_ids = (
        block_ids[:, None] * pair_count + jnp.arange(pair_count, dtype=jnp.int32)[None, :]
    ).reshape(-1)
    col_pairs = pair_list[mine_ids]
    flat_rhs = relayed.reshape(owners * pair_count, -1)
    partial_value = cycle_all(coupling, pair_list, col_pairs, flat_rhs)
    partial_value = partial_value.reshape(
        owners, sub_count, pair_count, relayed.shape[3], col_count
    )
    cycle_term = lax.psum_scatter(
        partial_value.astype(jnp.bfloat16), "sub", scatter_dimension=1, tiled=True
    ).astype(jnp.float32)
    total_sum = relayed.astype(jnp.float32) + cycle_term
    energy_gap = (
        pair_gap[:, :, :, None, None]
        + row_energy[None, None, None, :, None]
        + col_energy[None, None, None, None, :]
    )
    return (-total_sum / energy_gap).astype(jnp.bfloat16)


def in_hbm(value):
    return pltpu.with_memory_space_constraint(value, pltpu.HBM)


def in_smem(value):
    return pltpu.with_memory_space_constraint(value, pltpu.SMEM)


def one_hot(hits):
    return jnp.where(hits, 1.0, 0.0).astype(jnp.bfloat16)


def square_iotas(size):
    return (lax.broadcasted_iota(jnp.int32, (size, size), axis) for axis in range(2))


def split3(value):
    high = value.astype(jnp.bfloat16)
    rest = value - high.astype(jnp.float32)
    mid = rest.astype(jnp.bfloat16)
    low = (rest - mid.astype(jnp.float32)).astype(jnp.bfloat16)
    return high, mid, low


def pick_columns(value, columns):
    high, mid, low = (
        jnp.dot(part, columns, preferred_element_type=jnp.float32) for part in split3(value)
    )
    return high + (mid + low)


def pick_rows(columns, value):
    dims = (((0,), (0,)), ((), ()))
    high, mid, low = (
        lax.dot_general(columns, part, dims, preferred_element_type=jnp.float32)
        for part in split3(value)
    )
    return high + (mid + low)


def hold_kernel(lam_ref, held_ref, swap_ref, sems):
    step = lam_ref.shape[2] // sems.shape[0]
    copies = []
    for i in range(sems.shape[0]):
        block = pl.ds(i * step, step)
        copy = pltpu.make_async_copy(
            lam_ref.at[:, :, block], held_ref.at[:, :, block], sems.at[i]
        )
        copy.start()
        copies.append(copy)
    to, frm = square_iotas(ROWS * ROWS)
    swap_ref[...] = one_hot(to == (frm % ROWS) * ROWS + frm // ROWS)
    for copy in copies:
        copy.wait()


def hold(lambda_amps):
    anywhere = pl.BlockSpec(memory_space=pl.ANY)
    return pl.pallas_call(
        hold_kernel,
        in_specs=[anywhere],
        out_specs=[anywhere, pl.BlockSpec(memory_space=pltpu.VMEM)],
        out_shape=[
            jax.ShapeDtypeStruct(lambda_amps.shape, lambda_amps.dtype),
            jax.ShapeDtypeStruct((ROWS * ROWS, ROWS * ROWS), jnp.bfloat16),
        ],
        scratch_shapes=[pltpu.SemaphoreType.DMA((8,))],
        compiler_params=pltpu.CompilerParams(vmem_limit_bytes=VMEM_BYTES),
        cost_estimate=pl.CostEstimate(
            flops=0, bytes_accessed=4 * lambda_amps.size, transcendentals=0
        ),
    )(in_hbm(lambda_amps))


def weights_kernel(
    pair_ref, coupling_ref, gap_ref, place_ref, row_ref, col_ref, w_ref, inverse_ref, full
):
    total = pair_ref.shape[1]
    depth = coupling_ref.shape[0]
    owners, _, pairs = gap_ref.shape
    me, sub = place_ref[0], place_ref[1]
    orbital = lax.broadcasted_iota(jnp.int32, (depth, total), 0)
    coupling = coupling_ref[...]
    product = None
    for side in range(2):
        columns = one_hot(orbital == pair_ref[side : side + 1, :])
        picked = pick_rows(columns, pick_columns(coupling, columns))
        product = picked if product is None else product * picked
    frm, to = square_iotas(total)
    block, within = to // pairs, to % pairs
    source = ((me ^ (block % owners)) * 2 + (sub ^ (block // owners))) * pairs + within
    full[...] = jnp.dot(
        product.astype(jnp.bfloat16), one_hot(frm == source), preferred_element_type=jnp.float32
    )
    row, column = square_iotas(pairs)
    for k in range(owners):
        start = pl.multiple_of(((me ^ k) * 2 + sub) * pairs, pairs)
        rows = pl.ds(k * pairs, pairs)
        w_ref[rows, :] = full[pl.ds(start, pairs), :].astype(jnp.bfloat16)
        gap = jnp.sum(jnp.where(row == column, gap_ref[me ^ k], 0.0), axis=1, keepdims=True)
        for a in range(inverse_ref.shape[0]):
            inverse_ref[a, rows, :] = -1.0 / ((gap + row_ref[a]) + col_ref[...])


def make_weights(pair_list, coupling, pair_gap, place, row_energy, col_energy):
    owners, _, pairs = pair_gap.shape
    total = pair_list.shape[0]
    mine = owners * pairs
    rows, cols = row_energy.shape[0], col_energy.shape[0]
    smem = pl.BlockSpec(memory_space=pltpu.SMEM)
    vmem = pl.BlockSpec(memory_space=pltpu.VMEM)
    return pl.pallas_call(
        weights_kernel,
        in_specs=[vmem, vmem, vmem, smem, smem, vmem],
        out_specs=[vmem, vmem],
        out_shape=[
            jax.ShapeDtypeStruct((mine, total), jnp.bfloat16),
            jax.ShapeDtypeStruct((rows, mine, cols), jnp.float32),
        ],
        scratch_shapes=[pltpu.VMEM((total, total), jnp.float32)],
        compiler_params=pltpu.CompilerParams(vmem_limit_bytes=VMEM_BYTES),
        cost_estimate=pl.CostEstimate(
            flops=12 * total * coupling.size, bytes_accessed=4 * coupling.size, transcendentals=0
        ),
    )(pair_list.T, coupling, pair_gap, place, row_energy, col_energy.reshape(1, cols))


def dress_kernel(owners, rows, groups, place_ref, tile_of_ref, mask_ref, *refs):
    tile_refs, lam_ref = (refs[0], refs[owners - 1], *refs[1 : owners - 1]), refs[owners]
    swap_ref = refs[owners + 1]
    out_refs = refs[owners + 2 : -2]
    tiles, stage = refs[-2:]
    me = place_ref[0]
    flat = [(k, c, out, j) for out, group in zip(out_refs, groups) for j, (k, c) in enumerate(group)]
    starts = [pl.multiple_of((me ^ k) * rows + c * ROWS, ROWS) for k, c, _, _ in flat]
    tile_rows, cols = lam_ref.shape[3:]
    row = lax.broadcasted_iota(jnp.int32, (ROWS, tile_rows), 0)
    column = lax.broadcasted_iota(jnp.int32, (ROWS, tile_rows), 1)
    for n, start in enumerate(starts):
        block = pl.ds(n * ROWS, ROWS)
        own_row = one_hot(column == row + start)
        for k in range(owners):
            tiles[k, block, :tile_rows] = tile_refs[k][0, pl.ds(start, ROWS), :]
            tiles[k, block, tile_rows:] = own_row
    swap = swap_ref[...]
    parts = mask_ref.shape[2]
    width = cols // parts
    for g in range(lam_ref.shape[2] // ROWS):
        for i in range(ROWS):
            pair = g * ROWS + i
            amps = lam_ref[0, 0, pair]
            kept = [
                amps[:, part * width : (part + 1) * width]
                * mask_ref[0, 0, part, pair].astype(jnp.float32).astype(jnp.bfloat16)
                for part in range(parts)
            ]
            both = jnp.concatenate([jnp.concatenate(kept, axis=1), amps], axis=0)
            full = jnp.dot(
                tiles[tile_of_ref[0, 0, pair] ^ me], both, preferred_element_type=jnp.float32
            ).astype(jnp.bfloat16)
            for n in range(len(flat)):
                stage[g, n, pl.ds(i * ROWS, ROWS), :] = full[n * ROWS : (n + 1) * ROWS]
        for n, (_, _, out, j) in enumerate(flat):
            turned = jnp.dot(swap, stage[g, n], preferred_element_type=jnp.float32)
            out[j, :, pl.ds(g * ROWS, ROWS), :] = turned.astype(jnp.bfloat16).reshape(
                ROWS, ROWS, turned.shape[1]
            )


def dress(groups, place, tile_of, tile_mask, tiles, lambda_amps, swap):
    owners = len(tiles)
    pairs, tile_rows, cols = lambda_amps.shape[2:]
    rows = tile_rows // owners
    smem = pl.BlockSpec(memory_space=pltpu.SMEM)
    vmem = pl.BlockSpec(memory_space=pltpu.VMEM)
    count = sum(len(group) for group in groups)
    return pl.pallas_call(
        functools.partial(dress_kernel, owners, rows, groups),
        in_specs=[smem] * 3 + [vmem] * (owners + 2),
        out_specs=[vmem] * len(groups),
        out_shape=[
            jax.ShapeDtypeStruct((len(group), ROWS, pairs, cols), jnp.bfloat16)
            for group in groups
        ],
        scratch_shapes=[
            pltpu.VMEM((owners, count * ROWS, 2 * tile_rows), jnp.bfloat16),
            pltpu.VMEM((pairs // ROWS, count, ROWS * ROWS, cols), jnp.bfloat16),
        ],
        compiler_params=pltpu.CompilerParams(vmem_limit_bytes=VMEM_BYTES),
        cost_estimate=pl.CostEstimate(
            flops=2 * pairs * count * ROWS * tile_rows * cols,
            bytes_accessed=3 * pairs * tile_rows * cols,
            transcendentals=0,
        ),
    )(
        in_smem(place),
        in_smem(tile_of),
        in_smem(jnp.swapaxes(tile_mask, 2, 3)),
        tiles[0],
        *tiles[2:],
        tiles[1],
        lambda_amps,
        swap,
    )


def finish_blocks(indices, chunk, swap_ref, w_ref, inverse_ref, piece_refs, done, ys, then, turns):
    groups, _, rows, _ = done.shape
    swap = swap_ref[...]
    share = groups // turns
    for turn in range(turns):
        mine = slice(turn * share * ROWS, (turn + 1) * share * ROWS)
        weights = w_ref[mine, :]
        for a in range(rows):
            amps = jnp.concatenate(
                [ref[index, a] for ref, index in zip(piece_refs, indices)], axis=0
            )
            cycle = jnp.dot(weights, amps, preferred_element_type=jnp.float32)
            total = amps[mine].astype(jnp.float32) + cycle
            value = (total * inverse_ref[chunk * rows + a, mine, :]).astype(jnp.bfloat16)
            for g in range(share):
                ys[turn * share + g, pl.ds(a * ROWS, ROWS), :] = value[g * ROWS : (g + 1) * ROWS]
        for g in range(turn * share, (turn + 1) * share):
            turned = jnp.dot(swap, ys[g], preferred_element_type=jnp.float32)
            done[g] = turned.astype(jnp.bfloat16).reshape(done.shape[1:])
            then(g)


def early_kernel(indices, chunk, swap_ref, w_ref, inverse_ref, *refs):
    piece_refs, (done, ys) = refs[:-2], refs[-2:]
    finish_blocks(
        indices, chunk, swap_ref, w_ref, inverse_ref, piece_refs, done, ys, lambda g: None, 1
    )


def last_kernel(indices, chunk, swap_ref, w_ref, inverse_ref, place_ref, *refs):
    ready_refs, piece_refs, (out_ref, done, ys, sems) = refs[:chunk], refs[chunk:-4], refs[-4:]
    groups, _, rows, _ = done.shape
    halves = 2 * groups // len(indices)
    me = place_ref[0]
    leaving = []

    def write(source, c, g):
        k, h = g // halves, g % halves
        copy = pltpu.make_async_copy(
            source.at[g],
            out_ref.at[me ^ k, 0, pl.ds(h * ROWS, ROWS), pl.ds(c * rows, rows), :],
            sems.at[c, g],
        )
        copy.start()
        leaving.append(copy)

    for c, ref in enumerate(ready_refs):
        for g in range(groups):
            write(ref, c, g)
    finish_blocks(
        indices,
        chunk,
        swap_ref,
        w_ref,
        inverse_ref,
        piece_refs,
        done,
        ys,
        lambda g: write(done, chunk, g),
        2,
    )
    for copy in leaving:
        copy.wait()


def finish(chunk, swap, weights, inverse, pieces, place=None, ready=(), shape=None):
    _, rows, pairs, cols = pieces[0][0].shape
    groups = len(pieces) // 2 * (pairs // ROWS)
    indices = [index for _, index in pieces]
    vmem, anywhere = pl.BlockSpec(memory_space=pltpu.VMEM), pl.BlockSpec(memory_space=pl.ANY)
    block = (groups, ROWS, rows, cols)
    ys = pltpu.VMEM((groups, ROWS * rows, cols), jnp.bfloat16)
    args, in_specs = [swap, weights, inverse], [vmem] * 3
    if shape is None:
        kernel = functools.partial(early_kernel, indices, chunk)
        out_spec, out_shape = vmem, jax.ShapeDtypeStruct(block, jnp.bfloat16)
        scratch = [ys]
    else:
        kernel = functools.partial(last_kernel, indices, chunk)
        out_spec, out_shape = anywhere, jax.ShapeDtypeStruct(shape, jnp.bfloat16)
        scratch = [pltpu.VMEM(block, jnp.bfloat16), ys]
        scratch += [pltpu.SemaphoreType.DMA((chunk + 1, groups))]
        args += [place, *ready]
        in_specs += [pl.BlockSpec(memory_space=pltpu.SMEM)] + [anywhere] * len(ready)
    return pl.pallas_call(
        kernel,
        in_specs=in_specs + [vmem] * len(pieces),
        out_specs=out_spec,
        out_shape=out_shape,
        scratch_shapes=scratch,
        compiler_params=pltpu.CompilerParams(vmem_limit_bytes=VMEM_BYTES),
        cost_estimate=pl.CostEstimate(flops=0, bytes_accessed=0, transcendentals=0),
    )(*args, *[piece for piece, _ in pieces])


def local_chunked(
    lambda_amps,
    integral_tiles,
    tile_of,
    tile_mask,
    pair_list,
    coupling,
    pair_gap,
    row_energy,
    col_energy,
):
    pairs, tile_rows, cols = lambda_amps.shape[2:]
    owners = lax.axis_size("pair")
    rows = tile_rows // owners
    chunks = rows // ROWS
    me = lax.axis_index("pair").astype(jnp.int32)
    sub = lax.axis_index("sub").astype(jnp.int32)
    place = jnp.stack([me, sub])

    def to_owner(value, k):
        return lax.ppermute(value, "pair", [(o, o ^ k) for o in range(owners)])

    def to_sibling(value):
        return lax.ppermute(value, "sub", [(0, 1), (1, 0)])

    def after(value, earlier):
        return value if earlier is None else lax.optimization_barrier((value, earlier))[0]

    tiles = [integral_tiles] + [to_owner(integral_tiles, k) for k in range(1, owners)]

    far = list(range(2, owners))
    last = far[-1]
    groups = [((k, c),) for c in range(chunks) for k in far[::-1]]
    groups += [tuple((k, c) for c in range(chunks)) for k in (1, 0)]
    held, swap = hold(lambda_amps)
    sent = dict(zip(groups, dress(groups, place, tile_of, tile_mask, tiles, held, swap)))
    weights, inverse = make_weights(
        after(pair_list, sent[groups[0]]), coupling, pair_gap, place, row_energy, col_energy
    )
    own, near = sent[groups[-1]], to_owner(sent[groups[-2]], 1)

    @functools.cache
    def landed(k, c):
        earlier = landed(k, c - 1) if c and k == last else None
        return to_owner(after(sent[((k, c),)], earlier), k)

    @functools.cache
    def passed(k, c):
        earlier = passed(far[0], c - 1) if c else (weights, inverse) if k == last else None
        return to_sibling(after(landed(k, c), earlier))

    @functools.cache
    def passed_whole(k):
        return to_sibling(after(near, (weights, inverse, passed(last, 0))) if k else after(own, near))

    chunk_pieces = []
    for c in range(chunks - 1, -1, -1):
        pieces = [(own, c), (near, c)] + [(landed(k, c), 0) for k in far]
        pieces += [(passed_whole(k), c) for k in (0, 1)] + [(passed(k, c), 0) for k in far]
        chunk_pieces.insert(0, pieces)
    ready = [finish(c, swap, weights, inverse, chunk_pieces[c]) for c in range(chunks - 1)]
    shape = (owners, 1, pairs, rows, cols)
    return finish(chunks - 1, swap, weights, inverse, chunk_pieces[-1], place, ready, shape)


def solution(mesh):
    placed = (
        P(("mol", "pair"), "sub", None, None, "tile"),
        P(("mol", "pair"), None, None),
        P(("mol", "pair"), "sub", None),
        P(("mol", "pair"), "sub", None, "tile"),
        P("mol", None),
        P("mol", None),
        P("mol", "sub", None),
        P(("mol", "pair")),
        P(("mol", "tile")),
    )
    owners, subs = mesh.shape["pair"], mesh.shape["sub"]

    def local(*args):
        tile_rows, cols = args[0].shape[3:]
        rows = tile_rows // owners
        power = owners >= 4 and owners & (owners - 1) == 0
        fits = rows % ROWS == 0 and cols % LANES == 0 and args[1].shape[0] == 1
        if power and fits and subs == 2 and args[0].shape[2] % ROWS == 0:
            return local_chunked(*args)
        return local_general(*args)

    return jax.shard_map(
        local,
        mesh=mesh,
        in_specs=placed,
        out_specs=P("mol", "sub", None, "pair", "tile"),
        check_vma=False,
    )
```

```python
import functools
import math

import jax
import jax.numpy as jnp
from jax import lax
from jax.experimental import pallas as pl
from jax.experimental.pallas import tpu as pltpu
from jax.sharding import PartitionSpec as P

ROWS = 16
LANES = 128
VMEM_BYTES = 24 * 2**20


def column_tables(coupling, col_pairs):
    left_table = jnp.take(coupling.T, col_pairs[:, 0], axis=0).T
    right_table = jnp.take(coupling.T, col_pairs[:, 1], axis=0).T
    return (left_table, right_table)


def cycle_rows(left_table, right_table, row_pairs):
    left_part = jnp.take(left_table, row_pairs[:, 0], axis=0)
    right_part = jnp.take(right_table, row_pairs[:, 1], axis=0)
    return (left_part * right_part).astype(jnp.bfloat16)


def cycle_all(coupling, pair_list, col_pairs, flat_rhs):
    total_pairs = pair_list.shape[0]
    step_rows = math.gcd(total_pairs, 512)
    row_blocks = pair_list.reshape(total_pairs // step_rows, step_rows, 2)
    left_table, right_table = column_tables(coupling, col_pairs)

    def one_block(row_pairs):
        weights = cycle_rows(left_table, right_table, row_pairs)
        return jnp.dot(weights, flat_rhs, preferred_element_type=jnp.float32)

    return lax.map(one_block, row_blocks).reshape(total_pairs, -1)


def local_general(
    lambda_amps,
    integral_tiles,
    tile_of,
    tile_mask,
    pair_list,
    coupling,
    pair_gap,
    row_energy,
    col_energy,
):
    pair_count = lambda_amps.shape[2]
    tile_rows = lambda_amps.shape[3]
    col_count = lambda_amps.shape[4]
    owners = lax.axis_size("pair")
    sub_count = lax.axis_size("sub")
    wanted = tile_of.reshape(pair_count)
    empty_tiles = jnp.zeros((pair_count, tile_rows, tile_rows), integral_tiles.dtype)
    shard_piece = lax.all_gather(integral_tiles, "pair", axis=0, tiled=True)
    inside = (wanted >= 0) & (wanted < shard_piece.shape[0])
    taken_rows = shard_piece[jnp.clip(wanted, 0, shard_piece.shape[0] - 1)]
    chosen = jnp.where(inside[:, None, None], taken_rows, empty_tiles)
    amplitudes = lambda_amps.reshape(pair_count, tile_rows, col_count)
    ladder = jnp.einsum("pac,pcb->pab", chosen, amplitudes, preferred_element_type=jnp.float32)
    blocks = tile_mask.shape[3]
    keep_mask = tile_mask.reshape(pair_count, 1, blocks, 1).astype(jnp.float32)
    ladder = (
        ladder.reshape(pair_count, tile_rows, blocks, col_count // blocks) * keep_mask
    ).reshape(pair_count, tile_rows, col_count)
    dressed = (amplitudes.astype(jnp.float32) + ladder).astype(jnp.bfloat16)
    dressed = dressed.reshape(1, 1, pair_count, tile_rows, col_count)
    relayed = lax.all_to_all(dressed, "pair", split_axis=3, concat_axis=0, tiled=True)
    sub_index = lax.axis_index("sub")
    block_ids = jnp.arange(owners, dtype=jnp.int32) * sub_count + sub_index
    mine_ids = (
        block_ids[:, None] * pair_count + jnp.arange(pair_count, dtype=jnp.int32)[None, :]
    ).reshape(-1)
    col_pairs = pair_list[mine_ids]
    flat_rhs = relayed.reshape(owners * pair_count, -1)
    partial_value = cycle_all(coupling, pair_list, col_pairs, flat_rhs)
    partial_value = partial_value.reshape(
        owners, sub_count, pair_count, relayed.shape[3], col_count
    )
    cycle_term = lax.psum_scatter(
        partial_value.astype(jnp.bfloat16), "sub", scatter_dimension=1, tiled=True
    ).astype(jnp.float32)
    total_sum = relayed.astype(jnp.float32) + cycle_term
    energy_gap = (
        pair_gap[:, :, :, None, None]
        + row_energy[None, None, None, :, None]
        + col_energy[None, None, None, None, :]
    )
    return (-total_sum / energy_gap).astype(jnp.bfloat16)


def in_hbm(value):
    return pltpu.with_memory_space_constraint(value, pltpu.HBM)


def in_smem(value):
    return pltpu.with_memory_space_constraint(value, pltpu.SMEM)


def one_hot(hits):
    return jnp.where(hits, 1.0, 0.0).astype(jnp.bfloat16)


def square_iotas(size):
    return (lax.broadcasted_iota(jnp.int32, (size, size), axis) for axis in range(2))


def split3(value):
    high = value.astype(jnp.bfloat16)
    rest = value - high.astype(jnp.float32)
    mid = rest.astype(jnp.bfloat16)
    low = (rest - mid.astype(jnp.float32)).astype(jnp.bfloat16)
    return high, mid, low


def pick_columns(value, columns):
    high, mid, low = (
        jnp.dot(part, columns, preferred_element_type=jnp.float32) for part in split3(value)
    )
    return high + (mid + low)


def pick_rows(columns, value):
    dims = (((0,), (0,)), ((), ()))
    high, mid, low = (
        lax.dot_general(columns, part, dims, preferred_element_type=jnp.float32)
        for part in split3(value)
    )
    return high + (mid + low)


def hold_kernel(lam_ref, held_ref, swap_ref, sems):
    step = lam_ref.shape[2] // sems.shape[0]
    copies = []
    for i in range(sems.shape[0]):
        block = pl.ds(i * step, step)
        copy = pltpu.make_async_copy(
            lam_ref.at[:, :, block], held_ref.at[:, :, block], sems.at[i]
        )
        copy.start()
        copies.append(copy)
    to, frm = square_iotas(ROWS * ROWS)
    swap_ref[...] = one_hot(to == (frm % ROWS) * ROWS + frm // ROWS)
    for copy in copies:
        copy.wait()


def hold(lambda_amps):
    anywhere = pl.BlockSpec(memory_space=pl.ANY)
    return pl.pallas_call(
        hold_kernel,
        in_specs=[anywhere],
        out_specs=[anywhere, pl.BlockSpec(memory_space=pltpu.VMEM)],
        out_shape=[
            jax.ShapeDtypeStruct(lambda_amps.shape, lambda_amps.dtype),
            jax.ShapeDtypeStruct((ROWS * ROWS, ROWS * ROWS), jnp.bfloat16),
        ],
        scratch_shapes=[pltpu.SemaphoreType.DMA((8,))],
        compiler_params=pltpu.CompilerParams(vmem_limit_bytes=VMEM_BYTES),
        cost_estimate=pl.CostEstimate(
            flops=0, bytes_accessed=4 * lambda_amps.size, transcendentals=0
        ),
    )(in_hbm(lambda_amps))


def weights_kernel(
    pair_ref, coupling_ref, gap_ref, place_ref, row_ref, col_ref, w_ref, inverse_ref, full
):
    total = pair_ref.shape[1]
    depth = coupling_ref.shape[0]
    owners, _, pairs = gap_ref.shape
    me, sub = place_ref[0], place_ref[1]
    orbital = lax.broadcasted_iota(jnp.int32, (depth, total), 0)
    coupling = coupling_ref[...]
    product = None
    for side in range(2):
        columns = one_hot(orbital == pair_ref[side : side + 1, :])
        picked = pick_rows(columns, pick_columns(coupling, columns))
        product = picked if product is None else product * picked
    frm, to = square_iotas(total)
    block, within = to // pairs, to % pairs
    source = ((me ^ (block % owners)) * 2 + (sub ^ (block // owners))) * pairs + within
    full[...] = jnp.dot(
        product.astype(jnp.bfloat16), one_hot(frm == source), preferred_element_type=jnp.float32
    )
    row, column = square_iotas(pairs)
    for k in range(owners):
        start = pl.multiple_of(((me ^ k) * 2 + sub) * pairs, pairs)
        rows = pl.ds(k * pairs, pairs)
        w_ref[rows, :] = full[pl.ds(start, pairs), :].astype(jnp.bfloat16)
        gap = jnp.sum(jnp.where(row == column, gap_ref[me ^ k], 0.0), axis=1, keepdims=True)
        for a in range(inverse_ref.shape[0]):
            inverse_ref[a, rows, :] = -1.0 / ((gap + row_ref[a]) + col_ref[...])


def make_weights(pair_list, coupling, pair_gap, place, row_energy, col_energy):
    owners, _, pairs = pair_gap.shape
    total = pair_list.shape[0]
    mine = owners * pairs
    rows, cols = row_energy.shape[0], col_energy.shape[0]
    smem = pl.BlockSpec(memory_space=pltpu.SMEM)
    vmem = pl.BlockSpec(memory_space=pltpu.VMEM)
    return pl.pallas_call(
        weights_kernel,
        in_specs=[vmem, vmem, vmem, smem, smem, vmem],
        out_specs=[vmem, vmem],
        out_shape=[
            jax.ShapeDtypeStruct((mine, total), jnp.bfloat16),
            jax.ShapeDtypeStruct((rows, mine, cols), jnp.float32),
        ],
        scratch_shapes=[pltpu.VMEM((total, total), jnp.float32)],
        compiler_params=pltpu.CompilerParams(vmem_limit_bytes=VMEM_BYTES),
        cost_estimate=pl.CostEstimate(
            flops=12 * total * coupling.size, bytes_accessed=4 * coupling.size, transcendentals=0
        ),
    )(pair_list.T, coupling, pair_gap, place, row_energy, col_energy.reshape(1, cols))


def dress_kernel(owners, rows, groups, place_ref, tile_of_ref, mask_ref, *refs):
    tile_refs, lam_ref = (refs[0], refs[owners - 1], *refs[1 : owners - 1]), refs[owners]
    swap_ref = refs[owners + 1]
    out_refs = refs[owners + 2 : -2]
    tiles, stage = refs[-2:]
    me = place_ref[0]
    flat = [(k, c, out, j) for out, group in zip(out_refs, groups) for j, (k, c) in enumerate(group)]
    starts = [pl.multiple_of((me ^ k) * rows + c * ROWS, ROWS) for k, c, _, _ in flat]
    tile_rows, cols = lam_ref.shape[3:]
    row = lax.broadcasted_iota(jnp.int32, (ROWS, tile_rows), 0)
    column = lax.broadcasted_iota(jnp.int32, (ROWS, tile_rows), 1)
    for n, start in enumerate(starts):
        block = pl.ds(n * ROWS, ROWS)
        own_row = one_hot(column == row + start)
        for k in range(owners):
            tiles[k, block, :tile_rows] = tile_refs[k][0, pl.ds(start, ROWS), :]
            tiles[k, block, tile_rows:] = own_row
    swap = swap_ref[...]
    parts = mask_ref.shape[2]
    width = cols // parts
    for g in range(lam_ref.shape[2] // ROWS):
        for i in range(ROWS):
            pair = g * ROWS + i
            amps = lam_ref[0, 0, pair]
            kept = [
                amps[:, part * width : (part + 1) * width]
                * mask_ref[0, 0, part, pair].astype(jnp.float32).astype(jnp.bfloat16)
                for part in range(parts)
            ]
            both = jnp.concatenate([jnp.concatenate(kept, axis=1), amps], axis=0)
            full = jnp.dot(
                tiles[tile_of_ref[0, 0, pair] ^ me], both, preferred_element_type=jnp.float32
            ).astype(jnp.bfloat16)
            for n in range(len(flat)):
                stage[g, n, pl.ds(i * ROWS, ROWS), :] = full[n * ROWS : (n + 1) * ROWS]
        for n, (_, _, out, j) in enumerate(flat):
            turned = jnp.dot(swap, stage[g, n], preferred_element_type=jnp.float32)
            out[j, :, pl.ds(g * ROWS, ROWS), :] = turned.astype(jnp.bfloat16).reshape(
                ROWS, ROWS, turned.shape[1]
            )


def dress(groups, place, tile_of, tile_mask, tiles, lambda_amps, swap):
    owners = len(tiles)
    pairs, tile_rows, cols = lambda_amps.shape[2:]
    rows = tile_rows // owners
    smem = pl.BlockSpec(memory_space=pltpu.SMEM)
    vmem = pl.BlockSpec(memory_space=pltpu.VMEM)
    count = sum(len(group) for group in groups)
    return pl.pallas_call(
        functools.partial(dress_kernel, owners, rows, groups),
        in_specs=[smem] * 3 + [vmem] * (owners + 2),
        out_specs=[vmem] * len(groups),
        out_shape=[
            jax.ShapeDtypeStruct((len(group), ROWS, pairs, cols), jnp.bfloat16)
            for group in groups
        ],
        scratch_shapes=[
            pltpu.VMEM((owners, count * ROWS, 2 * tile_rows), jnp.bfloat16),
            pltpu.VMEM((pairs // ROWS, count, ROWS * ROWS, cols), jnp.bfloat16),
        ],
        compiler_params=pltpu.CompilerParams(vmem_limit_bytes=VMEM_BYTES),
        cost_estimate=pl.CostEstimate(
            flops=2 * pairs * count * ROWS * tile_rows * cols,
            bytes_accessed=3 * pairs * tile_rows * cols,
            transcendentals=0,
        ),
    )(
        in_smem(place),
        in_smem(tile_of),
        in_smem(jnp.swapaxes(tile_mask, 2, 3)),
        tiles[0],
        *tiles[2:],
        tiles[1],
        lambda_amps,
        swap,
    )


def finish_blocks(indices, chunk, swap_ref, w_ref, inverse_ref, piece_refs, done, ys, then):
    groups, _, rows, _ = done.shape
    mine = groups * ROWS
    weights = w_ref[...]
    for a in range(rows):
        amps = jnp.concatenate([ref[index, a] for ref, index in zip(piece_refs, indices)], axis=0)
        cycle = jnp.dot(weights, amps, preferred_element_type=jnp.float32)
        total = amps[:mine].astype(jnp.float32) + cycle
        value = (total * inverse_ref[chunk * rows + a]).astype(jnp.bfloat16)
        for g in range(groups):
            ys[g, pl.ds(a * ROWS, ROWS), :] = value[g * ROWS : (g + 1) * ROWS]
    swap = swap_ref[...]
    for g in range(groups):
        turned = jnp.dot(swap, ys[g], preferred_element_type=jnp.float32)
        done[g] = turned.astype(jnp.bfloat16).reshape(done.shape[1:])
        then(g)


def early_kernel(indices, chunk, swap_ref, w_ref, inverse_ref, *refs):
    piece_refs, (done, ys) = refs[:-2], refs[-2:]
    finish_blocks(
        indices, chunk, swap_ref, w_ref, inverse_ref, piece_refs, done, ys, lambda g: None
    )


def last_kernel(indices, chunk, swap_ref, w_ref, inverse_ref, place_ref, *refs):
    ready_refs, piece_refs, (out_ref, done, ys, sems) = refs[:chunk], refs[chunk:-4], refs[-4:]
    groups, _, rows, _ = done.shape
    halves = 2 * groups // len(indices)
    me = place_ref[0]
    leaving = []

    def write(source, c, g):
        k, h = g // halves, g % halves
        copy = pltpu.make_async_copy(
            source.at[g],
            out_ref.at[me ^ k, 0, pl.ds(h * ROWS, ROWS), pl.ds(c * rows, rows), :],
            sems.at[c, g],
        )
        copy.start()
        leaving.append(copy)

    for c, ref in enumerate(ready_refs):
        for g in range(groups):
            write(ref, c, g)
    finish_blocks(
        indices,
        chunk,
        swap_ref,
        w_ref,
        inverse_ref,
        piece_refs,
        done,
        ys,
        lambda g: write(done, chunk, g),
    )
    for copy in leaving:
        copy.wait()


def finish(chunk, swap, weights, inverse, pieces, place=None, ready=(), shape=None):
    _, rows, pairs, cols = pieces[0][0].shape
    groups = len(pieces) // 2 * (pairs // ROWS)
    indices = [index for _, index in pieces]
    vmem, anywhere = pl.BlockSpec(memory_space=pltpu.VMEM), pl.BlockSpec(memory_space=pl.ANY)
    block = (groups, ROWS, rows, cols)
    ys = pltpu.VMEM((groups, ROWS * rows, cols), jnp.bfloat16)
    args, in_specs = [swap, weights, inverse], [vmem] * 3
    if shape is None:
        kernel = functools.partial(early_kernel, indices, chunk)
        out_spec, out_shape = vmem, jax.ShapeDtypeStruct(block, jnp.bfloat16)
        scratch = [ys]
    else:
        kernel = functools.partial(last_kernel, indices, chunk)
        out_spec, out_shape = anywhere, jax.ShapeDtypeStruct(shape, jnp.bfloat16)
        scratch = [pltpu.VMEM(block, jnp.bfloat16), ys]
        scratch += [pltpu.SemaphoreType.DMA((chunk + 1, groups))]
        args += [place, *ready]
        in_specs += [pl.BlockSpec(memory_space=pltpu.SMEM)] + [anywhere] * len(ready)
    return pl.pallas_call(
        kernel,
        in_specs=in_specs + [vmem] * len(pieces),
        out_specs=out_spec,
        out_shape=out_shape,
        scratch_shapes=scratch,
        compiler_params=pltpu.CompilerParams(vmem_limit_bytes=VMEM_BYTES),
        cost_estimate=pl.CostEstimate(flops=0, bytes_accessed=0, transcendentals=0),
    )(*args, *[piece for piece, _ in pieces])


def local_chunked(
    lambda_amps,
    integral_tiles,
    tile_of,
    tile_mask,
    pair_list,
    coupling,
    pair_gap,
    row_energy,
    col_energy,
):
    pairs, tile_rows, cols = lambda_amps.shape[2:]
    owners = lax.axis_size("pair")
    rows = tile_rows // owners
    chunks = rows // ROWS
    me = lax.axis_index("pair").astype(jnp.int32)
    sub = lax.axis_index("sub").astype(jnp.int32)
    place = jnp.stack([me, sub])

    def to_owner(value, k):
        return lax.ppermute(value, "pair", [(o, o ^ k) for o in range(owners)])

    def to_sibling(value):
        return lax.ppermute(value, "sub", [(0, 1), (1, 0)])

    def after(value, earlier):
        return value if earlier is None else lax.optimization_barrier((value, earlier))[0]

    tiles = [integral_tiles] + [to_owner(integral_tiles, k) for k in range(1, owners)]

    far = list(range(2, owners))
    last = far[-1]
    groups = [((k, c),) for c in range(chunks) for k in far[::-1]]
    groups += [tuple((k, c) for c in range(chunks)) for k in (1, 0)]
    held, swap = hold(lambda_amps)
    sent = dict(zip(groups, dress(groups, place, tile_of, tile_mask, tiles, held, swap)))
    weights, inverse = make_weights(
        after(pair_list, sent[groups[0]]), coupling, pair_gap, place, row_energy, col_energy
    )
    own, near = sent[groups[-1]], to_owner(sent[groups[-2]], 1)

    @functools.cache
    def landed(k, c):
        earlier = landed(k, c - 1) if c and k == last else None
        return to_owner(after(sent[((k, c),)], earlier), k)

    @functools.cache
    def passed(k, c):
        earlier = passed(far[0], c - 1) if c else (weights, inverse) if k == last else None
        return to_sibling(after(landed(k, c), earlier))

    @functools.cache
    def passed_whole(k):
        return to_sibling(after(near, (weights, inverse, passed(last, 0))) if k else after(own, landed(last, 0)))

    chunk_pieces = []
    for c in range(chunks - 1, -1, -1):
        pieces = [(own, c), (near, c)] + [(landed(k, c), 0) for k in far]
        pieces += [(passed_whole(k), c) for k in (0, 1)] + [(passed(k, c), 0) for k in far]
        chunk_pieces.insert(0, pieces)
    ready = [finish(c, swap, weights, inverse, chunk_pieces[c]) for c in range(chunks - 1)]
    shape = (owners, 1, pairs, rows, cols)
    return finish(chunks - 1, swap, weights, inverse, chunk_pieces[-1], place, ready, shape)


def solution(mesh):
    placed = (
        P(("mol", "pair"), "sub", None, None, "tile"),
        P(("mol", "pair"), None, None),
        P(("mol", "pair"), "sub", None),
        P(("mol", "pair"), "sub", None, "tile"),
        P("mol", None),
        P("mol", None),
        P("mol", "sub", None),
        P(("mol", "pair")),
        P(("mol", "tile")),
    )
    owners, subs = mesh.shape["pair"], mesh.shape["sub"]

    def local(*args):
        tile_rows, cols = args[0].shape[3:]
        rows = tile_rows // owners
        power = owners >= 4 and owners & (owners - 1) == 0
        fits = rows % ROWS == 0 and cols % LANES == 0 and args[1].shape[0] == 1
        if power and fits and subs == 2 and args[0].shape[2] % ROWS == 0:
            return local_chunked(*args)
        return local_general(*args)

    return jax.shard_map(
        local,
        mesh=mesh,
        in_specs=placed,
        out_specs=P("mol", "sub", None, "pair", "tile"),
        check_vma=False,
    )
```
